128 devices in a mesh: layer: 4 (over y), trace: 32 (over x, z, core).
Axes of the slice: x: 4, y: 4, z: 4, core: 2. Of those that a mesh axis runs over, the one named last changes fastest.
Arguments:
- pool_inputs: bfloat16 [4, 64, 128, 4096], P('layer', 'trace'), may hold values from -6 to 6
- val_inputs: bfloat16 [4, 64, 128, 4096], P('layer', 'trace'), may hold values from -6 to 6
- pool_top: bfloat16 [64, 128, 4096], P('trace'), may hold values from -6 to 6
- val_top: bfloat16 [64, 128, 4096], P('trace'), may hold values from -6 to 6
- weight: bfloat16 [4, 4096, 4096], P('layer', 'trace'), may hold values from -0.0625 to 0.0625
- proj_in: bfloat16 [4, 4096, 64], P('layer'), may hold values from -0.09375 to 0.09375
- proj_out: bfloat16 [4, 4096, 64], P('layer'), may hold values from -0.09375 to 0.09375
- pool_len: int32 [64], P('trace'), may hold values from 32 to 128, as said below
- val_len: int32 [64], P('trace'), may hold values from 32 to 128, as said below
Outputs:
- scores: float32 [64, 64], P('trace', 'layer')
The draws below stay inside these ranges and needn't reach their ends.
Inputs may be any that keep to these rules, and one draw needn't show every extreme that they name: `pool_len`: every length lies in range and some pool trace and some validation trace have exactly 128 valid tokens. `val_len`: as for pool_len.
All inputs are finite; a program needn't handle non-finite values.
Results may differ from the reference program's by a relative error of at most 0.0056.
Values may be sent and summed in bfloat16 or wider, within the bound.
A program may use at most 192 MiB of HBM per device.

```python
import jax
import jax.numpy as jnp
from jax import lax

D = 4096
RANK = 64
LEN = 128
POOL = 64
VAL = 64
LAYERS = 4


def draw_pool_len(key, part):
    key = jax.random.fold_in(key, 11)
    values = jax.random.randint(key, (POOL,), LEN // 4, LEN + 1)
    return values.at[0].set(LEN).astype(jnp.int32)


def draw_val_len(key, part):
    key = jax.random.fold_in(key, 23)
    values = jax.random.randint(key, (VAL,), LEN // 4, LEN + 1)
    return values.at[0].set(LEN).astype(jnp.int32)


def shard_levels(key, dims, cuts, least, largest):
    def one(dim, parts):
        steps = jax.random.uniform(jax.random.fold_in(jax.random.fold_in(key, 6), dim), (parts,), jnp.float32, least / len(cuts), largest / len(cuts))
        return jnp.repeat(jnp.exp(steps), dims[dim] // parts).reshape((-1,) + (1,) * (len(dims) - dim - 1))

    factor_of = one(*cuts[0])
    for cut in cuts[1:]:
        factor_of = factor_of * one(*cut)
    return factor_of


def noise(own_key, extent, scale, bound, shards=(), kind=jnp.bfloat16):
    loudness = shard_levels(own_key, extent, shards, -0.22, 0.18) if shards else 1.0
    entries = jax.random.normal(own_key, extent, jnp.float32) * scale * loudness
    return jnp.minimum(jnp.maximum(entries, -bound), bound).astype(kind)


def setup_inputs(seed: int = 0) -> dict:
    keys = jax.random.split(jax.random.key(seed), 10)
    pool_inputs = noise(keys[0], (LAYERS, POOL, LEN, D), 1.0, 6.0, ((0, 4), (1, 32)))
    val_inputs = noise(keys[1], (LAYERS, VAL, LEN, D), 1.0, 6.0, ((0, 4), (1, 32)))
    pool_top = noise(keys[2], (POOL, LEN, D), 1.0, 6.0, ((0, 32),))
    val_top = noise(keys[3], (VAL, LEN, D), 1.0, 6.0, ((0, 32),))
    weight = noise(keys[4], (LAYERS, D, D), (2 * D) ** -0.5, 0.0625, ((0, 4), (1, 32)))
    proj_in = noise(keys[5], (LAYERS, D, RANK), D ** -0.5, 0.09375, ((0, 4),))
    proj_out = noise(keys[6], (LAYERS, D, RANK), D ** -0.5, 0.09375, ((0, 4),))
    pool_len = draw_pool_len(jax.random.fold_in(keys[9], 71), 0)
    val_len = draw_val_len(jax.random.fold_in(keys[9], 71), 0)
    return {"pool_inputs": pool_inputs, "val_inputs": val_inputs, "pool_top": pool_top, "val_top": val_top, "weight": weight, "proj_in": proj_in, "proj_out": proj_out, "pool_len": pool_len, "val_len": val_len}


def damped_inverse(factor):
    size_rank = factor.shape[0]
    identity = jnp.eye(size_rank, dtype=jnp.float32)
    damping = 0.1 * jnp.trace(factor) / size_rank
    lower_factor = jnp.linalg.cholesky(factor + damping * identity)
    return jax.scipy.linalg.cho_solve((lower_factor, True), identity)

def silu_slope(values):
    logistic = jax.nn.sigmoid(values)
    return logistic * (1.0 + values * (1.0 - logistic))

def reference(pool_inputs, val_inputs, pool_top, val_top, weight, proj_in, proj_out, pool_len, val_len):
    positions = jnp.arange(LEN, dtype=jnp.int32)
    pool_mask = positions[None, :] < pool_len[:, None].astype(jnp.int32)
    val_mask = positions[None, :] < val_len[:, None].astype(jnp.int32)
    valid_mask = jnp.concatenate([pool_mask, val_mask], 0).astype(jnp.float32)
    token_count = jnp.sum(pool_len).astype(jnp.float32)
    grads = jnp.concatenate([pool_top, val_top], 0)
    traces = POOL + VAL
    score_sum = jnp.zeros((POOL, VAL), jnp.float32)
    highest = lax.Precision.HIGHEST
    for layer_index in range(LAYERS - 1, -1, -1):
        flat_grads = grads.reshape(traces * LEN, D)
        layer_inputs = jnp.concatenate([pool_inputs[layer_index], val_inputs[layer_index]], 0).reshape(traces * LEN, D)
        grad_low = jnp.dot(flat_grads.astype(jnp.float32), proj_out[layer_index].astype(jnp.float32), preferred_element_type=jnp.float32).reshape(traces, LEN, RANK) * valid_mask[:, :, None]
        input_low = jnp.dot(layer_inputs.astype(jnp.float32), proj_in[layer_index].astype(jnp.float32), preferred_element_type=jnp.float32).reshape(traces, LEN, RANK) * valid_mask[:, :, None]
        trace_grads = jnp.einsum('nti,ntj->nij', grad_low, input_low, precision=highest)
        pool_in = input_low[:POOL].reshape(POOL * LEN, RANK)
        pool_out = grad_low[:POOL].reshape(POOL * LEN, RANK)
        factor_in = jnp.dot(pool_in.T, pool_in, precision=highest) / token_count
        factor_out = jnp.dot(pool_out.T, pool_out, precision=highest) / token_count
        inv_in = damped_inverse(factor_in)
        inv_out = damped_inverse(factor_out)
        scaled = jnp.einsum('ab,nbc,cd->nad', inv_out, trace_grads[POOL:], inv_in, precision=highest)
        score_sum = score_sum + jnp.dot(trace_grads[:POOL].reshape(POOL, RANK * RANK), scaled.reshape(VAL, RANK * RANK).T, precision=highest)
        if layer_index > 0:
            gated = (flat_grads.astype(jnp.float32) * silu_slope(layer_inputs.astype(jnp.float32))).astype(jnp.bfloat16)
            lowered = flat_grads.astype(jnp.float32) + jnp.dot(gated.astype(jnp.float32), weight[layer_index].astype(jnp.float32), preferred_element_type=jnp.float32)
            grads = lowered.astype(jnp.bfloat16).reshape(traces, LEN, D)
    return score_sum / (RANK * LEN)
```

```python
import functools

import jax
import jax.numpy as jnp
from jax import lax
from jax.experimental import pallas as pl
from jax.experimental.pallas import tpu as pltpu
from jax.sharding import PartitionSpec as P

MESH = pl.DeviceIdType.MESH
WIDTH = 4096
TOKENS = 128
CHUNKS = 16
COLS = WIDTH // CHUNKS
PAIRS = CHUNKS // 2
SHARE = 128
MAIN = 384
REST = 128
LAG_FORWARD, LAG_ROW, LAG_ROW_FORWARD, LAG_LAST, LAG_USE = 1, 2, 3, 4, 5
LAG_GRAD = 6
CATCH_UP = 3
SLOTS = 13


def silu_slope(values):
    logistic = jax.nn.sigmoid(values)
    return logistic * (1.0 + values * (1.0 - logistic))


def chain_kernel(
    pool_in, val_in, pool_top, val_top, weight,
    grad2_out, grad1_out, gated_out,
    held, first, second, gated, grad, total,
    send, recv, grad_send, grad_recv, act_send, act_recv, local, out_sem,
):
    layer = lax.axis_index("layer")
    trace = lax.axis_index("trace")
    x, z, c = trace // 8, (trace // 2) % 4, trace % 2
    xp, xm, xo = (x + 1) % 4, (x + 3) % 4, (x + 2) % 4
    zp, zm, zo = (z + 1) % 4, (z + 3) % 4, (z + 2) % 4
    other = 1 - c

    def at(xi, zi, ci):
        return {"trace": xi * 8 + zi * 2 + ci}

    above = {"layer": (layer + 1) % 4}
    below = {"layer": (layer + 3) % 4}

    barrier = pltpu.get_barrier_semaphore()
    for device in (at(xp, z, c), at(xm, z, c), at(x, zp, c), at(x, zm, c), at(x, z, other), above, below):
        pl.semaphore_signal(barrier, inc=1, device_id=device, device_id_type=MESH)
    pl.semaphore_wait(barrier, 7)

    def columns(j):
        return pl.ds(pl.multiple_of(j * COLS, COLS), COLS)

    def remote(src, dst, j, slot, device):
        return pltpu.make_async_remote_copy(
            src_ref=src, dst_ref=dst, send_sem=send.at[j, slot], recv_sem=recv.at[j, slot],
            device_id=device, device_id_type=MESH,
        )

    def arrived(ref, j, slot):
        remote(ref, ref, j, slot, at(x, z, other)).wait_recv()

    def push(ref, j, slot, device):
        remote(ref, ref, j, slot, device).start()

    def own(j):
        return held.at[j, x, z, c]

    def share_out(j, device):
        return remote(weight.at[:, columns(j)], own(j), j, 12, device)

    def share_local(j):
        return pltpu.make_async_copy(weight.at[:, columns(j)], own(j), local.at[j])

    def act_copy(src, dst, index, device):
        return pltpu.make_async_remote_copy(
            src_ref=src, dst_ref=dst, send_sem=act_send.at[index], recv_sem=act_recv.at[index],
            device_id=device, device_id_type=MESH,
        )

    def load(src, dst, index):
        return pltpu.make_async_copy(src, dst, local.at[CHUNKS + index])

    def loads(kind):
        if kind == 3:
            return [
                load(pool_in.at[0], first.at[0:128], 0), load(pool_in.at[1], first.at[128:256], 1),
                load(val_in.at[0], first.at[256:384], 2),
                load(pool_top.at[0], second.at[0:128], 3), load(pool_top.at[1], second.at[128:256], 4),
                load(val_top.at[0], second.at[256:384], 5),
            ]
        if kind == 2:
            return [
                load(pool_in.at[0], first.at[0:128], 0), load(pool_in.at[1], first.at[128:256], 1),
                load(val_in.at[0], first.at[256:384], 2),
            ]
        if kind == 1:
            return [load(val_in.at[1], second.at[0:128], 0)]
        return [load(val_top.at[1], second.at[0:128], 0)]

    def sends(kind):
        if kind == 3:
            return [act_copy(val_in.at[1], first.at[0:128], 0, above)]
        if kind == 2:
            return [act_copy(val_in.at[1], first.at[0:128], 0, below)]
        if kind == 1:
            return [
                act_copy(pool_in.at[0], second.at[0:128], 0, above),
                act_copy(pool_in.at[1], second.at[128:256], 1, above),
                act_copy(val_in.at[0], second.at[256:384], 2, above),
            ]
        return []

    def receives(kind):
        if kind == 2:
            return [act_copy(second.at[i * 128:(i + 1) * 128], second.at[i * 128:(i + 1) * 128], i, above) for i in range(3)]
        if kind in (0, 1):
            return [act_copy(first.at[0:128], first.at[0:128], 0, above)]
        return []

    @pl.when(layer >= 2)
    def _():
        def body(j, carry):
            share_local(j).start()
            return carry
        lax.fori_loop(0, CHUNKS, body, 0)

    for kind, partner in ((3, above), (2, below)):
        @pl.when(layer == kind)
        def _():
            for copy in loads(kind):
                copy.start()
            for j in range(4):
                share_out(j, partner).start()
            for copy in sends(kind):
                copy.start()
            for j in range(4, CHUNKS):
                share_out(j, partner).start()
    for kind in (1, 0):
        @pl.when(layer == kind)
        def _():
            for copy in loads(kind) + sends(kind):
                copy.start()

    def have_share(j):
        @pl.when(layer >= 2)
        def _():
            share_local(j).wait()

        @pl.when(layer < 2)
        def _():
            arrived(own(j), j, 12)

    half = SHARE // 2

    def stage_share(p):
        a, b = 2 * p, 2 * p + 1
        have_share(a)
        push(own(a), a, 0, at(xp, z, c))
        push(own(a), a, 1, at(xm, z, c))
        have_share(b)
        push(own(b), b, 0, at(x, zp, c))
        push(own(b), b, 1, at(x, zm, c))

    def stage_forward(p):
        a, b = 2 * p, 2 * p + 1
        arrived(held.at[a, xm, z, c], a, 0)
        push(held.at[a, xm, z, c, 0:half], a, 2, at(xp, z, c))
        arrived(held.at[b, x, zm, c], b, 0)
        push(held.at[b, x, zm, c, 0:half], b, 2, at(x, zp, c))
        arrived(held.at[a, xp, z, c], a, 1)
        push(held.at[a, xp, z, c, half:SHARE], a, 3, at(xm, z, c))
        arrived(held.at[b, x, zp, c], b, 1)
        push(held.at[b, x, zp, c, half:SHARE], b, 3, at(x, zm, c))

    def stage_row(p):
        a, b = 2 * p, 2 * p + 1
        arrived(held.at[a, xo, z, c, 0:half], a, 2)
        arrived(held.at[a, xo, z, c, half:SHARE], a, 3)
        push(held.at[a, :, z, c], a, 4, at(x, zp, c))
        push(held.at[a, :, z, c], a, 5, at(x, zm, c))
        arrived(held.at[b, x, zo, c, 0:half], b, 2)
        arrived(held.at[b, x, zo, c, half:SHARE], b, 3)
        push(held.at[b, x, :, c], b, 4, at(xp, z, c))
        push(held.at[b, x, :, c], b, 5, at(xm, z, c))
        push(held.at[a, :, z, c], a, 8, at(x, z, other))
        push(held.at[b, x, :, c], b, 8, at(x, z, other))

    def stage_row_forward(p):
        a, b = 2 * p, 2 * p + 1
        arrived(held.at[a, :, zm, c], a, 4)
        push(held.at[a, 0:2, zm, c], a, 6, at(x, zp, c))
        arrived(held.at[b, xm, :, c], b, 4)
        push(held.at[b, xm, 0:2, c], b, 6, at(xp, z, c))
        arrived(held.at[a, :, zp, c], a, 5)
        push(held.at[a, 2:4, zp, c], a, 7, at(x, zm, c))
        arrived(held.at[b, xp, :, c], b, 5)
        push(held.at[b, xp, 2:4, c], b, 7, at(xm, z, c))
        push(held.at[a, :, zm, c], a, 9, at(x, z, other))
        push(held.at[b, xm, :, c], b, 9, at(x, z, other))
        push(held.at[a, :, zp, c], a, 10, at(x, z, other))
        push(held.at[b, xp, :, c], b, 10, at(x, z, other))

    def stage_last(p):
        a, b = 2 * p, 2 * p + 1
        arrived(held.at[a, 0:2, zo, c], a, 6)
        arrived(held.at[a, 2:4, zo, c], a, 7)
        push(held.at[a, :, zo, c], a, 11, at(x, z, other))
        arrived(held.at[b, xo, 0:2, c], b, 6)
        arrived(held.at[b, xo, 2:4, c], b, 7)
        push(held.at[b, xo, :, c], b, 11, at(x, z, other))

    def stage_whole(p):
        a, b = 2 * p, 2 * p + 1
        for slot, zi in ((8, z), (9, zm), (10, zp), (11, zo)):
            arrived(held.at[a, :, zi, other], a, slot)
        for slot, xi in ((8, x), (9, xm), (10, xp), (11, xo)):
            arrived(held.at[b, xi, :, other], b, slot)

    def gate(rows, block):
        base = pl.multiple_of(block * 32, 32)
        value = first[pl.ds(base, 32), :].astype(jnp.float32)
        top = second[pl.ds(base, 32), :].astype(jnp.float32)
        gated[pl.ds(base, 32), :] = (top * silu_slope(value)).astype(jnp.bfloat16)

    def gate_all(rows):
        def body(block, carry):
            gate(rows, block)
            return carry
        lax.fori_loop(0, rows // 32, body, 0)

    def grad_copy(j, rows, device):
        return pltpu.make_async_remote_copy(
            src_ref=grad.at[j, 0:rows], dst_ref=grad.at[j, 0:rows],
            send_sem=grad_send.at[j], recv_sem=grad_recv.at[j],
            device_id=device, device_id_type=MESH,
        )

    def upper_chunk(j, rows, device):
        total[0, 0:rows] = second[0:rows, columns(j)].astype(jnp.float32)

        def body(xi, carry):
            block = held[j, xi].reshape(WIDTH // 4, COLS)
            left = gated[0:rows, pl.ds(pl.multiple_of(xi * (WIDTH // 4), WIDTH // 4), WIDTH // 4)]
            total[0, 0:rows] += jnp.dot(left, block, preferred_element_type=jnp.float32)
            return carry
        lax.fori_loop(0, 4, body, 0)
        grad[j, 0:rows] = total[0, 0:rows].astype(jnp.bfloat16)
        grad_copy(j, rows, device).start()

    def add_product(n, q, rows):
        block = held[n, q // 2, pl.ds(2 * (q % 2), 2)].reshape(4 * SHARE, COLS)
        left = gated[0:rows, pl.ds(pl.multiple_of(q * 2 * COLS, 2 * COLS), 2 * COLS)]
        total[n, 0:rows] += jnp.dot(left, block, preferred_element_type=jnp.float32)

    def lower_weight(n, ready, rows):
        total[n, 0:rows] = jnp.zeros((rows, COLS), jnp.float32)

        def body(k, carry):
            add_product(n, k, rows)
            return carry
        lax.fori_loop(0, ready, body, 0)

    def lower_grad(q, ready, rows):
        for k in (2 * q, 2 * q + 1):
            grad_copy(k, rows, above).wait_recv()

            def gating(block, carry):
                base = pl.multiple_of(block * 64, 64)
                value = first[pl.ds(base, 64), columns(k)].astype(jnp.float32)
                up = grad[k, pl.ds(base, 64)].astype(jnp.float32)
                gated[pl.ds(base, 64), columns(k)] = (up * silu_slope(value)).astype(jnp.bfloat16)
                return carry
            lax.fori_loop(0, rows // 64, gating, 0)

        def body(n, carry):
            add_product(n, q, rows)
            return carry
        lax.fori_loop(0, ready, body, 0)

    def upper_use(p, rows, device):
        upper_chunk(2 * p, rows, device)
        upper_chunk(2 * p + 1, rows, device)

    def lower_use(p, ready, rows):
        lower_weight(2 * p, ready, rows)
        lower_weight(2 * p + 1, ready, rows)

    def when_in(t, lag, what):
        @pl.when((t >= lag) & (t < PAIRS + lag))
        def _():
            what(t - lag)

    def step(t, carry):
        when_in(t, 0, stage_share)
        when_in(t, LAG_FORWARD, stage_forward)
        when_in(t, LAG_ROW, stage_row)
        when_in(t, LAG_ROW_FORWARD, stage_row_forward)
        when_in(t, LAG_LAST, stage_last)

        @pl.when((t == 0) & (layer == 3))
        def _():
            for copy in loads(3):
                copy.wait()
            gate_all(MAIN)

        @pl.when((t == 0) & (layer == 2))
        def _():
            for copy in loads(2):
                copy.wait()

        when_in(t, LAG_USE, stage_whole)

        @pl.when((t == LAG_USE + CATCH_UP) & (layer == 0))
        def _():
            for copy in loads(0):
                copy.wait()
            for copy in receives(0):
                copy.wait_recv()
            gate_all(REST)

            def body(j, carry):
                upper_chunk(j, REST, above)
                return carry
            lax.fori_loop(0, 2 * CATCH_UP, body, 0)

        @pl.when((t == LAG_USE) & (layer == 1))
        def _():
            for copy in loads(1):
                copy.wait()
            for copy in receives(1):
                copy.wait_recv()

        @pl.when((layer == 3) & (t >= LAG_USE) & (t < PAIRS + LAG_USE))
        def _():
            upper_use(t - LAG_USE, MAIN, below)

        @pl.when((layer == 0) & (t >= LAG_USE + CATCH_UP) & (t < PAIRS + LAG_USE))
        def _():
            upper_use(t - LAG_USE, REST, above)

        whole = jnp.minimum(2 * (t - LAG_USE) + 2, CHUNKS)

        @pl.when((layer == 2) & (t >= LAG_USE) & (t < PAIRS + LAG_USE))
        def _():
            lower_use(t - LAG_USE, jnp.maximum(t - LAG_GRAD, 0), MAIN)

        @pl.when((layer == 2) & (t >= LAG_GRAD) & (t < PAIRS + LAG_GRAD))
        def _():
            lower_grad(t - LAG_GRAD, whole, MAIN)

        first_rest = LAG_USE + CATCH_UP + 1

        @pl.when((layer == 1) & (t >= LAG_USE) & (t < PAIRS + LAG_USE))
        def _():
            since = jnp.maximum(t - first_rest, 0)
            lower_use(t - LAG_USE, jnp.where(since < 3, 2 * since, since + 3), REST)

        @pl.when((layer == 1) & (t >= first_rest) & (t < first_rest + 3))
        def _():
            q = 2 * (t - first_rest)
            lower_grad(q, whole, REST)
            lower_grad(q + 1, whole, REST)

        @pl.when((layer == 1) & (t >= first_rest + 3) & (t < first_rest + 5))
        def _():
            lower_grad(t - first_rest + 3, whole, REST)
        return carry

    lax.fori_loop(0, max(PAIRS + LAG_GRAD, LAG_USE + CATCH_UP + 6), step, 0)

    def finish(kind, rows):
        for copy in receives(kind) if kind == 2 else ():
            copy.wait_recv()

        def body(n, carry):
            def inner(block, inner_carry):
                base = pl.multiple_of(block * 64, 64)
                up = grad[n, pl.ds(base, 64)].astype(jnp.float32)
                value = second[pl.ds(base, 64), columns(n)].astype(jnp.float32)
                low = (up + total[n, pl.ds(base, 64)]).astype(jnp.bfloat16)
                first[pl.ds(base, 64), columns(n)] = low
                gated[pl.ds(base, 64), columns(n)] = (low.astype(jnp.float32) * silu_slope(value)).astype(jnp.bfloat16)
                return inner_carry
            lax.fori_loop(0, rows // 64, inner, 0)
            return carry
        lax.fori_loop(0, CHUNKS, body, 0)
        copies = [
            pltpu.make_async_copy(grad.at[:, 0:rows], grad2_out.at[:, 0:rows], out_sem.at[0]),
            pltpu.make_async_copy(first.at[0:rows], grad1_out.at[0:rows], out_sem.at[1]),
            pltpu.make_async_copy(gated.at[0:rows], gated_out.at[0:rows], out_sem.at[2]),
        ]
        for copy in copies:
            copy.start()
        for copy in copies:
            copy.wait()

    for kind, rows in ((2, MAIN), (1, REST)):
        @pl.when(layer == kind)
        def _():
            finish(kind, rows)

    def drain(p, carry):
        a, b = 2 * p, 2 * p + 1
        there = at(x, z, other)

        def left(ref, j, slot):
            remote(ref, ref, j, slot, there).wait_send()
        for slot in (0, 1):
            left(own(a), a, slot)
            left(own(b), b, slot)
        for slot in (2, 3):
            left(held.at[a, xm, z, c, 0:half], a, slot)
            left(held.at[b, x, zm, c, 0:half], b, slot)
        for slot in (4, 5, 8, 9, 10, 11):
            left(held.at[a, :, z, c], a, slot)
            left(held.at[b, x, :, c], b, slot)
        for slot in (6, 7):
            left(held.at[a, 0:2, z, c], a, slot)
            left(held.at[b, x, 0:2, c], b, slot)

        @pl.when(layer >= 2)
        def _():
            left(own(a), a, 12)
            left(own(b), b, 12)

        for kind, rows in ((3, MAIN), (0, REST)):
            @pl.when(layer == kind)
            def _():
                grad_copy(a, rows, above).wait_send()
                grad_copy(b, rows, above).wait_send()
        return carry
    lax.fori_loop(0, PAIRS, drain, 0)
    for kind in (3, 2, 1):
        @pl.when(layer == kind)
        def _():
            for copy in sends(kind):
                copy.wait_send()


def chain(pool_in, val_in, pool_top, val_top, weight):
    anywhere = pl.BlockSpec(memory_space=pl.ANY)
    wide = jax.ShapeDtypeStruct((MAIN, WIDTH), jnp.bfloat16)
    return pl.pallas_call(
        chain_kernel,
        out_shape=(jax.ShapeDtypeStruct((CHUNKS, MAIN, COLS), jnp.bfloat16), wide, wide),
        in_specs=[anywhere] * 5,
        out_specs=(anywhere,) * 3,
        scratch_shapes=[
            pltpu.VMEM((CHUNKS, 4, 4, 2, SHARE, COLS), jnp.bfloat16),
            pltpu.VMEM((MAIN, WIDTH), jnp.bfloat16),
            pltpu.VMEM((MAIN, WIDTH), jnp.bfloat16),
            pltpu.VMEM((MAIN, WIDTH), jnp.bfloat16),
            pltpu.VMEM((CHUNKS, MAIN, COLS), jnp.bfloat16),
            pltpu.VMEM((CHUNKS, MAIN, COLS), jnp.float32),
            pltpu.SemaphoreType.DMA((CHUNKS, SLOTS)),
            pltpu.SemaphoreType.DMA((CHUNKS, SLOTS)),
            pltpu.SemaphoreType.DMA((CHUNKS,)),
            pltpu.SemaphoreType.DMA((CHUNKS,)),
            pltpu.SemaphoreType.DMA((3,)),
            pltpu.SemaphoreType.DMA((3,)),
            pltpu.SemaphoreType.DMA((CHUNKS + 6,)),
            pltpu.SemaphoreType.DMA((3,)),
        ],
        compiler_params=pltpu.CompilerParams(
            collective_id=0, has_side_effects=True, vmem_limit_bytes=60 * 1024 * 1024
        ),
        cost_estimate=pl.CostEstimate(flops=26_000_000_000, bytes_accessed=30_000_000, transcendentals=3_000_000),
        name="chain",
    )(pool_in, val_in, pool_top, val_top, weight)


def damped_inverse(factor):
    size_rank = factor.shape[0]
    identity = jnp.eye(size_rank, dtype=jnp.float32)
    damping = 0.1 * jnp.trace(factor) / size_rank
    lower_factor = jnp.linalg.cholesky(factor + damping * identity)
    return jax.scipy.linalg.cho_solve((lower_factor, True), identity)


def sent(value, pairs):
    return lax.ppermute(value, "layer", pairs)


def on_device(
    pool_inputs, val_inputs, pool_top, val_top, weight, proj_in, proj_out, pool_len, val_len
):
    highest = lax.Precision.HIGHEST
    rank = proj_in.shape[2]
    pool_local, val_local = pool_top.shape[0], val_top.shape[0]
    layer = lax.axis_index("layer")
    f32 = jnp.float32

    projections = lax.all_gather(proj_out[0], "layer", axis=0)
    grad2, grad1, gated1 = chain(pool_inputs[0], val_inputs[0], pool_top, val_top, weight[0])
    folded = jnp.dot(weight[0], projections[0], preferred_element_type=f32).astype(jnp.bfloat16)
    folded = lax.all_gather(folded, "trace", axis=0, tiled=True)
    folded = jnp.where(layer == 2, sent(folded, [(1, 2)]), folded)

    flat_top = jnp.concatenate([pool_top, val_top], 0).reshape(-1, WIDTH)
    low_top = jnp.dot(flat_top, proj_out[0], preferred_element_type=f32)
    flat_inputs = jnp.concatenate([pool_inputs[0], val_inputs[0]], 0).reshape(-1, WIDTH)
    low_in = jnp.dot(flat_inputs, proj_in[0], preferred_element_type=f32)

    low2 = sum(
        jnp.dot(grad2[n], lax.dynamic_slice_in_dim(projections[2], n * COLS, COLS, 0), preferred_element_type=f32)
        for n in range(CHUNKS)
    )
    low1 = jnp.dot(grad1, projections[1], preferred_element_type=f32)
    low0 = jnp.dot(grad1, projections[0], preferred_element_type=f32) + jnp.dot(
        gated1, folded, preferred_element_type=f32
    )
    down = sent(jnp.where(layer == 2, low1, low0), [(2, 1), (1, 0)])
    up = sent(low2[:REST], [(1, 2)])
    far = sent(low0, [(2, 0)])
    main = jnp.where(layer == 2, low2, jnp.where(layer == 1, down, far))
    rest = jnp.where(layer == 2, up, jnp.where(layer == 1, low1[:REST], down[:REST]))
    low_out = jnp.where(layer == 3, low_top, jnp.concatenate([main, rest], 0))

    positions = jnp.arange(TOKENS, dtype=jnp.int32)
    lengths = jnp.concatenate([pool_len, val_len], 0)
    valid = positions[None, :] < lengths[:, None]
    grad_low = jnp.where(valid[:, :, None], low_out.reshape(-1, TOKENS, rank), 0.0)
    input_low = jnp.where(valid[:, :, None], low_in.reshape(-1, TOKENS, rank), 0.0)
    trace_grads = jnp.einsum("nti,ntj->nij", grad_low, input_low, precision=highest)
    pool_grads, val_grads = trace_grads[:pool_local], trace_grads[pool_local:]
    pool_in = input_low[:pool_local].reshape(-1, rank)
    pool_out = grad_low[:pool_local].reshape(-1, rank)
    local_in = jnp.dot(pool_in.T, pool_in, precision=highest)
    local_out = jnp.dot(pool_out.T, pool_out, precision=highest)
    local_count = jnp.sum(pool_len).astype(f32)
    factor_in, factor_out, token_count = lax.psum((local_in, local_out, local_count), "trace")
    inv_in = damped_inverse(factor_in / token_count)
    inv_out = damped_inverse(factor_out / token_count)
    scaled = jnp.einsum("ab,nbc,cd->nad", inv_out, val_grads, inv_in, precision=highest)
    everything = lax.all_gather(scaled.reshape(val_local, rank * rank), "trace", axis=0, tiled=True)
    partial_scores = jnp.dot(pool_grads.reshape(pool_local, rank * rank), everything.T, precision=highest)
    summed = lax.psum_scatter(partial_scores, "layer", scatter_dimension=1, tiled=True)
    return summed / (rank * TOKENS)


def solution(mesh):
    placed = (
        P("layer", "trace", None, None),
        P("layer", "trace", None, None),
        P("trace", None, None),
        P("trace", None, None),
        P("layer", "trace", None),
        P("layer", None, None),
        P("layer", None, None),
        P("trace"),
        P("trace"),
    )
    return jax.shard_map(
        on_device, mesh=mesh, in_specs=placed, out_specs=P("trace", "layer"), check_vma=False
    )
```

```python
import functools

import jax
import jax.numpy as jnp
from jax import lax
from jax.experimental import pallas as pl
from jax.experimental.pallas import tpu as pltpu
from jax.sharding import PartitionSpec as P

MESH = pl.DeviceIdType.MESH
WIDTH = 4096
TOKENS = 128
RANK = 64
CHUNKS = 16
COLS = WIDTH // CHUNKS
PAIRS = CHUNKS // 2
SHARE = 128
MAIN = 384
REST = 128
LAG_FORWARD, LAG_ROW, LAG_ROW_FORWARD, LAG_LAST, LAG_USE = 1, 2, 3, 4, 5
LAG_GRAD = 6
CATCH_UP = 3
SLOTS = 13


def silu_slope(values):
    logistic = jax.nn.sigmoid(values)
    return logistic * (1.0 + values * (1.0 - logistic))


def chain_kernel(
    pool_in, val_in, pool_top, val_top, weight,
    grad2_out, grad1_out, gated_out,
    held, first, second, gated, grad, total,
    send, recv, grad_send, grad_recv, act_send, act_recv, local, out_sem,
):
    layer = lax.axis_index("layer")
    trace = lax.axis_index("trace")
    x, z, c = trace // 8, (trace // 2) % 4, trace % 2
    xp, xm, xo = (x + 1) % 4, (x + 3) % 4, (x + 2) % 4
    zp, zm, zo = (z + 1) % 4, (z + 3) % 4, (z + 2) % 4
    other = 1 - c

    def at(xi, zi, ci):
        return {"trace": xi * 8 + zi * 2 + ci}

    above = {"layer": (layer + 1) % 4}
    below = {"layer": (layer + 3) % 4}

    barrier = pltpu.get_barrier_semaphore()
    for device in (at(xp, z, c), at(xm, z, c), at(x, zp, c), at(x, zm, c), at(x, z, other), above, below):
        pl.semaphore_signal(barrier, inc=1, device_id=device, device_id_type=MESH)
    pl.semaphore_wait(barrier, 7)

    def columns(j):
        return pl.ds(pl.multiple_of(j * COLS, COLS), COLS)

    def remote(src, dst, j, slot, device):
        return pltpu.make_async_remote_copy(
            src_ref=src, dst_ref=dst, send_sem=send.at[j, slot], recv_sem=recv.at[j, slot],
            device_id=device, device_id_type=MESH,
        )

    def arrived(ref, j, slot):
        remote(ref, ref, j, slot, at(x, z, other)).wait_recv()

    def push(ref, j, slot, device):
        remote(ref, ref, j, slot, device).start()

    def own(j):
        return held.at[j, x, z, c]

    def share_out(j, device):
        return remote(weight.at[:, columns(j)], own(j), j, 12, device)

    def share_local(j):
        return pltpu.make_async_copy(weight.at[:, columns(j)], own(j), local.at[j])

    def act_copy(src, dst, index, device):
        return pltpu.make_async_remote_copy(
            src_ref=src, dst_ref=dst, send_sem=act_send.at[index], recv_sem=act_recv.at[index],
            device_id=device, device_id_type=MESH,
        )

    def load(src, dst, index):
        return pltpu.make_async_copy(src, dst, local.at[CHUNKS + index])

    def loads(kind):
        if kind == 3:
            return [
                load(pool_in.at[0], first.at[0:128], 0), load(pool_in.at[1], first.at[128:256], 1),
                load(val_in.at[0], first.at[256:384], 2),
                load(pool_top.at[0], second.at[0:128], 3), load(pool_top.at[1], second.at[128:256], 4),
                load(val_top.at[0], second.at[256:384], 5),
            ]
        if kind == 2:
            return [
                load(pool_in.at[0], first.at[0:128], 0), load(pool_in.at[1], first.at[128:256], 1),
                load(val_in.at[0], first.at[256:384], 2),
            ]
        if kind == 1:
            return [load(val_in.at[1], second.at[0:128], 0)]
        return [load(val_top.at[1], second.at[0:128], 0)]

    def sends(kind):
        if kind == 3:
            return [act_copy(val_in.at[1], first.at[0:128], 0, above)]
        if kind == 2:
            return [act_copy(val_in.at[1], first.at[0:128], 0, below)]
        if kind == 1:
            return [
                act_copy(pool_in.at[0], second.at[0:128], 0, above),
                act_copy(pool_in.at[1], second.at[128:256], 1, above),
                act_copy(val_in.at[0], second.at[256:384], 2, above),
            ]
        return []

    def receives(kind):
        if kind == 2:
            return [act_copy(second.at[i * 128:(i + 1) * 128], second.at[i * 128:(i + 1) * 128], i, above) for i in range(3)]
        if kind in (0, 1):
            return [act_copy(first.at[0:128], first.at[0:128], 0, above)]
        return []

    @pl.when(layer >= 2)
    def _():
        def body(j, carry):
            share_local(j).start()
            return carry
        lax.fori_loop(0, CHUNKS, body, 0)

    for kind, partner in ((3, above), (2, below)):
        @pl.when(layer == kind)
        def _():
            for copy in loads(kind):
                copy.start()
            for j in range(4):
                share_out(j, partner).start()
            for copy in sends(kind):
                copy.start()
            for j in range(4, CHUNKS):
                share_out(j, partner).start()
    for kind in (1, 0):
        @pl.when(layer == kind)
        def _():
            for copy in loads(kind) + sends(kind):
                copy.start()

    def have_share(j):
        @pl.when(layer >= 2)
        def _():
            share_local(j).wait()

        @pl.when(layer < 2)
        def _():
            arrived(own(j), j, 12)

    half = SHARE // 2

    def stage_share(p):
        a, b = 2 * p, 2 * p + 1
        have_share(a)
        push(own(a), a, 0, at(xp, z, c))
        push(own(a), a, 1, at(xm, z, c))
        have_share(b)
        push(own(b), b, 0, at(x, zp, c))
        push(own(b), b, 1, at(x, zm, c))

    def stage_forward(p):
        a, b = 2 * p, 2 * p + 1
        arrived(held.at[a, xm, z, c], a, 0)
        push(held.at[a, xm, z, c, 0:half], a, 2, at(xp, z, c))
        arrived(held.at[b, x, zm, c], b, 0)
        push(held.at[b, x, zm, c, 0:half], b, 2, at(x, zp, c))
        arrived(held.at[a, xp, z, c], a, 1)
        push(held.at[a, xp, z, c, half:SHARE], a, 3, at(xm, z, c))
        arrived(held.at[b, x, zp, c], b, 1)
        push(held.at[b, x, zp, c, half:SHARE], b, 3, at(x, zm, c))

    def stage_row(p):
        a, b = 2 * p, 2 * p + 1
        arrived(held.at[a, xo, z, c, 0:half], a, 2)
        arrived(held.at[a, xo, z, c, half:SHARE], a, 3)
        push(held.at[a, :, z, c], a, 4, at(x, zp, c))
        push(held.at[a, :, z, c], a, 5, at(x, zm, c))
        arrived(held.at[b, x, zo, c, 0:half], b, 2)
        arrived(held.at[b, x, zo, c, half:SHARE], b, 3)
        push(held.at[b, x, :, c], b, 4, at(xp, z, c))
        push(held.at[b, x, :, c], b, 5, at(xm, z, c))
        push(held.at[a, :, z, c], a, 8, at(x, z, other))
        push(held.at[b, x, :, c], b, 8, at(x, z, other))

    def stage_row_forward(p):
        a, b = 2 * p, 2 * p + 1
        arrived(held.at[a, :, zm, c], a, 4)
        push(held.at[a, 0:2, zm, c], a, 6, at(x, zp, c))
        arrived(held.at[b, xm, :, c], b, 4)
        push(held.at[b, xm, 0:2, c], b, 6, at(xp, z, c))
        arrived(held.at[a, :, zp, c], a, 5)
        push(held.at[a, 2:4, zp, c], a, 7, at(x, zm, c))
        arrived(held.at[b, xp, :, c], b, 5)
        push(held.at[b, xp, 2:4, c], b, 7, at(xm, z, c))
        push(held.at[a, :, zm, c], a, 9, at(x, z, other))
        push(held.at[b, xm, :, c], b, 9, at(x, z, other))
        push(held.at[a, :, zp, c], a, 10, at(x, z, other))
        push(held.at[b, xp, :, c], b, 10, at(x, z, other))

    def stage_last(p):
        a, b = 2 * p, 2 * p + 1
        arrived(held.at[a, 0:2, zo, c], a, 6)
        arrived(held.at[a, 2:4, zo, c], a, 7)
        push(held.at[a, :, zo, c], a, 11, at(x, z, other))
        arrived(held.at[b, xo, 0:2, c], b, 6)
        arrived(held.at[b, xo, 2:4, c], b, 7)
        push(held.at[b, xo, :, c], b, 11, at(x, z, other))

    def stage_whole(p):
        a, b = 2 * p, 2 * p + 1
        for slot, zi in ((8, z), (9, zm), (10, zp), (11, zo)):
            arrived(held.at[a, :, zi, other], a, slot)
        for slot, xi in ((8, x), (9, xm), (10, xp), (11, xo)):
            arrived(held.at[b, xi, :, other], b, slot)

    def gate(rows, block):
        base = pl.multiple_of(block * 32, 32)
        value = first[pl.ds(base, 32), :].astype(jnp.float32)
        top = second[pl.ds(base, 32), :].astype(jnp.float32)
        gated[pl.ds(base, 32), :] = (top * silu_slope(value)).astype(jnp.bfloat16)

    def gate_all(rows):
        def body(block, carry):
            gate(rows, block)
            return carry
        lax.fori_loop(0, rows // 32, body, 0)

    def grad_copy(j, rows, device):
        return pltpu.make_async_remote_copy(
            src_ref=grad.at[j, 0:rows], dst_ref=grad.at[j, 0:rows],
            send_sem=grad_send.at[j], recv_sem=grad_recv.at[j],
            device_id=device, device_id_type=MESH,
        )

    def upper_chunk(j, rows, device):
        total[0, 0:rows] = second[0:rows, columns(j)].astype(jnp.float32)

        def body(xi, carry):
            block = held[j, xi].reshape(WIDTH // 4, COLS)
            left = gated[0:rows, pl.ds(pl.multiple_of(xi * (WIDTH // 4), WIDTH // 4), WIDTH // 4)]
            total[0, 0:rows] += jnp.dot(left, block, preferred_element_type=jnp.float32)
            return carry
        lax.fori_loop(0, 4, body, 0)
        grad[j, 0:rows] = total[0, 0:rows].astype(jnp.bfloat16)
        grad_copy(j, rows, device).start()

    def add_product(n, q, rows):
        block = held[n, q // 2, pl.ds(2 * (q % 2), 2)].reshape(4 * SHARE, COLS)
        left = gated[0:rows, pl.ds(pl.multiple_of(q * 2 * COLS, 2 * COLS), 2 * COLS)]
        total[n, 0:rows] += jnp.dot(left, block, preferred_element_type=jnp.float32)

    def lower_weight(n, ready, rows):
        total[n, 0:rows] = jnp.zeros((rows, COLS), jnp.float32)

        def body(k, carry):
            add_product(n, k, rows)
            return carry
        lax.fori_loop(0, ready, body, 0)

    def lower_grad(q, ready, rows):
        for k in (2 * q, 2 * q + 1):
            grad_copy(k, rows, above).wait_recv()

            def gating(block, carry):
                base = pl.multiple_of(block * 64, 64)
                value = first[pl.ds(base, 64), columns(k)].astype(jnp.float32)
                up = grad[k, pl.ds(base, 64)].astype(jnp.float32)
                gated[pl.ds(base, 64), columns(k)] = (up * silu_slope(value)).astype(jnp.bfloat16)
                return carry
            lax.fori_loop(0, rows // 64, gating, 0)

        def body(n, carry):
            add_product(n, q, rows)
            return carry
        lax.fori_loop(0, ready, body, 0)

    def upper_use(p, rows, device):
        upper_chunk(2 * p, rows, device)
        upper_chunk(2 * p + 1, rows, device)

    def lower_use(p, ready, rows):
        lower_weight(2 * p, ready, rows)
        lower_weight(2 * p + 1, ready, rows)

    def when_in(t, lag, what):
        @pl.when((t >= lag) & (t < PAIRS + lag))
        def _():
            what(t - lag)

    def step(t, carry):
        when_in(t, 0, stage_share)
        when_in(t, LAG_FORWARD, stage_forward)
        when_in(t, LAG_ROW, stage_row)
        when_in(t, LAG_ROW_FORWARD, stage_row_forward)
        when_in(t, LAG_LAST, stage_last)

        @pl.when((t == 0) & (layer == 3))
        def _():
            for copy in loads(3):
                copy.wait()
            gate_all(MAIN)

        @pl.when((t == 0) & (layer == 2))
        def _():
            for copy in loads(2):
                copy.wait()

        when_in(t, LAG_USE, stage_whole)

        @pl.when((t == LAG_USE + CATCH_UP) & (layer == 0))
        def _():
            for copy in loads(0):
                copy.wait()
            for copy in receives(0):
                copy.wait_recv()
            gate_all(REST)

            def body(j, carry):
                upper_chunk(j, REST, above)
                return carry
            lax.fori_loop(0, 2 * CATCH_UP, body, 0)

        @pl.when((t == LAG_USE) & (layer == 1))
        def _():
            for copy in loads(1):
                copy.wait()
            for copy in receives(1):
                copy.wait_recv()

        @pl.when((layer == 3) & (t >= LAG_USE) & (t < PAIRS + LAG_USE))
        def _():
            upper_use(t - LAG_USE, MAIN, below)

        @pl.when((layer == 0) & (t >= LAG_USE + CATCH_UP) & (t < PAIRS + LAG_USE))
        def _():
            upper_use(t - LAG_USE, REST, above)

        whole = jnp.minimum(2 * (t - LAG_USE) + 2, CHUNKS)

        @pl.when((layer == 2) & (t >= LAG_USE) & (t < PAIRS + LAG_USE))
        def _():
            lower_use(t - LAG_USE, jnp.maximum(t - LAG_GRAD, 0), MAIN)

        @pl.when((layer == 2) & (t >= LAG_GRAD) & (t < PAIRS + LAG_GRAD))
        def _():
            lower_grad(t - LAG_GRAD, whole, MAIN)

        first_rest = LAG_USE + CATCH_UP + 1

        @pl.when((layer == 1) & (t >= LAG_USE) & (t < PAIRS + LAG_USE))
        def _():
            since = jnp.maximum(t - first_rest, 0)
            lower_use(t - LAG_USE, jnp.where(since < 3, 2 * since, since + 3), REST)

        @pl.when((layer == 1) & (t >= first_rest) & (t < first_rest + 3))
        def _():
            q = 2 * (t - first_rest)
            lower_grad(q, whole, REST)
            lower_grad(q + 1, whole, REST)

        @pl.when((layer == 1) & (t >= first_rest + 3) & (t < first_rest + 5))
        def _():
            lower_grad(t - first_rest + 3, whole, REST)
        return carry

    lax.fori_loop(0, max(PAIRS + LAG_GRAD, LAG_USE + CATCH_UP + 6), step, 0)

    def finish(kind, rows):
        for copy in receives(kind) if kind == 2 else ():
            copy.wait_recv()

        def body(n, carry):
            def inner(block, inner_carry):
                base = pl.multiple_of(block * 64, 64)
                up = grad[n, pl.ds(base, 64)].astype(jnp.float32)
                value = second[pl.ds(base, 64), columns(n)].astype(jnp.float32)
                low = (up + total[n, pl.ds(base, 64)]).astype(jnp.bfloat16)
                first[pl.ds(base, 64), columns(n)] = low
                gated[pl.ds(base, 64), columns(n)] = (low.astype(jnp.float32) * silu_slope(value)).astype(jnp.bfloat16)
                return inner_carry
            lax.fori_loop(0, rows // 64, inner, 0)
            return carry
        lax.fori_loop(0, CHUNKS, body, 0)
        copies = [
            pltpu.make_async_copy(grad.at[:, 0:rows], grad2_out.at[:, 0:rows], out_sem.at[0]),
            pltpu.make_async_copy(first.at[0:rows], grad1_out.at[0:rows], out_sem.at[1]),
            pltpu.make_async_copy(gated.at[0:rows], gated_out.at[0:rows], out_sem.at[2]),
        ]
        for copy in copies:
            copy.start()
        for copy in copies:
            copy.wait()

    for kind, rows in ((2, MAIN), (1, REST)):
        @pl.when(layer == kind)
        def _():
            finish(kind, rows)

    def drain(p, carry):
        a, b = 2 * p, 2 * p + 1
        there = at(x, z, other)

        def left(ref, j, slot):
            remote(ref, ref, j, slot, there).wait_send()
        for slot in (0, 1):
            left(own(a), a, slot)
            left(own(b), b, slot)
        for slot in (2, 3):
            left(held.at[a, xm, z, c, 0:half], a, slot)
            left(held.at[b, x, zm, c, 0:half], b, slot)
        for slot in (4, 5, 8, 9, 10, 11):
            left(held.at[a, :, z, c], a, slot)
            left(held.at[b, x, :, c], b, slot)
        for slot in (6, 7):
            left(held.at[a, 0:2, z, c], a, slot)
            left(held.at[b, x, 0:2, c], b, slot)

        @pl.when(layer >= 2)
        def _():
            left(own(a), a, 12)
            left(own(b), b, 12)

        for kind, rows in ((3, MAIN), (0, REST)):
            @pl.when(layer == kind)
            def _():
                grad_copy(a, rows, above).wait_send()
                grad_copy(b, rows, above).wait_send()
        return carry
    lax.fori_loop(0, PAIRS, drain, 0)
    for kind in (3, 2, 1):
        @pl.when(layer == kind)
        def _():
            for copy in sends(kind):
                copy.wait_send()


def chain(pool_in, val_in, pool_top, val_top, weight):
    anywhere = pl.BlockSpec(memory_space=pl.ANY)
    wide = jax.ShapeDtypeStruct((MAIN, WIDTH), jnp.bfloat16)
    return pl.pallas_call(
        chain_kernel,
        out_shape=(jax.ShapeDtypeStruct((CHUNKS, MAIN, COLS), jnp.bfloat16), wide, wide),
        in_specs=[anywhere] * 5,
        out_specs=(anywhere,) * 3,
        scratch_shapes=[
            pltpu.VMEM((CHUNKS, 4, 4, 2, SHARE, COLS), jnp.bfloat16),
            pltpu.VMEM((MAIN, WIDTH), jnp.bfloat16),
            pltpu.VMEM((MAIN, WIDTH), jnp.bfloat16),
            pltpu.VMEM((MAIN, WIDTH), jnp.bfloat16),
            pltpu.VMEM((CHUNKS, MAIN, COLS), jnp.bfloat16),
            pltpu.VMEM((CHUNKS, MAIN, COLS), jnp.float32),
            pltpu.SemaphoreType.DMA((CHUNKS, SLOTS)),
            pltpu.SemaphoreType.DMA((CHUNKS, SLOTS)),
            pltpu.SemaphoreType.DMA((CHUNKS,)),
            pltpu.SemaphoreType.DMA((CHUNKS,)),
            pltpu.SemaphoreType.DMA((3,)),
            pltpu.SemaphoreType.DMA((3,)),
            pltpu.SemaphoreType.DMA((CHUNKS + 6,)),
            pltpu.SemaphoreType.DMA((3,)),
        ],
        compiler_params=pltpu.CompilerParams(
            collective_id=0, has_side_effects=True, vmem_limit_bytes=60 * 1024 * 1024
        ),
        cost_estimate=pl.CostEstimate(flops=26_000_000_000, bytes_accessed=30_000_000, transcendentals=3_000_000),
        name="chain",
    )(pool_in, val_in, pool_top, val_top, weight)


def low_half(shape):
    return lax.broadcasted_iota(jnp.int32, shape, len(shape) - 1) < RANK


def damped_inverses(pair):
    rows = lax.broadcasted_iota(jnp.int32, pair.shape, 0)
    lanes = lax.broadcasted_iota(jnp.int32, pair.shape, 1)
    lower = lanes < RANK
    column = jnp.where(lower, lanes, lanes - RANK)
    diagonal = rows == column
    on_diagonal = jnp.where(diagonal, pair, 0.0)
    trace_first = jnp.sum(jnp.where(lower, on_diagonal, 0.0), keepdims=True)
    trace_second = jnp.sum(jnp.where(lower, 0.0, on_diagonal), keepdims=True)
    damping = jnp.where(lower, trace_first, trace_second) * (0.1 / RANK)
    value = jnp.where(diagonal, pair + damping, pair)
    for k in range(RANK):
        left = jnp.where(
            lower,
            jnp.broadcast_to(value[:, k:k + 1], pair.shape),
            jnp.broadcast_to(value[:, RANK + k:RANK + k + 1], pair.shape),
        )
        pivot = 1.0 / left[k:k + 1]
        row = jnp.where(column[k:k + 1] == k, pivot, value[k:k + 1] * pivot)
        left = jnp.where(rows == k, -1.0, left)
        value = jnp.where((rows == k) | (column == k), 0.0, value) - left * row
    return value


def score_kernel(
    top_low, mid_low, in_low, counts, scores_out,
    landed, factors, factors_z, vals, layers,
    low_send, low_recv, fac_send, fac_recv, val_send, val_recv, facz_send, facz_recv, valz_send, valz_recv,
    lay_send, lay_recv,
):
    layer = lax.axis_index("layer")
    trace = lax.axis_index("trace")
    x, z, c = trace // 8, (trace // 2) % 4, trace % 2
    highest = lax.Precision.HIGHEST
    f32, bf16 = jnp.float32, jnp.bfloat16

    near = []
    for dx in range(4):
        for dc in range(2):
            if dx or dc:
                xi, ci = (x + dx) % 4, (c + dc) % 2
                near.append((xi * 2 + ci, xi, ci, {"trace": xi * 8 + z * 2 + ci}))
    across = [((z + dz) % 4, {"trace": x * 8 + (z + dz) % 4 * 2 + c}) for dz in (1, 3, 2)]
    planes = [((layer + dl) % 4, {"layer": (layer + dl) % 4}) for dl in (1, 3, 2)]
    barrier = pltpu.get_barrier_semaphore()
    for device in [n[3] for n in near] + [a[1] for a in across] + [q[1] for q in planes]:
        pl.semaphore_signal(barrier, inc=1, device_id=device, device_id_type=MESH)
    pl.semaphore_wait(barrier, len(near) + len(across) + len(planes))

    def copy(src, dst, send, recv, device):
        return pltpu.make_async_remote_copy(
            src_ref=src, dst_ref=dst, send_sem=send, recv_sem=recv, device_id=device, device_id_type=MESH
        )

    def low(source, slot, plane):
        return copy(source, landed.at[slot], low_send.at[slot + 3 * plane], low_recv.at[slot], {"layer": plane})

    def lows(kind):
        if kind == 2:
            return [low(mid_low.at[1, 0], 0, 1), low(mid_low.at[1, 1], 1, 1),
                    low(mid_low.at[0, 0], 0, 0), low(mid_low.at[0, 1], 1, 0)]
        if kind == 1:
            return [low(mid_low.at[0, 1], 2, 0), low(mid_low.at[2, 1], 2, 2)]
        return []

    def lows_in(kind):
        return [low(landed.at[slot], slot, (kind + 1) % 4) for slot in {3: (), 2: (2,), 1: (0, 1), 0: (0, 1, 2)}[kind]]

    for kind in (2, 1):
        @pl.when(layer == kind)
        def _():
            for item in lows(kind):
                item.start()

    @pl.when(layer == 3)
    def _():
        landed[0] = top_low[0]
        landed[1] = top_low[1]
        landed[2] = jnp.zeros_like(landed[2])

    @pl.when(layer == 2)
    def _():
        landed[0] = mid_low[2, 0]
        landed[1] = mid_low[2, 1]

    @pl.when(layer == 1)
    def _():
        landed[2] = mid_low[1, 1]

    for kind in (2, 1, 0):
        @pl.when(layer == kind)
        def _():
            for item in lows_in(kind):
                item.wait_recv()

    def across_tokens(left, right):
        return lax.dot_general(left, right, (((0,), (0,)), ((), ())), precision=highest, preferred_element_type=f32)

    wide = (RANK, 2 * RANK)
    lower = low_half(wide)

    def blocks(value):
        return jnp.where(lower, value[0:RANK], value[RANK:2 * RANK])

    def both(value):
        return value + pltpu.roll(value, RANK, 1)

    pool_out = landed[0].astype(f32)
    val_out = landed[1].astype(f32) + landed[2].astype(f32)
    pool_in, val_in = in_low[0], in_low[1]
    vals[x, z, c] = blocks(across_tokens(val_out, val_in)).astype(bf16)
    part_in = both(blocks(across_tokens(pool_in, pool_in)))
    part_out = both(blocks(across_tokens(pool_out, pool_out)))
    factors[x * 2 + c, 0:RANK] = jnp.where(lower, part_in, part_out)
    factors[x * 2 + c, RANK:RANK + 8] = counts[...]

    mine = x * 2 + c
    first = [copy(factors.at[mine], factors.at[mine], fac_send.at[i], fac_recv.at[mine], n[3]) for i, n in enumerate(near)]
    first += [copy(vals.at[x, z, c], vals.at[x, z, c], val_send.at[i], val_recv.at[mine], n[3]) for i, n in enumerate(near)]
    for item in first:
        item.start()
    pool_grads = blocks(across_tokens(pool_in, pool_out))
    for slot, xi, ci, device in near:
        copy(factors.at[slot], factors.at[slot], fac_send.at[0], fac_recv.at[slot], device).wait_recv()
    factors_z[z] = sum(factors[i] for i in range(1, 8)) + factors[0]
    second = [copy(factors_z.at[z], factors_z.at[z], facz_send.at[i], facz_recv.at[z], a[1]) for i, a in enumerate(across)]
    for item in second:
        item.start()
    for slot, xi, ci, device in near:
        copy(vals.at[xi, z, ci], vals.at[xi, z, ci], val_send.at[0], val_recv.at[slot], device).wait_recv()
    third = [copy(vals.at[:, z], vals.at[:, z], valz_send.at[i], valz_recv.at[z], a[1]) for i, a in enumerate(across)]
    for item in third:
        item.start()
    for zi, device in across:
        copy(factors_z.at[zi], factors_z.at[zi], facz_send.at[0], facz_recv.at[zi], device).wait_recv()
    total = factors_z[0] + factors_z[1] + factors_z[2] + factors_z[3]
    inverse = damped_inverses(total[0:RANK] / total[RANK:RANK + 1])
    inv_in = inverse[:, 0:RANK]
    turned = pltpu.roll(inverse, RANK, 1)
    twice = jnp.where(lower, turned, inverse)
    inv_out = jnp.concatenate([jnp.where(lower, twice, 0.0), jnp.where(lower, 0.0, twice)], 0)
    scaled = jnp.dot(inv_in, pool_grads, precision=highest, preferred_element_type=f32)
    scaled = jnp.dot(scaled, inv_out, precision=highest, preferred_element_type=f32)
    coarse = scaled.astype(bf16)
    fine = (scaled - coarse.astype(f32)).astype(bf16)
    empty = jnp.zeros(wide, bf16)

    def spread(value):
        return jnp.concatenate(
            [jnp.concatenate([value, empty], 1), jnp.concatenate([empty, value], 1)], 0
        )

    coarse, fine = spread(coarse), spread(fine)
    for zi, device in across:
        copy(vals.at[:, zi], vals.at[:, zi], valz_send.at[0], valz_recv.at[zi], device).wait_recv()
    every = vals[...].reshape(32 * RANK, 2 * RANK)
    product = jnp.dot(every, coarse, preferred_element_type=f32) + jnp.dot(every, fine, preferred_element_type=f32)
    at_row = lax.broadcasted_iota(jnp.int32, product.shape, 0) % RANK
    at_lane = lax.broadcasted_iota(jnp.int32, product.shape, 1) % RANK
    summed = jnp.where(at_row == at_lane, product, 0.0).reshape(32, RANK, 4 * RANK).sum(1)
    group = lax.broadcasted_iota(jnp.int32, (8, 4 * RANK), 1) // RANK
    picks = (lax.broadcasted_iota(jnp.int32, (8, 4 * RANK), 0) == group).astype(f32)
    part = lax.dot_general(picks, summed, (((1,), (1,)), ((), ())), precision=highest, preferred_element_type=f32)
    layers[layer] = jnp.concatenate([part, jnp.zeros((8, 96), f32)], 1)
    last = [copy(layers.at[layer], layers.at[layer], lay_send.at[i], lay_recv.at[layer], q[1]) for i, q in enumerate(planes)]
    for item in last:
        item.start()
    for plane, device in planes:
        copy(layers.at[plane], layers.at[plane], lay_send.at[0], lay_recv.at[plane], device).wait_recv()
    scores_out[...] = (layers[0] + layers[1] + layers[2] + layers[3]) * (1.0 / (RANK * TOKENS))

    for item in first + second + third + last:
        item.wait_send()
    for kind in (2, 1):
        @pl.when(layer == kind)
        def _():
            for item in lows(kind):
                item.wait_send()


def score(top_low, mid_low, in_low, counts):
    inside = pl.BlockSpec(memory_space=pltpu.VMEM)
    dma = pltpu.SemaphoreType.DMA
    return pl.pallas_call(
        score_kernel,
        out_shape=jax.ShapeDtypeStruct((8, 128), jnp.float32),
        in_specs=[inside] * 4,
        out_specs=inside,
        scratch_shapes=[
            pltpu.VMEM((3, TOKENS, 2 * RANK), jnp.bfloat16),
            pltpu.VMEM((8, RANK + 8, 2 * RANK), jnp.float32),
            pltpu.VMEM((4, RANK + 8, 2 * RANK), jnp.float32),
            pltpu.VMEM((4, 4, 2, RANK, 2 * RANK), jnp.bfloat16),
            pltpu.VMEM((4, 8, 128), jnp.float32),
            dma((12,)), dma((3,)), dma((7,)), dma((8,)), dma((7,)), dma((8,)),
            dma((3,)), dma((4,)), dma((3,)), dma((4,)), dma((3,)), dma((4,)),
        ],
        compiler_params=pltpu.CompilerParams(
            collective_id=1, has_side_effects=True, vmem_limit_bytes=32 * 1024 * 1024
        ),
        name="score",
    )(top_low, mid_low, in_low, counts)


def sent(value, pairs):
    return lax.ppermute(value, "layer", pairs)


def on_device(
    pool_inputs, val_inputs, pool_top, val_top, weight, proj_in, proj_out, pool_len, val_len
):
    rank = proj_in.shape[2]
    layer = lax.axis_index("layer")
    f32 = jnp.float32

    projections = lax.all_gather(proj_out[0], "layer", axis=0)
    grad2, grad1, gated1 = chain(pool_inputs[0], val_inputs[0], pool_top, val_top, weight[0])
    folded = jnp.dot(weight[0], projections[0], preferred_element_type=f32).astype(jnp.bfloat16)
    folded = lax.all_gather(folded, "trace", axis=0, tiled=True)
    folded = jnp.where(layer == 2, sent(folded, [(1, 2)]), folded)

    flat_top = jnp.concatenate([pool_top, val_top], 0).reshape(-1, WIDTH)
    low_top = jnp.dot(flat_top, proj_out[0], preferred_element_type=f32)
    flat_inputs = jnp.concatenate([pool_inputs[0], val_inputs[0]], 0).reshape(-1, WIDTH)
    low_in = jnp.dot(flat_inputs, proj_in[0], preferred_element_type=f32)

    low2 = sum(
        jnp.dot(grad2[n], lax.dynamic_slice_in_dim(projections[2], n * COLS, COLS, 0), preferred_element_type=f32)
        for n in range(CHUNKS)
    )
    low1 = jnp.dot(grad1, projections[1], preferred_element_type=f32)
    low0 = jnp.dot(grad1, projections[0], preferred_element_type=f32) + jnp.dot(
        gated1, folded, preferred_element_type=f32
    )
    positions = jnp.arange(TOKENS, dtype=jnp.int32)
    lengths = jnp.concatenate([pool_len, val_len], 0)
    valid = (positions[None, :] < lengths[:, None])[:, :, None]

    def packed(low):
        low = jnp.where(valid, low.reshape(4, TOKENS, rank), 0.0)
        return jnp.stack([jnp.concatenate([low[0], low[1]], 1), jnp.concatenate([low[2], low[3]], 1)])

    def spread(low):
        main = jnp.where(layer == 2, low, 0.0)
        return packed(jnp.concatenate([main, jnp.where(layer == 1, low[:REST], 0.0)], 0))

    mid_low = jnp.stack([spread(low0), spread(low1), spread(low2)]).astype(jnp.bfloat16)
    counts = jnp.full((8, 2 * rank), jnp.sum(pool_len).astype(f32))
    summed = score(packed(low_top).astype(jnp.bfloat16), mid_low, packed(low_in), counts)
    table = summed[:4, :32].reshape(2, 2, 32).transpose(1, 2, 0).reshape(2, 64)
    return lax.dynamic_slice_in_dim(table, layer * 16, 16, 1)


def solution(mesh):
    placed = (
        P("layer", "trace", None, None),
        P("layer", "trace", None, None),
        P("trace", None, None),
        P("trace", None, None),
        P("layer", "trace", None),
        P("layer", None, None),
        P("layer", None, None),
        P("trace"),
        P("trace"),
    )
    return jax.shard_map(
        on_device, mesh=mesh, in_specs=placed, out_specs=P("trace", "layer"), check_vma=False
    )
```

```python
import functools

import jax
import jax.numpy as jnp
from jax import lax
from jax.experimental import pallas as pl
from jax.experimental.pallas import tpu as pltpu
from jax.sharding import PartitionSpec as P

MESH = pl.DeviceIdType.MESH
WIDTH = 4096
TOKENS = 128
RANK = 64
CHUNKS = 16
COLS = WIDTH // CHUNKS
PAIRS = CHUNKS // 2
SHARE = 128
MAIN = 384
REST = 128
LAG_FORWARD, LAG_ROW, LAG_ROW_FORWARD, LAG_LAST, LAG_USE = 1, 2, 3, 4, 5
LAG_GRAD = 6
SLICE = 32
Q_LAG = 6


def silu_slope(values):
    logistic = jax.nn.sigmoid(values)
    return logistic * (1.0 + values * (1.0 - logistic))


def low_half(shape):
    return lax.broadcasted_iota(jnp.int32, shape, len(shape) - 1) < RANK


def damped_inverses(pair):
    rows = lax.broadcasted_iota(jnp.int32, pair.shape, 0)
    lanes = lax.broadcasted_iota(jnp.int32, pair.shape, 1)
    lower = lanes < RANK
    column = jnp.where(lower, lanes, lanes - RANK)
    diagonal = rows == column
    on_diagonal = jnp.where(diagonal, pair, 0.0)
    trace_first = jnp.sum(jnp.where(lower, on_diagonal, 0.0), keepdims=True)
    trace_second = jnp.sum(jnp.where(lower, 0.0, on_diagonal), keepdims=True)
    damping = jnp.where(lower, trace_first, trace_second) * (0.1 / RANK)
    value = jnp.where(diagonal, pair + damping, pair)
    for k in range(RANK):
        left = jnp.where(
            lower,
            jnp.broadcast_to(value[:, k:k + 1], pair.shape),
            jnp.broadcast_to(value[:, RANK + k:RANK + k + 1], pair.shape),
        )
        pivot = 1.0 / left[k:k + 1]
        row = jnp.where(column[k:k + 1] == k, pivot, value[k:k + 1] * pivot)
        left = jnp.where(rows == k, -1.0, left)
        value = jnp.where((rows == k) | (column == k), 0.0, value) - left * row
    return value


def whole_kernel(
    pool_in, val_in, pool_top, val_top, weight, proj_in, proj_out, valid, counts,
    scores_out,
    held, first, second, gated, grad, total, block, raw, wide_in, wide_out, folded,
    low_mid, low_two, low_in, outgoing,
    landed, factors, factors_z, vals, layers,
    send, recv, grad_send, grad_recv, act_send, act_recv, local, fold_send, fold_recv, proj_send, proj_recv,
    low_send, low_recv, fac_send, fac_recv, val_send, val_recv, facz_send, facz_recv, valz_send, valz_recv,
    lay_send, lay_recv,
):
    layer = lax.axis_index("layer")
    trace = lax.axis_index("trace")
    x, z, c = trace // 8, (trace // 2) % 4, trace % 2
    xp, xm, xo = (x + 1) % 4, (x + 3) % 4, (x + 2) % 4
    zp, zm, zo = (z + 1) % 4, (z + 3) % 4, (z + 2) % 4
    other = 1 - c
    highest = lax.Precision.HIGHEST
    f32, bf16 = jnp.float32, jnp.bfloat16

    def at(xi, zi, ci):
        return {"trace": xi * 8 + zi * 2 + ci}

    above = {"layer": (layer + 1) % 4}
    below = {"layer": (layer + 3) % 4}
    sibling = at(x, z, other)

    near = []
    for dx in range(4):
        for dc in range(2):
            if dx or dc:
                xi, ci = (x + dx) % 4, (c + dc) % 2
                near.append((xi * 2 + ci, xi, ci, at(xi, z, ci)))
    across = [((z + dz) % 4, at(x, (z + dz) % 4, c)) for dz in (1, 3, 2)]
    planes = [((layer + dl) % 4, {"layer": (layer + dl) % 4}) for dl in (1, 3, 2)]
    barrier = pltpu.get_barrier_semaphore()
    for device in [n[3] for n in near] + [a[1] for a in across] + [q[1] for q in planes]:
        pl.semaphore_signal(barrier, inc=1, device_id=device, device_id_type=MESH)
    pl.semaphore_wait(barrier, len(near) + len(across) + len(planes))

    def copy(src, dst, send_sem, recv_sem, device):
        return pltpu.make_async_remote_copy(
            src_ref=src, dst_ref=dst, send_sem=send_sem, recv_sem=recv_sem, device_id=device, device_id_type=MESH
        )

    def columns(j):
        return pl.ds(pl.multiple_of(j * COLS, COLS), COLS)

    def transposed(left, right):
        return lax.dot_general(left, right, (((1,), (1,)), ((), ())), preferred_element_type=f32)

    def on(kind):
        return pl.when(layer == kind)

    def own(j):
        return held.at[j, x, z, c]

    def share_out(j, device):
        return copy(weight.at[:, columns(j)], own(j), send.at[j, 12], recv.at[j, 12], device)

    def share_local(j):
        return pltpu.make_async_copy(weight.at[:, columns(j)], own(j), local.at[j])

    def load(src, dst, index):
        return pltpu.make_async_copy(src, dst, local.at[CHUNKS + index])

    def row_loads(pool, val, target, base):
        return [
            load(pool.at[0], target.at[0:128], base), load(pool.at[1], target.at[128:256], base + 1),
            load(val.at[0], target.at[256:384], base + 2),
        ]

    def loads(kind):
        return {
            3: lambda: row_loads(pool_in, val_in, first, 0) + row_loads(pool_top, val_top, second, 3),
            2: lambda: row_loads(pool_in, val_in, first, 0),
            1: lambda: [load(val_in.at[1], second.at[0:128], 0)],
            0: lambda: [load(val_top.at[1], second.at[0:128], 0)],
        }[kind]()

    def rows_of(base, i):
        return pl.ds(pl.multiple_of(base + i * SLICE, SLICE), SLICE)

    def rest_slice(i, device):
        return copy(
            val_in.at[1, rows_of(0, i)], first.at[rows_of(0, i)], act_send.at[i], act_recv.at[i], device
        )

    def main_slice(i, source, base):
        return copy(
            source.at[rows_of(0, i)], second.at[rows_of(base, i)],
            act_send.at[base // SLICE + i], act_recv.at[base // SLICE + i], above,
        )

    main_sources = ((pool_in.at[0], 0), (pool_in.at[1], 128), (val_in.at[0], 256))

    def gather_stages(j, view, flip, sems, part):
        send_j, recv_j = sems
        ahead, behind, far = (zp, zm, zo) if flip else (xp, xm, xo)
        up, down, beyond = (xp, xm, xo) if flip else (zp, zm, zo)
        lo, mid, hi = part

        def spot(along, over, ci, rows):
            return view(over, along, ci, *rows) if flip else view(along, over, ci, *rows)

        me_along, me_over = (z, x) if flip else (x, z)

        def to_along(i):
            return at(x, i, c) if flip else at(i, z, c)

        def to_over(i):
            return at(i, z, c) if flip else at(x, i, c)

        full = (lo, hi)
        every = slice(0, 4)

        def push(ref, slot, device):
            copy(ref, ref, send_j(j, slot), recv_j(j, slot), device).start()

        def arrived(ref, slot):
            copy(ref, ref, send_j(j, slot), recv_j(j, slot), sibling).wait_recv()

        def share():
            ref = spot(me_along, me_over, c, full)
            push(ref, 0, to_along(ahead))
            push(ref, 1, to_along(behind))

        def forward():
            arrived(spot(behind, me_over, c, full), 0)
            push(spot(behind, me_over, c, (lo, mid)), 2, to_along(ahead))
            arrived(spot(ahead, me_over, c, full), 1)
            push(spot(ahead, me_over, c, (mid, hi)), 3, to_along(behind))

        def row():
            arrived(spot(far, me_over, c, (lo, mid)), 2)
            arrived(spot(far, me_over, c, (mid, hi)), 3)
            ref = spot(every, me_over, c, full)
            push(ref, 4, to_over(up))
            push(ref, 5, to_over(down))
            push(ref, 8, sibling)

        def row_forward():
            arrived(spot(every, down, c, full), 4)
            push(spot(slice(0, 2), down, c, full), 6, to_over(up))
            arrived(spot(every, up, c, full), 5)
            push(spot(slice(2, 4), up, c, full), 7, to_over(down))
            push(spot(every, down, c, full), 9, sibling)
            push(spot(every, up, c, full), 10, sibling)

        def last():
            arrived(spot(slice(0, 2), beyond, c, full), 6)
            arrived(spot(slice(2, 4), beyond, c, full), 7)
            push(spot(every, beyond, c, full), 11, sibling)

        def whole():
            for slot, over in ((8, me_over), (9, down), (10, up), (11, beyond)):
                arrived(spot(every, over, other, full), slot)

        def drain():
            def left(ref, slot):
                copy(ref, ref, send_j(j, slot), recv_j(j, slot), sibling).wait_send()

            for slot in (0, 1):
                left(spot(me_along, me_over, c, full), slot)
            left(spot(me_along, me_over, c, (lo, mid)), 2)
            left(spot(me_along, me_over, c, (mid, hi)), 3)
            for slot in (4, 5, 8, 9, 10, 11):
                left(spot(every, me_over, c, full), slot)
            left(spot(slice(0, 2), me_over, c, full), 6)
            left(spot(slice(2, 4), me_over, c, full), 7)

        return share, forward, row, row_forward, last, whole, drain

    def weight_view(j):
        return lambda xi, zi, ci, lo, hi: held.at[j, xi, zi, ci, lo:hi]

    weight_sems = (lambda j, slot: send.at[j, slot], lambda j, slot: recv.at[j, slot])
    fold_sems = (lambda j, slot: fold_send.at[slot], lambda j, slot: fold_recv.at[slot])

    def weight_stages(p):
        a, b = 2 * p, 2 * p + 1
        part = (0, SHARE // 2, SHARE)
        return zip(
            gather_stages(a, weight_view(a), False, weight_sems, part),
            gather_stages(b, weight_view(b), True, weight_sems, part),
        )

    def run_stage(index):
        def stage(p):
            one, two = list(weight_stages(p))[index]
            one()
            two()
        return stage

    def fold_view(xi, zi, ci, lo, hi):
        return folded.at[xi, zi, ci, lo:hi]

    fold_stages = gather_stages(0, fold_view, False, fold_sems, (RANK, RANK + RANK // 2, 2 * RANK))

    def have_share(p):
        for j in (2 * p, 2 * p + 1):
            @pl.when(layer >= 2)
            def _():
                share_local(j).wait()

            @pl.when(layer < 2)
            def _():
                copy(own(j), own(j), send.at[j, 12], recv.at[j, 12], sibling).wait_recv()

    def half_of(which, index, low, ci):
        return which.at[index, low:low + RANK, pl.ds(pl.multiple_of(ci * (WIDTH // 2), WIDTH // 2), WIDTH // 2)]

    def proj_copy(index, low, slot, device):
        ref = half_of(wide_out, index, low, c)
        return copy(ref, ref, proj_send.at[slot], proj_recv.at[slot], device)

    def proj_out_copies(kind):
        if kind == 2:
            return [proj_copy(1, 0, 3, {"layer": 1})]
        if kind == 1:
            return [proj_copy(0, 0, 0, {"layer": 2})]
        if kind == 0:
            return [proj_copy(0, RANK, 1, {"layer": 1}), proj_copy(0, RANK, 2, {"layer": 2})]
        return []

    def proj_in_copies(kind):
        if kind == 2:
            return [proj_copy(0, 0, 0, above), proj_copy(0, RANK, 2, above)]
        if kind == 1:
            return [proj_copy(0, RANK, 1, above), proj_copy(1, 0, 3, above)]
        return []

    def proj_chip_copies(kind):
        if kind == 2:
            return [proj_copy(0, 0, 4, sibling), proj_copy(0, RANK, 5, sibling)]
        if kind == 1:
            return [proj_copy(0, RANK, 5, sibling), proj_copy(1, 0, 6, sibling)]
        return []

    def proj_chip_arrived(kind):
        for index, low, slot in {2: ((0, 0, 4), (0, RANK, 5)), 1: ((0, RANK, 5), (1, 0, 6))}[kind]:
            ref = half_of(wide_out, index, low, other)
            copy(ref, ref, proj_send.at[slot], proj_recv.at[slot], sibling).wait_recv()

    def turn(store):
        rows = lax.broadcasted_iota(jnp.int32, (2 * RANK, RANK), 0)
        lanes = lax.broadcasted_iota(jnp.int32, (2 * RANK, RANK), 1)
        unit = ((rows % RANK) == lanes).astype(bf16)

        def body(k, carry):
            piece = raw[pl.ds(pl.multiple_of(k * COLS, COLS), COLS), :]
            store(columns(k), transposed(unit, piece).astype(bf16))
            return carry
        lax.fori_loop(0, CHUNKS, body, 0)

    def load_raw(ref):
        return load(ref, raw, 6)

    def block_source(index):
        return (pool_in.at[0], pool_in.at[1], val_in.at[0], val_in.at[1],
                pool_top.at[0], pool_top.at[1], val_top.at[0], val_top.at[1])[index]

    def block_load(source):
        return load(source, block, 7)

    @pl.when(layer >= 2)
    def _():
        def body(j, carry):
            share_local(j).start()
            return carry
        lax.fori_loop(0, CHUNKS, body, 0)

    def share_pair(p):
        for kind, partner in ((3, above), (2, below)):
            @on(kind)
            def _():
                share_out(2 * p, partner).start()
                share_out(2 * p + 1, partner).start()

    share_pair(0)
    share_pair(1)
    load_raw(proj_out).start()
    for kind in range(4):
        @on(kind)
        def _():
            for item in loads(kind):
                item.start()
    block_load(block_source(0)).start()

    def gate_rows(index):
        base = pl.multiple_of(index * 32, 32)
        value = first[pl.ds(base, 32), :].astype(f32)
        top = second[pl.ds(base, 32), :].astype(f32)
        gated[pl.ds(base, 32), :] = (top * silu_slope(value)).astype(bf16)

    def gate_some(start, count):
        def body(i, carry):
            gate_rows(start + i)
            return carry
        lax.fori_loop(0, count, body, 0)

    def grad_copy(j, rows, device):
        return copy(grad.at[j, 0:rows], grad.at[j, 0:rows], grad_send.at[j], grad_recv.at[j], device)

    def upper_chunk(j, rows, device):
        total[0, 0:rows] = second[0:rows, columns(j)].astype(f32)

        def body(xi, carry):
            piece = held[j, xi].reshape(WIDTH // 4, COLS)
            left = gated[0:rows, pl.ds(pl.multiple_of(xi * (WIDTH // 4), WIDTH // 4), WIDTH // 4)]
            total[0, 0:rows] += jnp.dot(left, piece, preferred_element_type=f32)
            return carry
        lax.fori_loop(0, 4, body, 0)
        grad[j, 0:rows] = total[0, 0:rows].astype(bf16)
        grad_copy(j, rows, device).start()

    def add_product(n, q, rows):
        piece = held[n, q // 2, pl.ds(2 * (q % 2), 2)].reshape(4 * SHARE, COLS)
        left = gated[0:rows, pl.ds(pl.multiple_of(q * 2 * COLS, 2 * COLS), 2 * COLS)]
        total[n, 0:rows] += jnp.dot(left, piece, preferred_element_type=f32)

    def lower_weight(n, ready, rows):
        total[n, 0:rows] = jnp.zeros((rows, COLS), f32)

        def body(q, carry):
            add_product(n, q, rows)
            return carry
        lax.fori_loop(0, ready, body, 0)

    def lower_gate(q, rows):
        for k in (2 * q, 2 * q + 1):
            grad_copy(k, rows, above).wait_recv()

            def gating(i, carry):
                base = pl.multiple_of(i * 64, 64)
                value = first[pl.ds(base, 64), columns(k)].astype(f32)
                up = grad[k, pl.ds(base, 64)].astype(f32)
                gated[pl.ds(base, 64), columns(k)] = (up * silu_slope(value)).astype(bf16)
                return carry
            lax.fori_loop(0, rows // 64, gating, 0)

    def lower_grad(q, ready, rows):
        lower_gate(q, rows)

        def body(n, carry):
            add_product(n, q, rows)
            return carry
        lax.fori_loop(0, ready, body, 0)

    def when_in(t, lag, what):
        @pl.when((t >= lag) & (t < PAIRS + lag))
        def _():
            what(t - lag)

    def early(t):
        @pl.when(t == 0)
        def _():
            load_raw(proj_out).wait()

            def keep_out(cols, value):
                @pl.when(layer >= 2)
                def _():
                    wide_out[1, :, cols] = value

                @on(1)
                def _():
                    wide_out[0, 0:RANK, cols] = value[0:RANK]

                @on(0)
                def _():
                    wide_out[0, RANK:2 * RANK, cols] = value[0:RANK]
            turn(keep_out)
            for kind in (2, 1, 0):
                @on(kind)
                def _():
                    for item in proj_out_copies(kind):
                        item.start()
            load_raw(proj_in).start()
            folded[:, :, :, 0:RANK] = jnp.zeros((4, 4, 2, RANK, 2 * RANK), bf16)

        @pl.when(t == 1)
        def _():
            load_raw(proj_in).wait()

            def keep_in(cols, value):
                wide_in[:, cols] = value
            turn(keep_in)
            for kind in range(4):
                @on(kind)
                def _():
                    for item in loads(kind):
                        item.wait()

        for index in range(4):
            @pl.when(t == 1 + index)
            def _():
                block_load(block_source(index)).wait()
                low_in[index] = transposed(block[...], wide_in[...])
                if index < 3:
                    block_load(block_source(index + 1)).start()
                else:
                    @on(3)
                    def _():
                        block_load(block_source(4)).start()

                    @on(1)
                    def _():
                        block_load(weight).start()
        for index in range(4, 8):
            @pl.when((t == 1 + index) & (layer == 3))
            def _():
                block_load(block_source(index)).wait()
                low_mid[pl.ds((index - 4) * TOKENS, TOKENS)] = transposed(block[...], wide_out[1])
                if index < 7:
                    block_load(block_source(index + 1)).start()

        @pl.when((t >= 1) & (t < 5) & (layer == 3))
        def _():
            gate_some(3 * (t - 1), 3)

        for kind in (2, 1):
            @pl.when((t == 3) & (layer == kind))
            def _():
                for item in proj_in_copies(kind):
                    item.wait_recv()
                for item in proj_chip_copies(kind):
                    item.start()

            @pl.when((t == 4) & (layer == kind))
            def _():
                proj_chip_arrived(kind)
                if kind == 1:
                    wide_out[1, RANK:2 * RANK] = wide_out[1, 0:RANK]

        @pl.when((t == 5) & (layer == 1))
        def _():
            block_load(weight).wait()
            folded[x, z, c, RANK:2 * RANK] = transposed(wide_out[0, RANK:2 * RANK], block[...]).astype(bf16)
            mine = folded.at[x, z, c, RANK:2 * RANK]
            copy(mine, mine, fold_send.at[12], fold_recv.at[12], above).start()

        for index, stage in enumerate(fold_stages[:6]):
            @pl.when((t == Q_LAG + index) & ((layer == 1) | (layer == 2)))
            def _():
                if index == 0:
                    @on(2)
                    def _():
                        mine = folded.at[x, z, c, RANK:2 * RANK]
                        copy(mine, mine, fold_send.at[12], fold_recv.at[12], above).wait_recv()
                stage()

    def step(t, carry):
        @pl.when(t + 2 < PAIRS)
        def _():
            share_pair(t + 2)
        for kind, partner in ((3, above), (2, below)):
            @pl.when((t < 4) & (layer == kind))
            def _():
                rest_slice(t, partner).start()

        @pl.when((t < 4) & (layer == 1))
        def _():
            for source, base in main_sources:
                main_slice(t, source, base).start()

        when_in(t, 0, have_share)
        for lag, index in ((0, 0), (LAG_FORWARD, 1), (LAG_ROW, 2), (LAG_ROW_FORWARD, 3), (LAG_LAST, 4)):
            when_in(t, lag, run_stage(index))
        early(t)
        when_in(t, LAG_USE, run_stage(5))

        @pl.when((t == LAG_USE) & (layer < 2))
        def _():
            for i in range(4):
                rest_slice(i, above).wait_recv()

            @on(0)
            def _():
                gate_some(0, REST // 32)

        for kind, rows, target in ((3, MAIN, below), (0, REST, above)):
            @pl.when((layer == kind) & (t >= LAG_USE) & (t < PAIRS + LAG_USE))
            def _():
                upper_chunk(2 * (t - LAG_USE), rows, target)
                upper_chunk(2 * (t - LAG_USE) + 1, rows, target)

        whole = jnp.minimum(2 * (t - LAG_USE) + 2, CHUNKS)
        for kind, rows in ((2, MAIN), (1, REST)):
            @pl.when((layer == kind) & (t >= LAG_USE) & (t < PAIRS + LAG_USE))
            def _():
                ready = jnp.maximum(t - LAG_GRAD, 0)
                lower_weight(2 * (t - LAG_USE), ready, rows)
                lower_weight(2 * (t - LAG_USE) + 1, ready, rows)

            @pl.when((layer == kind) & (t >= LAG_GRAD) & (t < PAIRS + LAG_GRAD - 1))
            def _():
                lower_grad(t - LAG_GRAD, whole, rows)
        return carry

    lax.fori_loop(0, PAIRS + LAG_GRAD - 1, step, 0)

    def finish(kind, rows):
        if kind == 2:
            for i in range(4):
                for source, base in main_sources:
                    main_slice(i, source, base).wait_recv()
        lower_gate(PAIRS - 1, rows)
        low_mid[0:rows] = jnp.zeros((rows, 2 * RANK), f32)
        low_two[0:rows] = jnp.zeros((rows, 2 * RANK), f32)

        def body(n, carry):
            add_product(n, PAIRS - 1, rows)
            low_two[0:rows] += transposed(grad[n, 0:rows], wide_out[1, :, columns(n)])

            def inner(i, inner_carry):
                base = pl.multiple_of(i * 64, 64)
                up = grad[n, pl.ds(base, 64)].astype(f32)
                value = second[pl.ds(base, 64), columns(n)].astype(f32)
                low = (up + total[n, pl.ds(base, 64)]).astype(bf16)
                first[pl.ds(base, 64), columns(n)] = low
                grad[n, pl.ds(base, 64)] = (low.astype(f32) * silu_slope(value)).astype(bf16)
                return inner_carry
            lax.fori_loop(0, rows // 64, inner, 0)
            fold = folded[n // 4, n % 4]
            low_mid[0:rows] += (
                transposed(first[0:rows, columns(n)], wide_out[0, :, columns(n)])
                + transposed(grad[n, 0:rows, 0:SHARE], fold[0])
                + transposed(grad[n, 0:rows, SHARE:COLS], fold[1])
            )
            return carry
        lax.fori_loop(0, CHUNKS, body, 0)

    wide = (RANK, 2 * RANK)
    lower = low_half(wide)
    lower_rows = low_half((TOKENS, 2 * RANK))

    def swap(value):
        return pltpu.roll(value, RANK, 1)

    def put(index, slot, value, mask):
        outgoing[index, slot] = (value * valid[mask]).astype(bf16)

    @on(3)
    def _():
        rows = [low_mid[i * TOKENS:(i + 1) * TOKENS] for i in range(4)]
        landed[0] = (jnp.where(lower_rows, rows[0], rows[1]) * valid[0]).astype(bf16)
        landed[1] = (jnp.where(lower_rows, rows[2], rows[3]) * valid[1]).astype(bf16)
        landed[2] = jnp.zeros_like(landed[2])

    @on(2)
    def _():
        finish(2, MAIN)
        mid = [low_mid[i * TOKENS:(i + 1) * TOKENS] for i in range(3)]
        two = [low_two[i * TOKENS:(i + 1) * TOKENS] for i in range(3)]
        put(1, 0, jnp.where(lower_rows, mid[0], swap(mid[1])), 0)
        put(1, 1, jnp.where(lower_rows, mid[2], 0.0), 1)
        put(0, 0, jnp.where(lower_rows, swap(mid[0]), mid[1]), 0)
        put(0, 1, jnp.where(lower_rows, swap(mid[2]), 0.0), 1)
        landed[0] = (jnp.where(lower_rows, two[0], two[1]) * valid[0]).astype(bf16)
        landed[1] = (jnp.where(lower_rows, two[2], 0.0) * valid[1]).astype(bf16)

    @on(1)
    def _():
        finish(1, REST)
        mid, two = low_mid[0:TOKENS], low_two[0:TOKENS]
        put(0, 1, jnp.where(lower_rows, 0.0, mid), 1)
        put(2, 1, jnp.where(lower_rows, 0.0, two), 1)
        landed[2] = (jnp.where(lower_rows, 0.0, swap(mid)) * valid[1]).astype(bf16)

    def low(source, slot, plane):
        return copy(source, landed.at[slot], low_send.at[slot + 3 * plane], low_recv.at[slot], {"layer": plane})

    def lows(kind):
        if kind == 2:
            return [low(outgoing.at[1, 0], 0, 1), low(outgoing.at[1, 1], 1, 1),
                    low(outgoing.at[0, 0], 0, 0), low(outgoing.at[0, 1], 1, 0)]
        if kind == 1:
            return [low(outgoing.at[0, 1], 2, 0), low(outgoing.at[2, 1], 2, 2)]
        return []

    def lows_in(kind):
        return [low(landed.at[slot], slot, (kind + 1) % 4) for slot in {3: (), 2: (2,), 1: (0, 1), 0: (0, 1, 2)}[kind]]

    for kind in (2, 1):
        @pl.when(layer == kind)
        def _():
            for item in lows(kind):
                item.start()

    for kind in (2, 1, 0):
        @pl.when(layer == kind)
        def _():
            for item in lows_in(kind):
                item.wait_recv()

    def across_tokens(left, right):
        return lax.dot_general(left, right, (((0,), (0,)), ((), ())), precision=highest, preferred_element_type=f32)

    def blocks(value):
        return jnp.where(lower, value[0:RANK], value[RANK:2 * RANK])

    def both(value):
        return value + swap(value)

    pool_low = jnp.where(lower_rows, low_in[0], low_in[1]) * valid[0]
    val_low = jnp.where(lower_rows, low_in[2], low_in[3]) * valid[1]
    pool_out = landed[0].astype(f32)
    val_out = landed[1].astype(f32) + landed[2].astype(f32)
    vals[x, z, c] = blocks(across_tokens(val_out, val_low)).astype(bf16)
    part_in = both(blocks(across_tokens(pool_low, pool_low)))
    part_out = both(blocks(across_tokens(pool_out, pool_out)))
    factors[x * 2 + c, 0:RANK] = jnp.where(lower, part_in, part_out)
    factors[x * 2 + c, RANK:RANK + 8] = counts[...]

    mine = x * 2 + c
    sent_one = [copy(factors.at[mine], factors.at[mine], fac_send.at[i], fac_recv.at[mine], n[3]) for i, n in enumerate(near)]
    sent_one += [copy(vals.at[x, z, c], vals.at[x, z, c], val_send.at[i], val_recv.at[mine], n[3]) for i, n in enumerate(near)]
    for item in sent_one:
        item.start()
    pool_grads = blocks(across_tokens(pool_low, pool_out))
    for slot, xi, ci, device in near:
        copy(factors.at[slot], factors.at[slot], fac_send.at[0], fac_recv.at[slot], device).wait_recv()
    factors_z[z] = sum(factors[i] for i in range(1, 8)) + factors[0]
    sent_two = [copy(factors_z.at[z], factors_z.at[z], facz_send.at[i], facz_recv.at[z], a[1]) for i, a in enumerate(across)]
    for item in sent_two:
        item.start()
    for slot, xi, ci, device in near:
        copy(vals.at[xi, z, ci], vals.at[xi, z, ci], val_send.at[0], val_recv.at[slot], device).wait_recv()
    sent_three = [copy(vals.at[:, z], vals.at[:, z], valz_send.at[i], valz_recv.at[z], a[1]) for i, a in enumerate(across)]
    for item in sent_three:
        item.start()
    for zi, device in across:
        copy(factors_z.at[zi], factors_z.at[zi], facz_send.at[0], facz_recv.at[zi], device).wait_recv()
    factor_sum = factors_z[0] + factors_z[1] + factors_z[2] + factors_z[3]
    inverse = damped_inverses(factor_sum[0:RANK] / factor_sum[RANK:RANK + 1])
    inv_in = inverse[:, 0:RANK]
    turned = swap(inverse)
    twice = jnp.where(lower, turned, inverse)
    inv_out = jnp.concatenate([jnp.where(lower, twice, 0.0), jnp.where(lower, 0.0, twice)], 0)
    scaled = jnp.dot(inv_in, pool_grads, precision=highest, preferred_element_type=f32)
    scaled = jnp.dot(scaled, inv_out, precision=highest, preferred_element_type=f32)
    coarse = scaled.astype(bf16)
    fine = (scaled - coarse.astype(f32)).astype(bf16)
    empty = jnp.zeros(wide, bf16)

    def spread(value):
        return jnp.concatenate(
            [jnp.concatenate([value, empty], 1), jnp.concatenate([empty, value], 1)], 0
        )

    coarse, fine = spread(coarse), spread(fine)
    for zi, device in across:
        copy(vals.at[:, zi], vals.at[:, zi], valz_send.at[0], valz_recv.at[zi], device).wait_recv()
    every = vals[...].reshape(32 * RANK, 2 * RANK)
    product = jnp.dot(every, coarse, preferred_element_type=f32) + jnp.dot(every, fine, preferred_element_type=f32)
    at_row = lax.broadcasted_iota(jnp.int32, product.shape, 0) % RANK
    at_lane = lax.broadcasted_iota(jnp.int32, product.shape, 1) % RANK
    summed = jnp.where(at_row == at_lane, product, 0.0).reshape(32, RANK, 4 * RANK).sum(1)
    group = lax.broadcasted_iota(jnp.int32, (8, 4 * RANK), 1) // RANK
    picks = (lax.broadcasted_iota(jnp.int32, (8, 4 * RANK), 0) == group).astype(f32)
    part = lax.dot_general(picks, summed, (((1,), (1,)), ((), ())), precision=highest, preferred_element_type=f32)
    layers[layer] = jnp.concatenate([part, jnp.zeros((8, 96), f32)], 1)
    sent_last = [copy(layers.at[layer], layers.at[layer], lay_send.at[i], lay_recv.at[layer], q[1]) for i, q in enumerate(planes)]
    for item in sent_last:
        item.start()
    for plane, device in planes:
        copy(layers.at[plane], layers.at[plane], lay_send.at[0], lay_recv.at[plane], device).wait_recv()
    scores_out[...] = (layers[0] + layers[1] + layers[2] + layers[3]) * (1.0 / (RANK * TOKENS))

    for item in sent_one + sent_two + sent_three + sent_last:
        item.wait_send()
    for kind in (2, 1):
        @pl.when(layer == kind)
        def _():
            for item in lows(kind):
                item.wait_send()

    def drain(p, carry):
        run_stage(6)(p)

        @pl.when(layer >= 2)
        def _():
            share_out(2 * p, above).wait_send()
            share_out(2 * p + 1, above).wait_send()
        for kind, rows in ((3, MAIN), (0, REST)):
            @on(kind)
            def _():
                grad_copy(2 * p, rows, above).wait_send()
                grad_copy(2 * p + 1, rows, above).wait_send()
        return carry
    lax.fori_loop(0, PAIRS, drain, 0)

    @pl.when(layer >= 2)
    def _():
        for i in range(4):
            rest_slice(i, above).wait_send()

    @on(1)
    def _():
        for i in range(4):
            for source, base in main_sources:
                main_slice(i, source, base).wait_send()
        mine = folded.at[x, z, c, RANK:2 * RANK]
        copy(mine, mine, fold_send.at[12], fold_recv.at[12], above).wait_send()

    @pl.when((layer == 1) | (layer == 2))
    def _():
        fold_stages[6]()
    for kind in (2, 1, 0):
        @on(kind)
        def _():
            for item in proj_out_copies(kind) + proj_chip_copies(kind):
                item.wait_send()


def whole(*operands):
    anywhere = pl.BlockSpec(memory_space=pl.ANY)
    inside = pl.BlockSpec(memory_space=pltpu.VMEM)
    dma = pltpu.SemaphoreType.DMA
    bf16, f32 = jnp.bfloat16, jnp.float32
    return pl.pallas_call(
        whole_kernel,
        out_shape=jax.ShapeDtypeStruct((8, 128), f32),
        in_specs=[anywhere] * 7 + [inside] * 2,
        out_specs=inside,
        scratch_shapes=[
            pltpu.VMEM((CHUNKS, 4, 4, 2, SHARE, COLS), bf16),
            pltpu.VMEM((MAIN, WIDTH), bf16),
            pltpu.VMEM((MAIN, WIDTH), bf16),
            pltpu.VMEM((MAIN, WIDTH), bf16),
            pltpu.VMEM((CHUNKS, MAIN, COLS), bf16),
            pltpu.VMEM((CHUNKS, MAIN, COLS), f32),
            pltpu.VMEM((TOKENS, WIDTH), bf16),
            pltpu.VMEM((WIDTH, RANK), bf16),
            pltpu.VMEM((2 * RANK, WIDTH), bf16),
            pltpu.VMEM((2, 2 * RANK, WIDTH), bf16),
            pltpu.VMEM((4, 4, 2, 2 * RANK, SHARE), bf16),
            pltpu.VMEM((4 * TOKENS, 2 * RANK), f32),
            pltpu.VMEM((MAIN, 2 * RANK), f32),
            pltpu.VMEM((4, TOKENS, 2 * RANK), f32),
            pltpu.VMEM((3, 2, TOKENS, 2 * RANK), bf16),
            pltpu.VMEM((3, TOKENS, 2 * RANK), bf16),
            pltpu.VMEM((8, RANK + 8, 2 * RANK), f32),
            pltpu.VMEM((4, RANK + 8, 2 * RANK), f32),
            pltpu.VMEM((4, 4, 2, RANK, 2 * RANK), bf16),
            pltpu.VMEM((4, 8, 128), f32),
            dma((CHUNKS, 13)), dma((CHUNKS, 13)), dma((CHUNKS,)), dma((CHUNKS,)), dma((12,)), dma((12,)),
            dma((CHUNKS + 8,)), dma((13,)), dma((13,)), dma((7,)), dma((7,)),
            dma((12,)), dma((3,)), dma((7,)), dma((8,)), dma((7,)), dma((8,)),
            dma((3,)), dma((4,)), dma((3,)), dma((4,)), dma((3,)), dma((4,)),
        ],
        compiler_params=pltpu.CompilerParams(
            collective_id=0, has_side_effects=True, vmem_limit_bytes=62 * 1024 * 1024
        ),
        name="whole",
    )(*operands)


def on_device(
    pool_inputs, val_inputs, pool_top, val_top, weight, proj_in, proj_out, pool_len, val_len
):
    layer = lax.axis_index("layer")
    positions = jnp.arange(TOKENS, dtype=jnp.int32)
    lengths = jnp.stack([pool_len, val_len])
    valid = (positions[None, :, None] < lengths[:, None, :]).astype(jnp.float32)
    valid = jnp.repeat(valid, RANK, axis=2)
    counts = jnp.full((8, 2 * RANK), jnp.sum(pool_len).astype(jnp.float32))
    summed = whole(
        pool_inputs[0], val_inputs[0], pool_top, val_top, weight[0], proj_in[0], proj_out[0], valid, counts
    )
    table = summed[:4, :32].reshape(2, 2, 32).transpose(1, 2, 0).reshape(2, 64)
    return lax.dynamic_slice_in_dim(table, layer * 16, 16, 1)


def solution(mesh):
    placed = (
        P("layer", "trace", None, None),
        P("layer", "trace", None, None),
        P("trace", None, None),
        P("trace", None, None),
        P("layer", "trace", None),
        P("layer", None, None),
        P("layer", None, None),
        P("trace"),
        P("trace"),
    )
    return jax.shard_map(
        on_device, mesh=mesh, in_specs=placed, out_specs=P("trace", "layer"), check_vma=False
    )
```

```python
import functools

import jax
import jax.numpy as jnp
from jax import lax
from jax.experimental import pallas as pl
from jax.experimental.pallas import tpu as pltpu
from jax.sharding import PartitionSpec as P

MESH = pl.DeviceIdType.MESH
WIDTH = 4096
TOKENS = 128
RANK = 64
CHUNKS = 16
COLS = WIDTH // CHUNKS
PAIRS = CHUNKS // 2
SHARE = 128
MAIN = 384
REST = 128
LAG_FORWARD, LAG_ROW, LAG_ROW_FORWARD, LAG_LAST, LAG_USE = 1, 2, 3, 4, 5
LAG_GRAD = 6
SLICE = 32
PART = 16
Q_LAG = 6


def silu_slope(values):
    logistic = jax.nn.sigmoid(values)
    return logistic * (1.0 + values * (1.0 - logistic))


def low_half(shape):
    return lax.broadcasted_iota(jnp.int32, shape, len(shape) - 1) < RANK


def damped_inverses(pair):
    rows = lax.broadcasted_iota(jnp.int32, pair.shape, 0)
    lanes = lax.broadcasted_iota(jnp.int32, pair.shape, 1)
    lower = lanes < RANK
    column = jnp.where(lower, lanes, lanes - RANK)
    diagonal = rows == column
    on_diagonal = jnp.where(diagonal, pair, 0.0)
    trace_first = jnp.sum(jnp.where(lower, on_diagonal, 0.0), keepdims=True)
    trace_second = jnp.sum(jnp.where(lower, 0.0, on_diagonal), keepdims=True)
    damping = jnp.where(lower, trace_first, trace_second) * (0.1 / RANK)
    value = jnp.where(diagonal, pair + damping, pair)
    for k in range(RANK):
        left = jnp.where(
            lower,
            jnp.broadcast_to(value[:, k:k + 1], pair.shape),
            jnp.broadcast_to(value[:, RANK + k:RANK + k + 1], pair.shape),
        )
        pivot = 1.0 / left[k:k + 1]
        row = jnp.where(column[k:k + 1] == k, pivot, value[k:k + 1] * pivot)
        left = jnp.where(rows == k, -1.0, left)
        value = jnp.where((rows == k) | (column == k), 0.0, value) - left * row
    return value


def whole_kernel(
    pool_in, val_in, pool_top, val_top, weight, proj_in, proj_out, pool_len, val_len,
    scores_out,
    held, first, second, gated, grad, total, block, wide_in, wide_out, folded,
    low_mid, low_two, low_in, outgoing,
    landed, factors, factors_z, vals, layers,
    send, recv, grad_send, grad_recv, act_send, act_recv, local, fold_send, fold_recv, proj_send, proj_recv,
    low_send, low_recv, fac_send, fac_recv, val_send, val_recv, facz_send, facz_recv, valz_send, valz_recv,
    lay_send, lay_recv,
):
    layer = lax.axis_index("layer")
    trace = lax.axis_index("trace")
    x, z, c = trace // 8, (trace // 2) % 4, trace % 2
    xp, xm, xo = (x + 1) % 4, (x + 3) % 4, (x + 2) % 4
    zp, zm, zo = (z + 1) % 4, (z + 3) % 4, (z + 2) % 4
    other = 1 - c
    highest = lax.Precision.HIGHEST
    f32, bf16 = jnp.float32, jnp.bfloat16

    def at(xi, zi, ci):
        return {"trace": xi * 8 + zi * 2 + ci}

    above = {"layer": (layer + 1) % 4}
    below = {"layer": (layer + 3) % 4}
    sibling = at(x, z, other)

    near = []
    for dx in range(4):
        for dc in range(2):
            if dx or dc:
                xi, ci = (x + dx) % 4, (c + dc) % 2
                near.append((xi * 2 + ci, xi, ci, at(xi, z, ci)))
    across = [((z + dz) % 4, at(x, (z + dz) % 4, c)) for dz in (1, 3, 2)]
    planes = [((layer + dl) % 4, {"layer": (layer + dl) % 4}) for dl in (1, 3, 2)]
    barrier = pltpu.get_barrier_semaphore()
    for device in [n[3] for n in near] + [a[1] for a in across] + [q[1] for q in planes]:
        pl.semaphore_signal(barrier, inc=1, device_id=device, device_id_type=MESH)
    pl.semaphore_wait(barrier, len(near) + len(across) + len(planes))

    def copy(src, dst, send_sem, recv_sem, device):
        return pltpu.make_async_remote_copy(
            src_ref=src, dst_ref=dst, send_sem=send_sem, recv_sem=recv_sem, device_id=device, device_id_type=MESH
        )

    def columns(j):
        return pl.ds(pl.multiple_of(j * COLS, COLS), COLS)

    def transposed(left, right):
        return lax.dot_general(left, right, (((1,), (1,)), ((), ())), preferred_element_type=f32)

    def on(kind):
        return pl.when(layer == kind)

    def own(j):
        return held.at[j, x, z, c]

    def share_out(j, device):
        return copy(weight.at[:, columns(j)], own(j), send.at[j, 12], recv.at[j, 12], device)

    def share_local(j):
        return pltpu.make_async_copy(weight.at[:, columns(j)], own(j), local.at[j])

    def load(src, dst, index):
        return pltpu.make_async_copy(src, dst, local.at[CHUNKS + index])

    def row_loads(pool, val, target, base):
        return [
            load(pool.at[0], target.at[0:128], base), load(pool.at[1], target.at[128:256], base + 1),
            load(val.at[0], target.at[256:384], base + 2),
        ]

    def loads(kind):
        return {
            3: lambda: row_loads(pool_in, val_in, first, 0) + row_loads(pool_top, val_top, second, 3),
            2: lambda: row_loads(pool_in, val_in, first, 0),
            1: lambda: [load(val_in.at[1], second.at[0:128], 0)],
            0: lambda: [load(val_top.at[1], second.at[0:128], 0)],
        }[kind]()

    def rows_of(base, i):
        return pl.ds(pl.multiple_of(base + i * SLICE, SLICE), SLICE)

    def rest_slice(i, device):
        return copy(
            val_in.at[1, rows_of(0, i)], first.at[rows_of(0, i)], act_send.at[i], act_recv.at[i], device
        )

    def main_slice(i, source, base):
        rows = pl.ds(pl.multiple_of(i * PART, PART), PART)
        there = pl.ds(pl.multiple_of(base + i * PART, PART), PART)
        index = base // PART + i
        return copy(source.at[rows], second.at[there], act_send.at[index], act_recv.at[index], above)

    main_sources = ((pool_in.at[0], 0), (pool_in.at[1], 128), (val_in.at[0], 256))

    def gather_stages(j, view, flip, sems, part):
        send_j, recv_j = sems
        ahead, behind, far = (zp, zm, zo) if flip else (xp, xm, xo)
        up, down, beyond = (xp, xm, xo) if flip else (zp, zm, zo)
        lo, mid, hi = part

        def spot(along, over, ci, rows):
            return view(over, along, ci, *rows) if flip else view(along, over, ci, *rows)

        me_along, me_over = (z, x) if flip else (x, z)

        def to_along(i):
            return at(x, i, c) if flip else at(i, z, c)

        def to_over(i):
            return at(i, z, c) if flip else at(x, i, c)

        full = (lo, hi)
        every = slice(0, 4)

        def push(ref, slot, device):
            copy(ref, ref, send_j(j, slot), recv_j(j, slot), device).start()

        def arrived(ref, slot):
            copy(ref, ref, send_j(j, slot), recv_j(j, slot), sibling).wait_recv()

        def share():
            ref = spot(me_along, me_over, c, full)
            push(ref, 0, to_along(ahead))
            push(ref, 1, to_along(behind))

        def forward():
            arrived(spot(behind, me_over, c, full), 0)
            push(spot(behind, me_over, c, (lo, mid)), 2, to_along(ahead))
            arrived(spot(ahead, me_over, c, full), 1)
            push(spot(ahead, me_over, c, (mid, hi)), 3, to_along(behind))

        def row():
            arrived(spot(far, me_over, c, (lo, mid)), 2)
            arrived(spot(far, me_over, c, (mid, hi)), 3)
            ref = spot(every, me_over, c, full)
            push(ref, 4, to_over(up))
            push(ref, 5, to_over(down))
            push(ref, 8, sibling)

        def row_forward():
            arrived(spot(every, down, c, full), 4)
            push(spot(slice(0, 2), down, c, full), 6, to_over(up))
            arrived(spot(every, up, c, full), 5)
            push(spot(slice(2, 4), up, c, full), 7, to_over(down))
            push(spot(every, down, c, full), 9, sibling)
            push(spot(every, up, c, full), 10, sibling)

        def last():
            arrived(spot(slice(0, 2), beyond, c, full), 6)
            arrived(spot(slice(2, 4), beyond, c, full), 7)
            push(spot(every, beyond, c, full), 11, sibling)

        def whole():
            for slot, over in ((8, me_over), (9, down), (10, up), (11, beyond)):
                arrived(spot(every, over, other, full), slot)

        def drain():
            def left(ref, slot):
                copy(ref, ref, send_j(j, slot), recv_j(j, slot), sibling).wait_send()

            for slot in (0, 1):
                left(spot(me_along, me_over, c, full), slot)
            left(spot(me_along, me_over, c, (lo, mid)), 2)
            left(spot(me_along, me_over, c, (mid, hi)), 3)
            for slot in (4, 5, 8, 9, 10, 11):
                left(spot(every, me_over, c, full), slot)
            left(spot(slice(0, 2), me_over, c, full), 6)
            left(spot(slice(2, 4), me_over, c, full), 7)

        return share, forward, row, row_forward, last, whole, drain

    def weight_view(j):
        return lambda xi, zi, ci, lo, hi: held.at[j, xi, zi, ci, lo:hi]

    weight_sems = (lambda j, slot: send.at[j, slot], lambda j, slot: recv.at[j, slot])
    fold_sems = (lambda j, slot: fold_send.at[slot], lambda j, slot: fold_recv.at[slot])

    def weight_stages(p):
        a, b = 2 * p, 2 * p + 1
        part = (0, SHARE // 2, SHARE)
        return zip(
            gather_stages(a, weight_view(a), False, weight_sems, part),
            gather_stages(b, weight_view(b), True, weight_sems, part),
        )

    def run_stage(index):
        def stage(p):
            one, two = list(weight_stages(p))[index]
            one()
            two()
        return stage

    def fold_view(xi, zi, ci, lo, hi):
        return folded.at[xi, zi, ci, lo:hi]

    fold_stages = gather_stages(0, fold_view, False, fold_sems, (RANK, RANK + RANK // 2, 2 * RANK))

    def have_share(p):
        for j in (2 * p, 2 * p + 1):
            @pl.when(layer >= 2)
            def _():
                share_local(j).wait()

            @pl.when(layer < 2)
            def _():
                copy(own(j), own(j), send.at[j, 12], recv.at[j, 12], sibling).wait_recv()

    def half_of(which, index, low, ci):
        return which.at[index, low:low + RANK, pl.ds(pl.multiple_of(ci * (WIDTH // 2), WIDTH // 2), WIDTH // 2)]

    def proj_copy(index, low, slot, device):
        ref = half_of(wide_out, index, low, c)
        return copy(ref, ref, proj_send.at[slot], proj_recv.at[slot], device)

    def proj_out_copies(kind):
        if kind == 2:
            return [proj_copy(1, 0, 3, {"layer": 1})]
        if kind == 1:
            return [proj_copy(0, 0, 0, {"layer": 2})]
        if kind == 0:
            return [proj_copy(0, RANK, 1, {"layer": 1}), proj_copy(0, RANK, 2, {"layer": 2})]
        return []

    def proj_in_copies(kind):
        if kind == 2:
            return [proj_copy(0, 0, 0, above), proj_copy(0, RANK, 2, above)]
        if kind == 1:
            return [proj_copy(0, RANK, 1, above), proj_copy(1, 0, 3, above)]
        return []

    def proj_chip_copies(kind):
        if kind == 2:
            return [proj_copy(0, 0, 4, sibling), proj_copy(0, RANK, 5, sibling)]
        if kind == 1:
            return [proj_copy(0, RANK, 5, sibling), proj_copy(1, 0, 6, sibling)]
        return []

    def proj_chip_arrived(kind):
        for index, low, slot in {2: ((0, 0, 4), (0, RANK, 5)), 1: ((0, RANK, 5), (1, 0, 6))}[kind]:
            ref = half_of(wide_out, index, low, other)
            copy(ref, ref, proj_send.at[slot], proj_recv.at[slot], sibling).wait_recv()

    def proj_loads(kind):
        places = {
            3: [(1, 0), (1, RANK)], 2: [(1, 0), (1, RANK)], 1: [(0, 0)], 0: [(0, RANK)],
        }[kind]
        return [
            load(proj_out, wide_out.at[index, low:low + RANK], 8 + i) for i, (index, low) in enumerate(places)
        ]

    def proj_in_loads():
        return [load(proj_in, wide_in.at[i * RANK:(i + 1) * RANK], 10 + i) for i in range(2)]

    def block_source(index):
        return (pool_in.at[0], pool_in.at[1], val_in.at[0], val_in.at[1],
                pool_top.at[0], pool_top.at[1], val_top.at[0], val_top.at[1])[index]

    def block_load(source):
        return load(source, block, 7)

    @pl.when(layer >= 2)
    def _():
        def body(j, carry):
            share_local(j).start()
            return carry
        lax.fori_loop(0, CHUNKS, body, 0)

    def share_pair(p):
        for kind, partner in ((3, above), (2, below)):
            @on(kind)
            def _():
                share_out(2 * p, partner).start()
                share_out(2 * p + 1, partner).start()

    share_pair(0)
    share_pair(1)
    for kind in range(4):
        @on(kind)
        def _():
            for item in proj_loads(kind) + loads(kind):
                item.start()
    for item in proj_in_loads():
        item.start()
    block_load(block_source(0)).start()

    def gate_rows(index):
        base = pl.multiple_of(index * 32, 32)
        value = first[pl.ds(base, 32), :].astype(f32)
        top = second[pl.ds(base, 32), :].astype(f32)
        gated[pl.ds(base, 32), :] = (top * silu_slope(value)).astype(bf16)

    def gate_some(start, count):
        def body(i, carry):
            gate_rows(start + i)
            return carry
        lax.fori_loop(0, count, body, 0)

    def grad_copy(j, rows, device):
        return copy(grad.at[j, 0:rows], grad.at[j, 0:rows], grad_send.at[j], grad_recv.at[j], device)

    def upper_chunk(j, rows, device):
        total[0, 0:rows] = second[0:rows, columns(j)].astype(f32)

        def body(xi, carry):
            piece = held[j, xi].reshape(WIDTH // 4, COLS)
            left = gated[0:rows, pl.ds(pl.multiple_of(xi * (WIDTH // 4), WIDTH // 4), WIDTH // 4)]
            total[0, 0:rows] += jnp.dot(left, piece, preferred_element_type=f32)
            return carry
        lax.fori_loop(0, 4, body, 0)
        grad[j, 0:rows] = total[0, 0:rows].astype(bf16)
        grad_copy(j, rows, device).start()

    def add_product(n, q, rows):
        piece = held[n, q // 2, pl.ds(2 * (q % 2), 2)].reshape(4 * SHARE, COLS)
        left = gated[0:rows, pl.ds(pl.multiple_of(q * 2 * COLS, 2 * COLS), 2 * COLS)]
        total[n, 0:rows] += jnp.dot(left, piece, preferred_element_type=f32)

    def lower_weight(n, ready, rows):
        total[n, 0:rows] = jnp.zeros((rows, COLS), f32)
        total[n + 1, 0:rows] = jnp.zeros((rows, COLS), f32)

        def body(q, carry):
            add_product(n, q, rows)
            add_product(n + 1, q, rows)
            return carry
        lax.fori_loop(0, ready, body, 0)

    def lower_gate(q, rows):
        for k in (2 * q, 2 * q + 1):
            grad_copy(k, rows, above).wait_recv()

            def gating(i, carry):
                base = pl.multiple_of(i * 64, 64)
                value = first[pl.ds(base, 64), columns(k)].astype(f32)
                up = grad[k, pl.ds(base, 64)].astype(f32)
                gated[pl.ds(base, 64), columns(k)] = (up * silu_slope(value)).astype(bf16)
                return carry
            lax.fori_loop(0, rows // 64, gating, 0)

    def lower_grad(q, ready, rows):
        lower_gate(q, rows)

        def body(n, carry):
            add_product(2 * n, q, rows)
            add_product(2 * n + 1, q, rows)
            return carry
        lax.fori_loop(0, ready // 2, body, 0)

    def when_in(t, lag, what):
        @pl.when((t >= lag) & (t < PAIRS + lag))
        def _():
            what(t - lag)

    def early(t):
        @pl.when(t == 0)
        def _():
            for kind in range(4):
                @on(kind)
                def _():
                    for item in proj_loads(kind):
                        item.wait()
                    for item in proj_out_copies(kind):
                        item.start()
            folded[:, :, :, 0:RANK] = jnp.zeros((4, 4, 2, RANK, 2 * RANK), bf16)

        @pl.when(t == 1)
        def _():
            for item in proj_in_loads():
                item.wait()
            for kind in range(4):
                @on(kind)
                def _():
                    for item in loads(kind):
                        item.wait()

        for index in range(4):
            @pl.when(t == 1 + index)
            def _():
                block_load(block_source(index)).wait()
                low_in[index] = transposed(block[...], wide_in[...])
                if index < 3:
                    block_load(block_source(index + 1)).start()
                else:
                    @on(3)
                    def _():
                        block_load(block_source(4)).start()

                    @on(1)
                    def _():
                        block_load(weight).start()
        for index in range(4, 8):
            @pl.when((t == 1 + index) & (layer == 3))
            def _():
                block_load(block_source(index)).wait()
                low_mid[pl.ds((index - 4) * TOKENS, TOKENS)] = transposed(block[...], wide_out[1])
                if index < 7:
                    block_load(block_source(index + 1)).start()

        @pl.when((t >= 1) & (t < 5) & (layer == 3))
        def _():
            gate_some(3 * (t - 1), 3)

        for kind in (2, 1):
            @pl.when((t == 3) & (layer == kind))
            def _():
                for item in proj_in_copies(kind):
                    item.wait_recv()
                for item in proj_chip_copies(kind):
                    item.start()

            @pl.when((t == 4) & (layer == kind))
            def _():
                proj_chip_arrived(kind)
                if kind == 1:
                    wide_out[1, RANK:2 * RANK] = wide_out[1, 0:RANK]

        @pl.when((t == 5) & (layer == 1))
        def _():
            block_load(weight).wait()
            folded[x, z, c, RANK:2 * RANK] = transposed(wide_out[0, RANK:2 * RANK], block[...]).astype(bf16)
            mine = folded.at[x, z, c, RANK:2 * RANK]
            copy(mine, mine, fold_send.at[12], fold_recv.at[12], above).start()

        for index, stage in enumerate(fold_stages[:6]):
            @pl.when((t == Q_LAG + index) & ((layer == 1) | (layer == 2)))
            def _():
                if index == 0:
                    @on(2)
                    def _():
                        mine = folded.at[x, z, c, RANK:2 * RANK]
                        copy(mine, mine, fold_send.at[12], fold_recv.at[12], above).wait_recv()
                stage()

    def step(t, carry):
        @pl.when(t + 2 < PAIRS)
        def _():
            share_pair(t + 2)
        for kind, partner in ((3, above), (2, below)):
            @pl.when((t < 4) & (layer == kind))
            def _():
                rest_slice(t, partner).start()

        @pl.when((t >= 1) & (t < 9) & (layer == 1))
        def _():
            for source, base in main_sources:
                main_slice(t - 1, source, base).start()

        when_in(t, 0, have_share)
        for lag, index in ((0, 0), (LAG_FORWARD, 1), (LAG_ROW, 2), (LAG_ROW_FORWARD, 3), (LAG_LAST, 4)):
            when_in(t, lag, run_stage(index))
        early(t)
        when_in(t, LAG_USE, run_stage(5))

        @pl.when((t == LAG_USE) & (layer < 2))
        def _():
            for i in range(4):
                rest_slice(i, above).wait_recv()

            @on(0)
            def _():
                gate_some(0, REST // 32)

        for kind, rows, target in ((3, MAIN, below), (0, REST, above)):
            @pl.when((layer == kind) & (t >= LAG_USE) & (t < PAIRS + LAG_USE))
            def _():
                upper_chunk(2 * (t - LAG_USE), rows, target)
                upper_chunk(2 * (t - LAG_USE) + 1, rows, target)

        whole = jnp.minimum(2 * (t - LAG_USE) + 2, CHUNKS)
        for kind, rows in ((2, MAIN), (1, REST)):
            @pl.when((layer == kind) & (t >= LAG_USE) & (t < PAIRS + LAG_USE))
            def _():
                ready = jnp.maximum(t - LAG_GRAD, 0)
                lower_weight(2 * (t - LAG_USE), ready, rows)

            @pl.when((layer == kind) & (t >= LAG_GRAD) & (t < PAIRS + LAG_GRAD - 1))
            def _():
                lower_grad(t - LAG_GRAD, whole, rows)
        return carry

    lax.fori_loop(0, PAIRS + LAG_GRAD - 1, step, 0)

    def finish(kind, rows):
        if kind == 2:
            for i in range(8):
                for source, base in main_sources:
                    main_slice(i, source, base).wait_recv()
        lower_gate(PAIRS - 1, rows)
        low_mid[0:rows] = jnp.zeros((rows, 2 * RANK), f32)
        low_two[0:rows] = jnp.zeros((rows, 2 * RANK), f32)

        def body(n, carry):
            add_product(n, PAIRS - 1, rows)
            low_two[0:rows] += transposed(grad[n, 0:rows], wide_out[1, :, columns(n)])

            def inner(i, inner_carry):
                base = pl.multiple_of(i * 64, 64)
                up = grad[n, pl.ds(base, 64)].astype(f32)
                value = second[pl.ds(base, 64), columns(n)].astype(f32)
                low = (up + total[n, pl.ds(base, 64)]).astype(bf16)
                first[pl.ds(base, 64), columns(n)] = low
                grad[n, pl.ds(base, 64)] = (low.astype(f32) * silu_slope(value)).astype(bf16)
                return inner_carry
            lax.fori_loop(0, rows // 64, inner, 0)
            fold = folded[n // 4, n % 4]
            low_mid[0:rows] += (
                transposed(first[0:rows, columns(n)], wide_out[0, :, columns(n)])
                + transposed(grad[n, 0:rows, 0:SHARE], fold[0])
                + transposed(grad[n, 0:rows, SHARE:COLS], fold[1])
            )
            return carry
        lax.fori_loop(0, CHUNKS, body, 0)

    wide = (RANK, 2 * RANK)
    lower = low_half(wide)
    lower_rows = low_half((TOKENS, 2 * RANK))

    tokens = lax.broadcasted_iota(jnp.int32, (TOKENS, 2 * RANK), 0)
    valid = [
        (tokens < jnp.where(lower_rows, lens[0], lens[1])).astype(f32) for lens in (pool_len, val_len)
    ]

    def swap(value):
        return pltpu.roll(value, RANK, 1)

    def put(index, slot, value, mask):
        outgoing[index, slot] = (value * valid[mask]).astype(bf16)

    @on(3)
    def _():
        rows = [low_mid[i * TOKENS:(i + 1) * TOKENS] for i in range(4)]
        landed[0] = (jnp.where(lower_rows, rows[0], rows[1]) * valid[0]).astype(bf16)
        landed[1] = (jnp.where(lower_rows, rows[2], rows[3]) * valid[1]).astype(bf16)
        landed[2] = jnp.zeros_like(landed[2])

    @on(2)
    def _():
        finish(2, MAIN)
        mid = [low_mid[i * TOKENS:(i + 1) * TOKENS] for i in range(3)]
        two = [low_two[i * TOKENS:(i + 1) * TOKENS] for i in range(3)]
        put(1, 0, jnp.where(lower_rows, mid[0], swap(mid[1])), 0)
        put(1, 1, jnp.where(lower_rows, mid[2], 0.0), 1)
        put(0, 0, jnp.where(lower_rows, swap(mid[0]), mid[1]), 0)
        put(0, 1, jnp.where(lower_rows, swap(mid[2]), 0.0), 1)
        landed[0] = (jnp.where(lower_rows, two[0], two[1]) * valid[0]).astype(bf16)
        landed[1] = (jnp.where(lower_rows, two[2], 0.0) * valid[1]).astype(bf16)

    @on(1)
    def _():
        finish(1, REST)
        mid, two = low_mid[0:TOKENS], low_two[0:TOKENS]
        put(0, 1, jnp.where(lower_rows, 0.0, mid), 1)
        put(2, 1, jnp.where(lower_rows, 0.0, two), 1)
        landed[2] = (jnp.where(lower_rows, 0.0, swap(mid)) * valid[1]).astype(bf16)

    def low(source, slot, plane):
        return copy(source, landed.at[slot], low_send.at[slot + 3 * plane], low_recv.at[slot], {"layer": plane})

    def lows(kind):
        if kind == 2:
            return [low(outgoing.at[1, 0], 0, 1), low(outgoing.at[1, 1], 1, 1),
                    low(outgoing.at[0, 0], 0, 0), low(outgoing.at[0, 1], 1, 0)]
        if kind == 1:
            return [low(outgoing.at[0, 1], 2, 0), low(outgoing.at[2, 1], 2, 2)]
        return []

    def lows_in(kind):
        return [low(landed.at[slot], slot, (kind + 1) % 4) for slot in {3: (), 2: (2,), 1: (0, 1), 0: (0, 1, 2)}[kind]]

    for kind in (2, 1):
        @pl.when(layer == kind)
        def _():
            for item in lows(kind):
                item.start()

    for kind in (2, 1, 0):
        @pl.when(layer == kind)
        def _():
            for item in lows_in(kind):
                item.wait_recv()

    def across_tokens(left, right):
        return lax.dot_general(left, right, (((0,), (0,)), ((), ())), precision=highest, preferred_element_type=f32)

    def blocks(value):
        return jnp.where(lower, value[0:RANK], value[RANK:2 * RANK])

    def both(value):
        return value + swap(value)

    pool_low = jnp.where(lower_rows, low_in[0], low_in[1]) * valid[0]
    val_low = jnp.where(lower_rows, low_in[2], low_in[3]) * valid[1]
    pool_out = landed[0].astype(f32)
    val_out = landed[1].astype(f32) + landed[2].astype(f32)
    vals[x, z, c] = blocks(across_tokens(val_out, val_low)).astype(bf16)
    part_in = both(blocks(across_tokens(pool_low, pool_low)))
    part_out = both(blocks(across_tokens(pool_out, pool_out)))
    factors[x * 2 + c, 0:RANK] = jnp.where(lower, part_in, part_out)
    factors[x * 2 + c, RANK:RANK + 8] = jnp.full((8, 2 * RANK), (pool_len[0] + pool_len[1]).astype(f32))

    mine = x * 2 + c
    sent_one = [copy(factors.at[mine], factors.at[mine], fac_send.at[i], fac_recv.at[mine], n[3]) for i, n in enumerate(near)]
    sent_one += [copy(vals.at[x, z, c], vals.at[x, z, c], val_send.at[i], val_recv.at[mine], n[3]) for i, n in enumerate(near)]
    for item in sent_one:
        item.start()
    pool_grads = blocks(across_tokens(pool_low, pool_out))
    for slot, xi, ci, device in near:
        copy(factors.at[slot], factors.at[slot], fac_send.at[0], fac_recv.at[slot], device).wait_recv()
    factors_z[z] = sum(factors[i] for i in range(1, 8)) + factors[0]
    sent_two = [copy(factors_z.at[z], factors_z.at[z], facz_send.at[i], facz_recv.at[z], a[1]) for i, a in enumerate(across)]
    for item in sent_two:
        item.start()
    for slot, xi, ci, device in near:
        copy(vals.at[xi, z, ci], vals.at[xi, z, ci], val_send.at[0], val_recv.at[slot], device).wait_recv()
    sent_three = [copy(vals.at[:, z], vals.at[:, z], valz_send.at[i], valz_recv.at[z], a[1]) for i, a in enumerate(across)]
    for item in sent_three:
        item.start()
    for zi, device in across:
        copy(factors_z.at[zi], factors_z.at[zi], facz_send.at[0], facz_recv.at[zi], device).wait_recv()
    factor_sum = factors_z[0] + factors_z[1] + factors_z[2] + factors_z[3]
    inverse = damped_inverses(factor_sum[0:RANK] / factor_sum[RANK:RANK + 1])
    inv_in = inverse[:, 0:RANK]
    turned = swap(inverse)
    twice = jnp.where(lower, turned, inverse)
    inv_out = jnp.concatenate([jnp.where(lower, twice, 0.0), jnp.where(lower, 0.0, twice)], 0)
    scaled = jnp.dot(inv_in, pool_grads, precision=highest, preferred_element_type=f32)
    scaled = jnp.dot(scaled, inv_out, precision=highest, preferred_element_type=f32)
    coarse = scaled.astype(bf16)
    fine = (scaled - coarse.astype(f32)).astype(bf16)
    empty = jnp.zeros(wide, bf16)

    def spread(value):
        return jnp.concatenate(
            [jnp.concatenate([value, empty], 1), jnp.concatenate([empty, value], 1)], 0
        )

    coarse, fine = spread(coarse), spread(fine)
    for zi, device in across:
        copy(vals.at[:, zi], vals.at[:, zi], valz_send.at[0], valz_recv.at[zi], device).wait_recv()
    every = vals[...].reshape(32 * RANK, 2 * RANK)
    product = jnp.dot(every, coarse, preferred_element_type=f32) + jnp.dot(every, fine, preferred_element_type=f32)
    at_row = lax.broadcasted_iota(jnp.int32, product.shape, 0) % RANK
    at_lane = lax.broadcasted_iota(jnp.int32, product.shape, 1) % RANK
    summed = jnp.where(at_row == at_lane, product, 0.0).reshape(32, RANK, 4 * RANK).sum(1)
    group = lax.broadcasted_iota(jnp.int32, (8, 4 * RANK), 1) // RANK
    picks = (lax.broadcasted_iota(jnp.int32, (8, 4 * RANK), 0) == group).astype(f32)
    part = lax.dot_general(picks, summed, (((1,), (1,)), ((), ())), precision=highest, preferred_element_type=f32)
    layers[layer] = jnp.concatenate([part, jnp.zeros((8, 96), f32)], 1)
    sent_last = [copy(layers.at[layer], layers.at[layer], lay_send.at[i], lay_recv.at[layer], q[1]) for i, q in enumerate(planes)]
    for item in sent_last:
        item.start()
    for plane, device in planes:
        copy(layers.at[plane], layers.at[plane], lay_send.at[0], lay_recv.at[plane], device).wait_recv()
    table = (layers[0] + layers[1] + layers[2] + layers[3]) * (1.0 / (RANK * TOKENS))
    lane = lax.broadcasted_iota(jnp.int32, (128, 16), 0)
    spot_of = lax.broadcasted_iota(jnp.int32, (128, 16), 1) + 16 * layer

    def placed(index):
        return jnp.dot(
            table, (2 * lane + index == spot_of).astype(f32), precision=highest, preferred_element_type=f32
        )

    scores_out[...] = placed(0)[0:2] + placed(1)[2:4]

    for item in sent_one + sent_two + sent_three + sent_last:
        item.wait_send()
    for kind in (2, 1):
        @pl.when(layer == kind)
        def _():
            for item in lows(kind):
                item.wait_send()

    def drain(p, carry):
        run_stage(6)(p)

        @pl.when(layer >= 2)
        def _():
            share_out(2 * p, above).wait_send()
            share_out(2 * p + 1, above).wait_send()
        for kind, rows in ((3, MAIN), (0, REST)):
            @on(kind)
            def _():
                grad_copy(2 * p, rows, above).wait_send()
                grad_copy(2 * p + 1, rows, above).wait_send()
        return carry
    lax.fori_loop(0, PAIRS, drain, 0)

    @pl.when(layer >= 2)
    def _():
        for i in range(4):
            rest_slice(i, above).wait_send()

    @on(1)
    def _():
        for i in range(8):
            for source, base in main_sources:
                main_slice(i, source, base).wait_send()
        mine = folded.at[x, z, c, RANK:2 * RANK]
        copy(mine, mine, fold_send.at[12], fold_recv.at[12], above).wait_send()

    @pl.when((layer == 1) | (layer == 2))
    def _():
        fold_stages[6]()
    for kind in (2, 1, 0):
        @on(kind)
        def _():
            for item in proj_out_copies(kind) + proj_chip_copies(kind):
                item.wait_send()


def whole(*operands):
    anywhere = pl.BlockSpec(memory_space=pl.ANY)
    inside = pl.BlockSpec(memory_space=pltpu.VMEM)
    dma = pltpu.SemaphoreType.DMA
    bf16, f32 = jnp.bfloat16, jnp.float32
    return pl.pallas_call(
        whole_kernel,
        out_shape=jax.ShapeDtypeStruct((2, 16), f32),
        in_specs=[anywhere] * 7 + [pl.BlockSpec(memory_space=pltpu.SMEM)] * 2,
        out_specs=inside,
        scratch_shapes=[
            pltpu.VMEM((CHUNKS, 4, 4, 2, SHARE, COLS), bf16),
            pltpu.VMEM((MAIN, WIDTH), bf16),
            pltpu.VMEM((MAIN, WIDTH), bf16),
            pltpu.VMEM((MAIN, WIDTH), bf16),
            pltpu.VMEM((CHUNKS, MAIN, COLS), bf16),
            pltpu.VMEM((CHUNKS, MAIN, COLS), f32),
            pltpu.VMEM((TOKENS, WIDTH), bf16),
            pltpu.VMEM((2 * RANK, WIDTH), bf16),
            pltpu.VMEM((2, 2 * RANK, WIDTH), bf16),
            pltpu.VMEM((4, 4, 2, 2 * RANK, SHARE), bf16),
            pltpu.VMEM((4 * TOKENS, 2 * RANK), f32),
            pltpu.VMEM((MAIN, 2 * RANK), f32),
            pltpu.VMEM((4, TOKENS, 2 * RANK), f32),
            pltpu.VMEM((3, 2, TOKENS, 2 * RANK), bf16),
            pltpu.VMEM((3, TOKENS, 2 * RANK), bf16),
            pltpu.VMEM((8, RANK + 8, 2 * RANK), f32),
            pltpu.VMEM((4, RANK + 8, 2 * RANK), f32),
            pltpu.VMEM((4, 4, 2, RANK, 2 * RANK), bf16),
            pltpu.VMEM((4, 8, 128), f32),
            dma((CHUNKS, 13)), dma((CHUNKS, 13)), dma((CHUNKS,)), dma((CHUNKS,)), dma((24,)), dma((24,)),
            dma((CHUNKS + 12,)), dma((13,)), dma((13,)), dma((7,)), dma((7,)),
            dma((12,)), dma((3,)), dma((7,)), dma((8,)), dma((7,)), dma((8,)),
            dma((3,)), dma((4,)), dma((3,)), dma((4,)), dma((3,)), dma((4,)),
        ],
        compiler_params=pltpu.CompilerParams(
            collective_id=0, has_side_effects=True, vmem_limit_bytes=62 * 1024 * 1024
        ),
        name="whole",
    )(*operands)


def on_device(
    pool_inputs, val_inputs, pool_top, val_top, weight, proj_in, proj_out, pool_len, val_len
):
    return whole(
        pool_inputs[0], val_inputs[0], pool_top, val_top, weight[0], proj_in[0].T, proj_out[0].T, pool_len, val_len
    )


def solution(mesh):
    placed = (
        P("layer", "trace", None, None),
        P("layer", "trace", None, None),
        P("trace", None, None),
        P("trace", None, None),
        P("layer", "trace", None),
        P("layer", None, None),
        P("layer", None, None),
        P("trace"),
        P("trace"),
    )
    return jax.shard_map(
        on_device, mesh=mesh, in_specs=placed, out_specs=P("trace", "layer"), check_vma=False
    )
```

```python
import functools

import jax
import jax.numpy as jnp
from jax import lax
from jax.experimental import pallas as pl
from jax.experimental.pallas import tpu as pltpu
from jax.sharding import PartitionSpec as P

MESH = pl.DeviceIdType.MESH
WIDTH = 4096
TOKENS = 128
RANK = 64
CHUNKS = 16
COLS = WIDTH // CHUNKS
PAIRS = CHUNKS // 2
SHARE = 128
MAIN = 384
REST = 128
LAG_FORWARD, LAG_ROW, LAG_ROW_FORWARD, LAG_LAST, LAG_USE = 1, 2, 3, 4, 5
LAG_GRAD = 6
AHEAD = 3
SLICE = 32
PART = 16
FOLD_ONE, FOLD_TWO = 5, 7


def silu_slope(values):
    logistic = jax.nn.sigmoid(values)
    return logistic * (1.0 + values * (1.0 - logistic))


def low_half(shape):
    return lax.broadcasted_iota(jnp.int32, shape, len(shape) - 1) < RANK


def damped_inverses(pair):
    rows = lax.broadcasted_iota(jnp.int32, pair.shape, 0)
    lanes = lax.broadcasted_iota(jnp.int32, pair.shape, 1)
    lower = lanes < RANK
    column = jnp.where(lower, lanes, lanes - RANK)
    diagonal = rows == column
    on_diagonal = jnp.where(diagonal, pair, 0.0)
    trace_first = jnp.sum(jnp.where(lower, on_diagonal, 0.0), keepdims=True)
    trace_second = jnp.sum(jnp.where(lower, 0.0, on_diagonal), keepdims=True)
    damping = jnp.where(lower, trace_first, trace_second) * (0.1 / RANK)
    value = jnp.where(diagonal, pair + damping, pair)
    at = column[0:1]

    def spread(k):
        return jnp.where(
            lower,
            jnp.broadcast_to(value[:, k:k + 1], pair.shape),
            jnp.broadcast_to(value[:, RANK + k:RANK + k + 1], pair.shape),
        )

    for k in range(0, RANK, 2):
        one, two = spread(k), spread(k + 1)
        a, b = one[k:k + 1], two[k:k + 1]
        c, d = one[k + 1:k + 2], two[k + 1:k + 2]
        scale = 1.0 / (a * d - b * c)
        a, b, c, d = a * scale, b * scale, c * scale, d * scale
        upper, under = value[k:k + 1], value[k + 1:k + 2]
        row_one = jnp.where(at == k, d, jnp.where(at == k + 1, -b, d * upper - b * under))
        row_two = jnp.where(at == k, -c, jnp.where(at == k + 1, a, a * under - c * upper))
        one = jnp.where(rows == k, -1.0, jnp.where(rows == k + 1, 0.0, one))
        two = jnp.where(rows == k + 1, -1.0, jnp.where(rows == k, 0.0, two))
        gone = (rows == k) | (rows == k + 1) | (column == k) | (column == k + 1)
        value = jnp.where(gone, 0.0, value) - one * row_one - two * row_two
    return value


def whole_kernel(
    pool_in, val_in, pool_top, val_top, weight, proj_in, proj_out, pool_len, val_len,
    scores_out,
    held, first, second, gated, grad, total, block, wide_in, wide_out, folded,
    low_mid, low_two, low_in, outgoing,
    landed, factors, factors_z, vals, layers,
    send, recv, grad_send, grad_recv, act_send, act_recv, local, fold_send, fold_recv, proj_send, proj_recv,
    low_send, low_recv, fac_send, fac_recv, val_send, val_recv, facz_send, facz_recv, valz_send, valz_recv,
    lay_send, lay_recv,
):
    layer = lax.axis_index("layer")
    trace = lax.axis_index("trace")
    x, z, c = trace // 8, (trace // 2) % 4, trace % 2
    xp, xm, xo = (x + 1) % 4, (x + 3) % 4, (x + 2) % 4
    zp, zm, zo = (z + 1) % 4, (z + 3) % 4, (z + 2) % 4
    other = 1 - c
    highest = lax.Precision.HIGHEST
    f32, bf16 = jnp.float32, jnp.bfloat16

    def at(xi, zi, ci):
        return {"trace": xi * 8 + zi * 2 + ci}

    above = {"layer": (layer + 1) % 4}
    below = {"layer": (layer + 3) % 4}
    sibling = at(x, z, other)

    near = []
    for dx in range(4):
        for dc in range(2):
            if dx or dc:
                xi, ci = (x + dx) % 4, (c + dc) % 2
                near.append((xi * 2 + ci, xi, ci, at(xi, z, ci)))
    across = [((z + dz) % 4, at(x, (z + dz) % 4, c)) for dz in (1, 3, 2)]
    planes = [((layer + dl) % 4, {"layer": (layer + dl) % 4}) for dl in (1, 3, 2)]
    barrier = pltpu.get_barrier_semaphore()
    for device in [n[3] for n in near] + [a[1] for a in across] + [q[1] for q in planes]:
        pl.semaphore_signal(barrier, inc=1, device_id=device, device_id_type=MESH)
    pl.semaphore_wait(barrier, len(near) + len(across) + len(planes))

    def copy(src, dst, send_sem, recv_sem, device):
        return pltpu.make_async_remote_copy(
            src_ref=src, dst_ref=dst, send_sem=send_sem, recv_sem=recv_sem, device_id=device, device_id_type=MESH
        )

    def columns(j):
        return pl.ds(pl.multiple_of(j * COLS, COLS), COLS)

    def transposed(left, right):
        return lax.dot_general(left, right, (((1,), (1,)), ((), ())), preferred_element_type=f32)

    def on(kind):
        return pl.when(layer == kind)

    def own(j):
        return held.at[j, x, z, c]

    def share_out(j, device):
        return copy(weight.at[:, columns(j)], own(j), send.at[j, 12], recv.at[j, 12], device)

    def share_local(j):
        return pltpu.make_async_copy(weight.at[:, columns(j)], own(j), local.at[j])

    def load(src, dst, index):
        return pltpu.make_async_copy(src, dst, local.at[CHUNKS + index])

    def row_loads(pool, val, target, base):
        return [
            load(pool.at[0], target.at[0:128], base), load(pool.at[1], target.at[128:256], base + 1),
            load(val.at[0], target.at[256:384], base + 2),
        ]

    def loads(kind):
        return {
            3: lambda: row_loads(pool_in, val_in, first, 0) + row_loads(pool_top, val_top, second, 3),
            2: lambda: row_loads(pool_in, val_in, first, 0),
            1: lambda: [load(val_in.at[1], second.at[0:128], 0)],
            0: lambda: [load(val_top.at[1], second.at[0:128], 0)],
        }[kind]()

    def rows_of(base, i):
        return pl.ds(pl.multiple_of(base + i * SLICE, SLICE), SLICE)

    def rest_slice(i, device):
        return copy(
            val_in.at[1, rows_of(0, i)], first.at[rows_of(0, i)], act_send.at[i], act_recv.at[i], device
        )

    def main_slice(i, source, base):
        rows = pl.ds(pl.multiple_of(i * PART, PART), PART)
        there = pl.ds(pl.multiple_of(base + i * PART, PART), PART)
        index = base // PART + i
        return copy(source.at[rows], second.at[there], act_send.at[index], act_recv.at[index], above)

    main_sources = ((pool_in.at[0], 0), (pool_in.at[1], 128), (val_in.at[0], 256))

    def gather_stages(j, view, flip, sems, part):
        send_j, recv_j = sems
        ahead, behind, far = (zp, zm, zo) if flip else (xp, xm, xo)
        up, down, beyond = (xp, xm, xo) if flip else (zp, zm, zo)
        lo, mid, hi = part

        def spot(along, over, ci, rows):
            return view(over, along, ci, *rows) if flip else view(along, over, ci, *rows)

        me_along, me_over = (z, x) if flip else (x, z)

        def to_along(i):
            return at(x, i, c) if flip else at(i, z, c)

        def to_over(i):
            return at(i, z, c) if flip else at(x, i, c)

        full = (lo, hi)
        every = slice(0, 4)

        def push(ref, slot, device):
            copy(ref, ref, send_j(j, slot), recv_j(j, slot), device).start()

        def arrived(ref, slot):
            copy(ref, ref, send_j(j, slot), recv_j(j, slot), sibling).wait_recv()

        def share():
            ref = spot(me_along, me_over, c, full)
            push(ref, 0, to_along(ahead))
            push(ref, 1, to_along(behind))

        def forward_up():
            arrived(spot(behind, me_over, c, full), 0)
            push(spot(behind, me_over, c, (lo, mid)), 2, to_along(ahead))

        def forward_down():
            arrived(spot(ahead, me_over, c, full), 1)
            push(spot(ahead, me_over, c, (mid, hi)), 3, to_along(behind))

        def row():
            arrived(spot(far, me_over, c, (lo, mid)), 2)
            arrived(spot(far, me_over, c, (mid, hi)), 3)
            ref = spot(every, me_over, c, full)
            push(ref, 4, to_over(up))
            push(ref, 5, to_over(down))

        def row_up():
            arrived(spot(every, down, c, full), 4)
            push(spot(slice(0, 2), down, c, full), 6, to_over(up))

        def row_down():
            arrived(spot(every, up, c, full), 5)
            push(spot(slice(2, 4), up, c, full), 7, to_over(down))

        def last():
            arrived(spot(slice(0, 2), beyond, c, full), 6)
            arrived(spot(slice(2, 4), beyond, c, full), 7)

        def over_chip(slot, over):
            return lambda: push(spot(every, over, c, full), slot, sibling)

        def whole():
            for slot, over in ((8, me_over), (9, down), (10, up), (11, beyond)):
                arrived(spot(every, over, other, full), slot)

        def drain():
            def left(ref, slot):
                copy(ref, ref, send_j(j, slot), recv_j(j, slot), sibling).wait_send()

            for slot in (0, 1):
                left(spot(me_along, me_over, c, full), slot)
            left(spot(me_along, me_over, c, (lo, mid)), 2)
            left(spot(me_along, me_over, c, (mid, hi)), 3)
            for slot in (4, 5, 8, 9, 10, 11):
                left(spot(every, me_over, c, full), slot)
            left(spot(slice(0, 2), me_over, c, full), 6)
            left(spot(slice(2, 4), me_over, c, full), 7)

        return (
            [share], [forward_up, forward_down], [row, over_chip(8, me_over)],
            [row_up, row_down, over_chip(9, down), over_chip(10, up)], [last, over_chip(11, beyond)], [whole], [drain],
        )

    def weight_view(j):
        return lambda xi, zi, ci, lo, hi: held.at[j, xi, zi, ci, lo:hi]

    weight_sems = (lambda j, slot: send.at[j, slot], lambda j, slot: recv.at[j, slot])
    fold_sems = (lambda j, slot: fold_send.at[slot], lambda j, slot: fold_recv.at[slot])

    def weight_stages(p):
        a, b = 2 * p, 2 * p + 1
        part = (0, SHARE // 2, SHARE)
        return zip(
            gather_stages(a, weight_view(a), False, weight_sems, part),
            gather_stages(b, weight_view(b), True, weight_sems, part),
        )

    def run_stage(index):
        def stage(p):
            for parts in zip(*list(weight_stages(p))[index]):
                for part in parts:
                    part()
        return stage

    def fold_view(xi, zi, ci, lo, hi):
        return folded.at[xi, zi, ci, lo:hi]

    fold_stages = gather_stages(0, fold_view, False, fold_sems, (RANK, RANK + RANK // 2, 2 * RANK))

    def have_share(p):
        for j in (2 * p, 2 * p + 1):
            @pl.when(layer >= 2)
            def _():
                share_local(j).wait()

            @pl.when(layer < 2)
            def _():
                copy(own(j), own(j), send.at[j, 12], recv.at[j, 12], sibling).wait_recv()

    def half_of(which, index, low, ci):
        return which.at[index, low:low + RANK, pl.ds(pl.multiple_of(ci * (WIDTH // 2), WIDTH // 2), WIDTH // 2)]

    def proj_copy(index, low, slot, device):
        ref = half_of(wide_out, index, low, c)
        return copy(ref, ref, proj_send.at[slot], proj_recv.at[slot], device)

    def proj_out_copies(kind):
        if kind == 2:
            return [proj_copy(1, 0, 3, {"layer": 1})]
        if kind == 1:
            return [proj_copy(0, 0, 0, {"layer": 2})]
        if kind == 0:
            return [proj_copy(0, RANK, 1, {"layer": 1}), proj_copy(0, RANK, 2, {"layer": 2})]
        return []

    def proj_in_copies(kind):
        if kind == 2:
            return [proj_copy(0, 0, 0, above), proj_copy(0, RANK, 2, above)]
        if kind == 1:
            return [proj_copy(0, RANK, 1, above), proj_copy(1, 0, 3, above)]
        return []

    def proj_chip_copies(kind):
        if kind == 2:
            return [proj_copy(0, 0, 4, sibling), proj_copy(0, RANK, 5, sibling)]
        if kind == 1:
            return [proj_copy(0, RANK, 5, sibling), proj_copy(1, 0, 6, sibling)]
        return []

    def proj_chip_arrived(kind):
        for index, low, slot in {2: ((0, 0, 4), (0, RANK, 5)), 1: ((0, RANK, 5), (1, 0, 6))}[kind]:
            ref = half_of(wide_out, index, low, other)
            copy(ref, ref, proj_send.at[slot], proj_recv.at[slot], sibling).wait_recv()

    def proj_loads(kind):
        places = {
            3: [(1, 0), (1, RANK)], 2: [(1, 0), (1, RANK)], 1: [(0, 0)], 0: [(0, RANK)],
        }[kind]
        return [
            load(proj_out, wide_out.at[index, low:low + RANK], 8 + i) for i, (index, low) in enumerate(places)
        ]

    def proj_in_loads():
        return [load(proj_in, wide_in.at[i * RANK:(i + 1) * RANK], 10 + i) for i in range(2)]

    def block_source(index):
        return (pool_in.at[0], pool_in.at[1], val_in.at[0], val_in.at[1],
                pool_top.at[0], pool_top.at[1], val_top.at[0], val_top.at[1])[index]

    def block_load(source):
        return load(source, block, 7)

    @pl.when(layer >= 2)
    def _():
        def body(j, carry):
            share_local(j).start()
            return carry
        lax.fori_loop(0, CHUNKS, body, 0)

    def share_pair(p):
        for kind, partner in ((3, above), (2, below)):
            @on(kind)
            def _():
                share_out(2 * p, partner).start()
                share_out(2 * p + 1, partner).start()

    for pair in range(AHEAD):
        share_pair(pair)
    for kind in range(4):
        @on(kind)
        def _():
            for item in proj_loads(kind) + loads(kind):
                item.start()
    for item in proj_in_loads():
        item.start()
    block_load(block_source(0)).start()

    def gate_rows(index):
        base = pl.multiple_of(index * 32, 32)
        value = first[pl.ds(base, 32), :].astype(f32)
        top = second[pl.ds(base, 32), :].astype(f32)
        gated[pl.ds(base, 32), :] = (top * silu_slope(value)).astype(bf16)

    def gate_some(start, count):
        def body(i, carry):
            gate_rows(start + i)
            return carry
        lax.fori_loop(0, count, body, 0)

    def grad_copy(j, rows, device):
        return copy(grad.at[j, 0:rows], grad.at[j, 0:rows], grad_send.at[j], grad_recv.at[j], device)

    def upper_chunk(j, rows, device):
        total[0, 0:rows] = second[0:rows, columns(j)].astype(f32)

        def body(xi, carry):
            piece = held[j, xi].reshape(WIDTH // 4, COLS)
            left = gated[0:rows, pl.ds(pl.multiple_of(xi * (WIDTH // 4), WIDTH // 4), WIDTH // 4)]
            total[0, 0:rows] += jnp.dot(left, piece, preferred_element_type=f32)
            return carry
        lax.fori_loop(0, 4, body, 0)
        grad[j, 0:rows] = total[0, 0:rows].astype(bf16)
        grad_copy(j, rows, device).start()

    def add_product(n, q, rows):
        piece = held[n, q // 2, pl.ds(2 * (q % 2), 2)].reshape(4 * SHARE, COLS)
        left = gated[0:rows, pl.ds(pl.multiple_of(q * 2 * COLS, 2 * COLS), 2 * COLS)]
        total[n, 0:rows] += jnp.dot(left, piece, preferred_element_type=f32)

    def lower_weight(n, ready, rows):
        total[n, 0:rows] = jnp.zeros((rows, COLS), f32)
        total[n + 1, 0:rows] = jnp.zeros((rows, COLS), f32)

        def body(q, carry):
            add_product(n, q, rows)
            add_product(n + 1, q, rows)
            return carry
        lax.fori_loop(0, ready, body, 0)

    def lower_gate(q, rows):
        for k in (2 * q, 2 * q + 1):
            grad_copy(k, rows, above).wait_recv()

            def gating(i, carry):
                base = pl.multiple_of(i * 64, 64)
                value = first[pl.ds(base, 64), columns(k)].astype(f32)
                up = grad[k, pl.ds(base, 64)].astype(f32)
                gated[pl.ds(base, 64), columns(k)] = (up * silu_slope(value)).astype(bf16)
                return carry
            lax.fori_loop(0, rows // 64, gating, 0)
            low_two[0:rows] += transposed(grad[k, 0:rows], wide_out[1, :, columns(k)])

    def lower_grad(q, ready, rows):
        lower_gate(q, rows)

        def body(n, carry):
            add_product(2 * n, q, rows)
            add_product(2 * n + 1, q, rows)
            return carry
        lax.fori_loop(0, ready // 2, body, 0)

    def when_in(t, lag, what):
        @pl.when((t >= lag) & (t < PAIRS + lag))
        def _():
            what(t - lag)

    def early(t):
        @pl.when(t == 0)
        def _():
            for kind in range(4):
                @on(kind)
                def _():
                    for item in proj_loads(kind):
                        item.wait()
                    for item in proj_out_copies(kind):
                        item.start()
            folded[:, :, :, 0:RANK] = jnp.zeros((4, 4, 2, RANK, 2 * RANK), bf16)
            low_two[...] = jnp.zeros((MAIN, 2 * RANK), f32)

        @pl.when(t == 1)
        def _():
            for item in proj_in_loads():
                item.wait()
            for kind in range(4):
                @on(kind)
                def _():
                    for item in loads(kind):
                        item.wait()

        for index in range(4):
            turn_of = 1 + index + jnp.where((layer == 1) & (index > 1), 2, 0)

            @pl.when(t == turn_of)
            def _():
                block_load(block_source(index)).wait()
                low_in[index] = transposed(block[...], wide_in[...])
                if index == 1:
                    @on(1)
                    def _():
                        block_load(weight).start()

                    @pl.when(layer != 1)
                    def _():
                        block_load(block_source(2)).start()
                elif index < 3:
                    block_load(block_source(index + 1)).start()
                else:
                    @on(3)
                    def _():
                        block_load(block_source(4)).start()
        for index in range(4, 8):
            @pl.when((t == 1 + index) & (layer == 3))
            def _():
                block_load(block_source(index)).wait()
                low_mid[pl.ds((index - 4) * TOKENS, TOKENS)] = transposed(block[...], wide_out[1])
                if index < 7:
                    block_load(block_source(index + 1)).start()

        @pl.when((t >= 1) & (t < 5) & (layer == 3))
        def _():
            gate_some(3 * (t - 1), 3)

        for kind, when in ((2, 9), (1, 3)):
            @pl.when((t == when) & (layer == kind))
            def _():
                for item in proj_in_copies(kind):
                    item.wait_recv()
                for item in proj_chip_copies(kind):
                    item.start()

            @pl.when((t == when + 1) & (layer == kind))
            def _():
                proj_chip_arrived(kind)
                if kind == 1:
                    wide_out[1, RANK:2 * RANK] = wide_out[1, 0:RANK]

        @pl.when((t == 4) & (layer == 1))
        def _():
            block_load(weight).wait()
            folded[x, z, c, RANK:2 * RANK] = transposed(wide_out[0, RANK:2 * RANK], block[...]).astype(bf16)
            mine = folded.at[x, z, c, RANK:2 * RANK]
            copy(mine, mine, fold_send.at[12], fold_recv.at[12], above).start()
            block_load(block_source(2)).start()

        for index, stage in enumerate(fold_stages[:6]):
            lag = jnp.where(layer == 1, FOLD_ONE, FOLD_TWO)

            @pl.when((t == lag + index) & ((layer == 1) | (layer == 2)))
            def _():
                if index == 0:
                    @on(2)
                    def _():
                        mine = folded.at[x, z, c, RANK:2 * RANK]
                        copy(mine, mine, fold_send.at[12], fold_recv.at[12], above).wait_recv()
                for part in stage:
                    part()

    def step(t, carry):
        @pl.when(t + AHEAD < PAIRS)
        def _():
            share_pair(t + AHEAD)
        for kind, partner in ((3, above), (2, below)):
            @pl.when((t >= 1) & (t < 5) & (layer == kind))
            def _():
                rest_slice(t - 1, partner).start()

        @pl.when((t >= 1) & (t < 9) & (layer == 1))
        def _():
            for source, base in main_sources:
                main_slice(t - 1, source, base).start()

        when_in(t, 0, have_share)
        for lag, index in ((0, 0), (LAG_FORWARD, 1), (LAG_ROW, 2), (LAG_ROW_FORWARD, 3), (LAG_LAST, 4)):
            when_in(t, lag, run_stage(index))
        early(t)
        when_in(t, LAG_USE, run_stage(5))

        @pl.when((t == LAG_USE) & (layer < 2))
        def _():
            for i in range(4):
                rest_slice(i, above).wait_recv()

            @on(0)
            def _():
                gate_some(0, REST // 32)

        for kind, rows, target in ((3, MAIN, below), (0, REST, above)):
            @pl.when((layer == kind) & (t >= LAG_USE) & (t < PAIRS + LAG_USE))
            def _():
                upper_chunk(2 * (t - LAG_USE), rows, target)
                upper_chunk(2 * (t - LAG_USE) + 1, rows, target)

        whole = jnp.minimum(2 * (t - LAG_USE) + 2, CHUNKS)
        for kind, rows in ((2, MAIN), (1, REST)):
            @pl.when((layer == kind) & (t >= LAG_USE) & (t < PAIRS + LAG_USE))
            def _():
                ready = jnp.maximum(t - LAG_GRAD, 0)
                lower_weight(2 * (t - LAG_USE), ready, rows)

            @pl.when((layer == kind) & (t >= LAG_GRAD) & (t < PAIRS + LAG_GRAD - 1))
            def _():
                lower_grad(t - LAG_GRAD, whole, rows)
        return carry

    lax.fori_loop(0, PAIRS + LAG_GRAD - 1, step, 0)

    def drain(p, carry):
        run_stage(6)(p)

        @pl.when(layer >= 2)
        def _():
            share_out(2 * p, above).wait_send()
            share_out(2 * p + 1, above).wait_send()
        for kind, rows in ((3, MAIN), (0, REST)):
            @on(kind)
            def _():
                grad_copy(2 * p, rows, above).wait_send()
                grad_copy(2 * p + 1, rows, above).wait_send()
        return carry
    lax.fori_loop(0, PAIRS, drain, 0)

    @pl.when(layer >= 2)
    def _():
        for i in range(4):
            rest_slice(i, above).wait_send()

    @on(1)
    def _():
        for i in range(8):
            for source, base in main_sources:
                main_slice(i, source, base).wait_send()
        mine = folded.at[x, z, c, RANK:2 * RANK]
        copy(mine, mine, fold_send.at[12], fold_recv.at[12], above).wait_send()

    @pl.when((layer == 1) | (layer == 2))
    def _():
        fold_stages[6][0]()
    for kind in (2, 1, 0):
        @on(kind)
        def _():
            for item in proj_out_copies(kind) + proj_chip_copies(kind):
                item.wait_send()

    def finish(kind, rows):
        if kind == 2:
            for i in range(8):
                for source, base in main_sources:
                    main_slice(i, source, base).wait_recv()
        lower_gate(PAIRS - 1, rows)
        low_mid[0:rows] = jnp.zeros((rows, 2 * RANK), f32)

        def body(i, carry):
            for n in (2 * i, 2 * i + 1):
                add_product(n, PAIRS - 1, rows)
                for base in range(0, rows, 64):
                    part = slice(base, base + 64)
                    up = grad[n, part].astype(f32)
                    value = second[part, columns(n)].astype(f32)
                    low = (up + total[n, part]).astype(bf16)
                    first[part, columns(n)] = low
                    grad[n, part] = (low.astype(f32) * silu_slope(value)).astype(bf16)
                fold = folded[n // 4, n % 4]
                left = jnp.concatenate([first[0:rows, columns(n)], grad[n, 0:rows]], 1)
                right = jnp.concatenate([wide_out[0, :, columns(n)], fold[0], fold[1]], 1)
                low_mid[0:rows] += transposed(left, right)
            return carry
        lax.fori_loop(0, PAIRS, body, 0)

    wide = (RANK, 2 * RANK)
    lower = low_half(wide)
    lower_rows = low_half((TOKENS, 2 * RANK))

    tokens = lax.broadcasted_iota(jnp.int32, (TOKENS, 2 * RANK), 0)
    valid = [
        (tokens < jnp.where(lower_rows, lens[0], lens[1])).astype(f32) for lens in (pool_len, val_len)
    ]

    def swap(value):
        return pltpu.roll(value, RANK, 1)

    def put(index, slot, value, mask):
        outgoing[index, slot] = (value * valid[mask]).astype(bf16)

    @on(3)
    def _():
        rows = [low_mid[i * TOKENS:(i + 1) * TOKENS] for i in range(4)]
        landed[0] = (jnp.where(lower_rows, rows[0], rows[1]) * valid[0]).astype(bf16)
        landed[1] = (jnp.where(lower_rows, rows[2], rows[3]) * valid[1]).astype(bf16)
        landed[2] = jnp.zeros_like(landed[2])

    @on(2)
    def _():
        finish(2, MAIN)
        mid = [low_mid[i * TOKENS:(i + 1) * TOKENS] for i in range(3)]
        two = [low_two[i * TOKENS:(i + 1) * TOKENS] for i in range(3)]
        put(1, 0, jnp.where(lower_rows, mid[0], swap(mid[1])), 0)
        put(1, 1, jnp.where(lower_rows, mid[2], 0.0), 1)
        put(0, 0, jnp.where(lower_rows, swap(mid[0]), mid[1]), 0)
        put(0, 1, jnp.where(lower_rows, swap(mid[2]), 0.0), 1)
        landed[0] = (jnp.where(lower_rows, two[0], two[1]) * valid[0]).astype(bf16)
        landed[1] = (jnp.where(lower_rows, two[2], 0.0) * valid[1]).astype(bf16)

    @on(1)
    def _():
        finish(1, REST)
        mid, two = low_mid[0:TOKENS], low_two[0:TOKENS]
        put(0, 1, jnp.where(lower_rows, 0.0, mid), 1)
        put(2, 1, jnp.where(lower_rows, 0.0, two), 1)
        landed[2] = (jnp.where(lower_rows, 0.0, swap(mid)) * valid[1]).astype(bf16)

    def low(source, slot, plane):
        return copy(source, landed.at[slot], low_send.at[slot + 3 * plane], low_recv.at[slot], {"layer": plane})

    def lows(kind):
        if kind == 2:
            return [low(outgoing.at[1, 0], 0, 1), low(outgoing.at[1, 1], 1, 1),
                    low(outgoing.at[0, 0], 0, 0), low(outgoing.at[0, 1], 1, 0)]
        if kind == 1:
            return [low(outgoing.at[0, 1], 2, 0), low(outgoing.at[2, 1], 2, 2)]
        return []

    def lows_in(kind):
        return [low(landed.at[slot], slot, (kind + 1) % 4) for slot in {3: (), 2: (2,), 1: (0, 1), 0: (0, 1, 2)}[kind]]

    for kind in (2, 1):
        @pl.when(layer == kind)
        def _():
            for item in lows(kind):
                item.start()

    for kind in (2, 1, 0):
        @pl.when(layer == kind)
        def _():
            for item in lows_in(kind):
                item.wait_recv()

    def across_tokens(left, right):
        return lax.dot_general(left, right, (((0,), (0,)), ((), ())), precision=highest, preferred_element_type=f32)

    def blocks(value):
        return jnp.where(lower, value[0:RANK], value[RANK:2 * RANK])

    def both(value):
        return value + swap(value)

    pool_low = jnp.where(lower_rows, low_in[0], low_in[1]) * valid[0]
    val_low = jnp.where(lower_rows, low_in[2], low_in[3]) * valid[1]
    pool_out = landed[0].astype(f32)
    val_out = landed[1].astype(f32) + landed[2].astype(f32)
    vals[x, z, c] = blocks(across_tokens(val_out, val_low)).astype(bf16)
    part_in = both(blocks(across_tokens(pool_low, pool_low)))
    part_out = both(blocks(across_tokens(pool_out, pool_out)))
    factors[x * 2 + c, 0:RANK] = jnp.where(lower, part_in, part_out)
    factors[x * 2 + c, RANK:RANK + 8] = jnp.full((8, 2 * RANK), (pool_len[0] + pool_len[1]).astype(f32))

    mine = x * 2 + c
    sent_one = [copy(factors.at[mine], factors.at[mine], fac_send.at[i], fac_recv.at[mine], n[3]) for i, n in enumerate(near)]
    sent_one += [copy(vals.at[x, z, c], vals.at[x, z, c], val_send.at[i], val_recv.at[mine], n[3]) for i, n in enumerate(near)]
    for item in sent_one:
        item.start()
    pool_grads = blocks(across_tokens(pool_low, pool_out))
    for slot, xi, ci, device in near:
        copy(factors.at[slot], factors.at[slot], fac_send.at[0], fac_recv.at[slot], device).wait_recv()
    factors_z[z] = sum(factors[i] for i in range(1, 8)) + factors[0]
    sent_two = [copy(factors_z.at[z], factors_z.at[z], facz_send.at[i], facz_recv.at[z], a[1]) for i, a in enumerate(across)]
    for item in sent_two:
        item.start()
    for slot, xi, ci, device in near:
        copy(vals.at[xi, z, ci], vals.at[xi, z, ci], val_send.at[0], val_recv.at[slot], device).wait_recv()
    sent_three = [copy(vals.at[:, z], vals.at[:, z], valz_send.at[i], valz_recv.at[z], a[1]) for i, a in enumerate(across)]
    for item in sent_three:
        item.start()
    for zi, device in across:
        copy(factors_z.at[zi], factors_z.at[zi], facz_send.at[0], facz_recv.at[zi], device).wait_recv()
    factor_sum = factors_z[0] + factors_z[1] + factors_z[2] + factors_z[3]
    inverse = damped_inverses(factor_sum[0:RANK] / factor_sum[RANK:RANK + 1])
    inv_in = inverse[:, 0:RANK]
    turned = swap(inverse)
    twice = jnp.where(lower, turned, inverse)
    inv_out = jnp.concatenate([jnp.where(lower, twice, 0.0), jnp.where(lower, 0.0, twice)], 0)
    scaled = jnp.dot(inv_in, pool_grads, precision=highest, preferred_element_type=f32)
    scaled = jnp.dot(scaled, inv_out, precision=highest, preferred_element_type=f32)
    coarse = scaled.astype(bf16)
    fine = (scaled - coarse.astype(f32)).astype(bf16)
    empty = jnp.zeros(wide, bf16)

    def spread(value):
        return jnp.concatenate(
            [jnp.concatenate([value, empty], 1), jnp.concatenate([empty, value], 1)], 0
        )

    coarse, fine = spread(coarse), spread(fine)
    for zi, device in across:
        copy(vals.at[:, zi], vals.at[:, zi], valz_send.at[0], valz_recv.at[zi], device).wait_recv()
    every = vals[...].reshape(32 * RANK, 2 * RANK)
    product = jnp.dot(every, coarse, preferred_element_type=f32) + jnp.dot(every, fine, preferred_element_type=f32)
    at_row = lax.broadcasted_iota(jnp.int32, product.shape, 0) % RANK
    at_lane = lax.broadcasted_iota(jnp.int32, product.shape, 1) % RANK
    summed = jnp.where(at_row == at_lane, product, 0.0).reshape(32, RANK, 4 * RANK).sum(1)
    group = lax.broadcasted_iota(jnp.int32, (8, 4 * RANK), 1) // RANK
    picks = (lax.broadcasted_iota(jnp.int32, (8, 4 * RANK), 0) == group).astype(f32)
    part = lax.dot_general(picks, summed, (((1,), (1,)), ((), ())), precision=highest, preferred_element_type=f32)
    layers[layer] = jnp.concatenate([part, jnp.zeros((8, 96), f32)], 1)
    sent_last = [copy(layers.at[layer], layers.at[layer], lay_send.at[i], lay_recv.at[layer], q[1]) for i, q in enumerate(planes)]
    for item in sent_last:
        item.start()
    for plane, device in planes:
        copy(layers.at[plane], layers.at[plane], lay_send.at[0], lay_recv.at[plane], device).wait_recv()
    table = (layers[0] + layers[1] + layers[2] + layers[3]) * (1.0 / (RANK * TOKENS))
    lane = lax.broadcasted_iota(jnp.int32, (128, 16), 0)
    spot_of = lax.broadcasted_iota(jnp.int32, (128, 16), 1) + 16 * layer

    def placed(index):
        return jnp.dot(
            table, (2 * lane + index == spot_of).astype(f32), precision=highest, preferred_element_type=f32
        )

    scores_out[...] = placed(0)[0:2] + placed(1)[2:4]

    for item in sent_one + sent_two + sent_three + sent_last:
        item.wait_send()
    for kind in (2, 1):
        @pl.when(layer == kind)
        def _():
            for item in lows(kind):
                item.wait_send()


def whole(*operands):
    anywhere = pl.BlockSpec(memory_space=pl.ANY)
    inside = pl.BlockSpec(memory_space=pltpu.VMEM)
    dma = pltpu.SemaphoreType.DMA
    bf16, f32 = jnp.bfloat16, jnp.float32
    return pl.pallas_call(
        whole_kernel,
        out_shape=jax.ShapeDtypeStruct((2, 16), f32),
        in_specs=[anywhere] * 7 + [pl.BlockSpec(memory_space=pltpu.SMEM)] * 2,
        out_specs=inside,
        scratch_shapes=[
            pltpu.VMEM((CHUNKS, 4, 4, 2, SHARE, COLS), bf16),
            pltpu.VMEM((MAIN, WIDTH), bf16),
            pltpu.VMEM((MAIN, WIDTH), bf16),
            pltpu.VMEM((MAIN, WIDTH), bf16),
            pltpu.VMEM((CHUNKS, MAIN, COLS), bf16),
            pltpu.VMEM((CHUNKS, MAIN, COLS), f32),
            pltpu.VMEM((TOKENS, WIDTH), bf16),
            pltpu.VMEM((2 * RANK, WIDTH), bf16),
            pltpu.VMEM((2, 2 * RANK, WIDTH), bf16),
            pltpu.VMEM((4, 4, 2, 2 * RANK, SHARE), bf16),
            pltpu.VMEM((4 * TOKENS, 2 * RANK), f32),
            pltpu.VMEM((MAIN, 2 * RANK), f32),
            pltpu.VMEM((4, TOKENS, 2 * RANK), f32),
            pltpu.VMEM((3, 2, TOKENS, 2 * RANK), bf16),
            pltpu.VMEM((3, TOKENS, 2 * RANK), bf16),
            pltpu.VMEM((8, RANK + 8, 2 * RANK), f32),
            pltpu.VMEM((4, RANK + 8, 2 * RANK), f32),
            pltpu.VMEM((4, 4, 2, RANK, 2 * RANK), bf16),
            pltpu.VMEM((4, 8, 128), f32),
            dma((CHUNKS, 13)), dma((CHUNKS, 13)), dma((CHUNKS,)), dma((CHUNKS,)), dma((24,)), dma((24,)),
            dma((CHUNKS + 12,)), dma((13,)), dma((13,)), dma((7,)), dma((7,)),
            dma((12,)), dma((3,)), dma((7,)), dma((8,)), dma((7,)), dma((8,)),
            dma((3,)), dma((4,)), dma((3,)), dma((4,)), dma((3,)), dma((4,)),
        ],
        compiler_params=pltpu.CompilerParams(
            collective_id=0, has_side_effects=True, vmem_limit_bytes=62 * 1024 * 1024
        ),
        name="whole",
    )(*operands)


def on_device(
    pool_inputs, val_inputs, pool_top, val_top, weight, proj_in, proj_out, pool_len, val_len
):
    return whole(
        pool_inputs[0], val_inputs[0], pool_top, val_top, weight[0], proj_in[0].T, proj_out[0].T, pool_len, val_len
    )


def solution(mesh):
    placed = (
        P("layer", "trace", None, None),
        P("layer", "trace", None, None),
        P("trace", None, None),
        P("trace", None, None),
        P("layer", "trace", None),
        P("layer", None, None),
        P("layer", None, None),
        P("trace"),
        P("trace"),
    )
    return jax.shard_map(
        on_device, mesh=mesh, in_specs=placed, out_specs=P("trace", "layer"), check_vma=False
    )
```

```python
import functools

import jax
import jax.numpy as jnp
from jax import lax
from jax.experimental import pallas as pl
from jax.experimental.pallas import tpu as pltpu
from jax.sharding import PartitionSpec as P

MESH = pl.DeviceIdType.MESH
WIDTH = 4096
TOKENS = 128
RANK = 64
CHUNKS = 16
COLS = WIDTH // CHUNKS
PAIRS = CHUNKS // 2
SHARE = 128
MAIN = 320
REST = 192
FIRST = MAIN - 2 * TOKENS
LATE = 2
LAG_FORWARD, LAG_ROW, LAG_ROW_FORWARD, LAG_LAST, LAG_USE = 1, 2, 3, 4, 5
LAG_GRAD = 6
AHEAD = 3
SLICE = 32
PART = 16
FOLD_ONE, FOLD_TWO = 5, 7


def silu_slope(values):
    logistic = jax.nn.sigmoid(values)
    return logistic * (1.0 + values * (1.0 - logistic))


def low_half(shape):
    return lax.broadcasted_iota(jnp.int32, shape, len(shape) - 1) < RANK


def damped_inverses(pair):
    rows = lax.broadcasted_iota(jnp.int32, pair.shape, 0)
    lanes = lax.broadcasted_iota(jnp.int32, pair.shape, 1)
    lower = lanes < RANK
    column = jnp.where(lower, lanes, lanes - RANK)
    diagonal = rows == column
    on_diagonal = jnp.where(diagonal, pair, 0.0)
    trace_first = jnp.sum(jnp.where(lower, on_diagonal, 0.0), keepdims=True)
    trace_second = jnp.sum(jnp.where(lower, 0.0, on_diagonal), keepdims=True)
    damping = jnp.where(lower, trace_first, trace_second) * (0.1 / RANK)
    value = jnp.where(diagonal, pair + damping, pair)
    at = column[0:1]

    def spread(k):
        return jnp.where(
            lower,
            jnp.broadcast_to(value[:, k:k + 1], pair.shape),
            jnp.broadcast_to(value[:, RANK + k:RANK + k + 1], pair.shape),
        )

    for k in range(0, RANK, 2):
        one, two = spread(k), spread(k + 1)
        a, b = one[k:k + 1], two[k:k + 1]
        c, d = one[k + 1:k + 2], two[k + 1:k + 2]
        scale = 1.0 / (a * d - b * c)
        a, b, c, d = a * scale, b * scale, c * scale, d * scale
        upper, under = value[k:k + 1], value[k + 1:k + 2]
        row_one = jnp.where(at == k, d, jnp.where(at == k + 1, -b, d * upper - b * under))
        row_two = jnp.where(at == k, -c, jnp.where(at == k + 1, a, a * under - c * upper))
        one = jnp.where(rows == k, -1.0, jnp.where(rows == k + 1, 0.0, one))
        two = jnp.where(rows == k + 1, -1.0, jnp.where(rows == k, 0.0, two))
        gone = (rows == k) | (rows == k + 1) | (column == k) | (column == k + 1)
        value = jnp.where(gone, 0.0, value) - one * row_one - two * row_two
    return value


def whole_kernel(
    pool_in, val_in, pool_top, val_top, weight, proj_in, proj_out, pool_len, val_len,
    scores_out,
    held, first, second, gated, grad, total, block, wide_in, wide_out, folded,
    low_mid, low_two, low_in, outgoing,
    landed, factors, factors_z, vals, layers,
    send, recv, grad_send, grad_recv, act_send, act_recv, local, fold_send, fold_recv, proj_send, proj_recv,
    low_send, low_recv, fac_send, fac_recv, val_send, val_recv, facz_send, facz_recv, valz_send, valz_recv,
    lay_send, lay_recv,
):
    layer = lax.axis_index("layer")
    trace = lax.axis_index("trace")
    x, z, c = trace // 8, (trace // 2) % 4, trace % 2
    xp, xm, xo = (x + 1) % 4, (x + 3) % 4, (x + 2) % 4
    zp, zm, zo = (z + 1) % 4, (z + 3) % 4, (z + 2) % 4
    other = 1 - c
    highest = lax.Precision.HIGHEST
    f32, bf16 = jnp.float32, jnp.bfloat16

    def at(xi, zi, ci):
        return {"trace": xi * 8 + zi * 2 + ci}

    above = {"layer": (layer + 1) % 4}
    below = {"layer": (layer + 3) % 4}
    sibling = at(x, z, other)

    near = []
    for dx in range(4):
        for dc in range(2):
            if dx or dc:
                xi, ci = (x + dx) % 4, (c + dc) % 2
                near.append((xi * 2 + ci, xi, ci, at(xi, z, ci)))
    across = [((z + dz) % 4, at(x, (z + dz) % 4, c)) for dz in (1, 3, 2)]
    planes = [((layer + dl) % 4, {"layer": (layer + dl) % 4}) for dl in (1, 3, 2)]
    barrier = pltpu.get_barrier_semaphore()
    for device in [n[3] for n in near] + [a[1] for a in across] + [q[1] for q in planes]:
        pl.semaphore_signal(barrier, inc=1, device_id=device, device_id_type=MESH)
    pl.semaphore_wait(barrier, len(near) + len(across) + len(planes))

    def copy(src, dst, send_sem, recv_sem, device):
        return pltpu.make_async_remote_copy(
            src_ref=src, dst_ref=dst, send_sem=send_sem, recv_sem=recv_sem, device_id=device, device_id_type=MESH
        )

    def columns(j):
        return pl.ds(pl.multiple_of(j * COLS, COLS), COLS)

    def transposed(left, right):
        return lax.dot_general(left, right, (((1,), (1,)), ((), ())), preferred_element_type=f32)

    def on(kind):
        return pl.when(layer == kind)

    def own(j):
        return held.at[j, x, z, c]

    def share_out(j, device):
        return copy(weight.at[:, columns(j)], own(j), send.at[j, 12], recv.at[j, 12], device)

    def share_local(j):
        return pltpu.make_async_copy(weight.at[:, columns(j)], own(j), local.at[j])

    def load(src, dst, index):
        return pltpu.make_async_copy(src, dst, local.at[CHUNKS + index])

    def row_loads(pool, val, target, base):
        return [
            load(pool, target.at[0:2 * TOKENS], base),
            load(val.at[0:FIRST], target.at[2 * TOKENS:MAIN], base + 1),
        ]

    def loads(kind):
        return {
            3: lambda: row_loads(pool_in, val_in, first, 0) + row_loads(pool_top, val_top, second, 3),
            2: lambda: row_loads(pool_in, val_in, first, 0),
            1: lambda: [load(val_in.at[FIRST:2 * TOKENS], second.at[0:REST], 0)],
            0: lambda: [load(val_top.at[FIRST:2 * TOKENS], second.at[0:REST], 0)],
        }[kind]()

    def rows_of(base, i):
        return pl.ds(pl.multiple_of(base + i * SLICE, SLICE), SLICE)

    def rest_slice(i, device):
        return copy(
            val_in.at[rows_of(FIRST, i)], first.at[rows_of(0, i)], act_send.at[i], act_recv.at[i], device
        )

    def main_part(source, low, i, base):
        rows = pl.ds(pl.multiple_of(i * PART, PART), PART)
        there = pl.ds(pl.multiple_of(low + i * PART, PART), PART)
        return copy(source.at[rows], second.at[there], act_send.at[base + i], act_recv.at[base + i], above)

    def pool_part(i):
        return main_part(pool_in, 0, i, 0)

    def val_part(i):
        return main_part(val_in, 2 * TOKENS, i, 2 * TOKENS // PART)

    def main_parts():
        return [pool_part(i) for i in range(2 * TOKENS // PART)] + [val_part(i) for i in range(FIRST // PART)]

    def gather_stages(j, view, flip, sems, part):
        send_j, recv_j = sems
        ahead, behind, far = (zp, zm, zo) if flip else (xp, xm, xo)
        up, down, beyond = (xp, xm, xo) if flip else (zp, zm, zo)
        lo, mid, hi = part

        def spot(along, over, ci, rows):
            return view(over, along, ci, *rows) if flip else view(along, over, ci, *rows)

        me_along, me_over = (z, x) if flip else (x, z)

        def to_along(i):
            return at(x, i, c) if flip else at(i, z, c)

        def to_over(i):
            return at(i, z, c) if flip else at(x, i, c)

        full = (lo, hi)
        every = slice(0, 4)

        def push(ref, slot, device):
            copy(ref, ref, send_j(j, slot), recv_j(j, slot), device).start()

        def arrived(ref, slot):
            copy(ref, ref, send_j(j, slot), recv_j(j, slot), sibling).wait_recv()

        def share():
            ref = spot(me_along, me_over, c, full)
            push(ref, 0, to_along(ahead))
            push(ref, 1, to_along(behind))

        def forward_up():
            arrived(spot(behind, me_over, c, full), 0)
            push(spot(behind, me_over, c, (lo, mid)), 2, to_along(ahead))

        def forward_down():
            arrived(spot(ahead, me_over, c, full), 1)
            push(spot(ahead, me_over, c, (mid, hi)), 3, to_along(behind))

        def row():
            arrived(spot(far, me_over, c, (lo, mid)), 2)
            arrived(spot(far, me_over, c, (mid, hi)), 3)
            ref = spot(every, me_over, c, full)
            push(ref, 4, to_over(up))
            push(ref, 5, to_over(down))

        def row_up():
            arrived(spot(every, down, c, full), 4)
            push(spot(slice(0, 2), down, c, full), 6, to_over(up))

        def row_down():
            arrived(spot(every, up, c, full), 5)
            push(spot(slice(2, 4), up, c, full), 7, to_over(down))

        def last():
            arrived(spot(slice(0, 2), beyond, c, full), 6)
            arrived(spot(slice(2, 4), beyond, c, full), 7)

        def over_chip(slot, over):
            return lambda: push(spot(every, over, c, full), slot, sibling)

        def whole():
            for slot, over in ((8, me_over), (9, down), (10, up), (11, beyond)):
                arrived(spot(every, over, other, full), slot)

        def drain():
            def left(ref, slot):
                copy(ref, ref, send_j(j, slot), recv_j(j, slot), sibling).wait_send()

            for slot in (0, 1):
                left(spot(me_along, me_over, c, full), slot)
            left(spot(me_along, me_over, c, (lo, mid)), 2)
            left(spot(me_along, me_over, c, (mid, hi)), 3)
            for slot in (4, 5, 8, 9, 10, 11):
                left(spot(every, me_over, c, full), slot)
            left(spot(slice(0, 2), me_over, c, full), 6)
            left(spot(slice(2, 4), me_over, c, full), 7)

        return (
            [share], [forward_up, forward_down], [row, over_chip(8, me_over)],
            [row_up, row_down, over_chip(9, down), over_chip(10, up)], [last, over_chip(11, beyond)], [whole], [drain],
        )

    def weight_view(j):
        return lambda xi, zi, ci, lo, hi: held.at[j, xi, zi, ci, lo:hi]

    weight_sems = (lambda j, slot: send.at[j, slot], lambda j, slot: recv.at[j, slot])
    fold_sems = (lambda j, slot: fold_send.at[slot], lambda j, slot: fold_recv.at[slot])

    def weight_stages(p):
        a, b = 2 * p, 2 * p + 1
        part = (0, SHARE // 2, SHARE)
        return zip(
            gather_stages(a, weight_view(a), False, weight_sems, part),
            gather_stages(b, weight_view(b), True, weight_sems, part),
        )

    def run_stage(index):
        def stage(p):
            for parts in zip(*list(weight_stages(p))[index]):
                for part in parts:
                    part()
        return stage

    def fold_view(xi, zi, ci, lo, hi):
        return folded.at[xi, zi, ci, lo:hi]

    fold_stages = gather_stages(0, fold_view, False, fold_sems, (RANK, RANK + RANK // 2, 2 * RANK))

    def have_share(p):
        for j in (2 * p, 2 * p + 1):
            @pl.when(layer >= 2)
            def _():
                share_local(j).wait()

            @pl.when(layer < 2)
            def _():
                copy(own(j), own(j), send.at[j, 12], recv.at[j, 12], sibling).wait_recv()

    def half_of(which, index, low, ci):
        return which.at[index, low:low + RANK, pl.ds(pl.multiple_of(ci * (WIDTH // 2), WIDTH // 2), WIDTH // 2)]

    def proj_copy(index, low, slot, device):
        ref = half_of(wide_out, index, low, c)
        return copy(ref, ref, proj_send.at[slot], proj_recv.at[slot], device)

    def proj_out_copies(kind):
        if kind == 2:
            return [proj_copy(1, 0, 3, {"layer": 1})]
        if kind == 1:
            return [proj_copy(0, 0, 0, {"layer": 2})]
        if kind == 0:
            return [proj_copy(0, RANK, 1, {"layer": 1}), proj_copy(0, RANK, 2, {"layer": 2})]
        return []

    def proj_in_copies(kind):
        if kind == 2:
            return [proj_copy(0, 0, 0, above), proj_copy(0, RANK, 2, above)]
        if kind == 1:
            return [proj_copy(0, RANK, 1, above), proj_copy(1, 0, 3, above)]
        return []

    def proj_chip_copies(kind):
        if kind == 2:
            return [proj_copy(0, 0, 4, sibling), proj_copy(0, RANK, 5, sibling)]
        if kind == 1:
            return [proj_copy(0, RANK, 5, sibling), proj_copy(1, 0, 6, sibling)]
        return []

    def proj_chip_arrived(kind):
        for index, low, slot in {2: ((0, 0, 4), (0, RANK, 5)), 1: ((0, RANK, 5), (1, 0, 6))}[kind]:
            ref = half_of(wide_out, index, low, other)
            copy(ref, ref, proj_send.at[slot], proj_recv.at[slot], sibling).wait_recv()

    def proj_loads(kind):
        places = {
            3: [(1, 0), (1, RANK)], 2: [(1, 0), (1, RANK)], 1: [(0, 0)], 0: [(0, RANK)],
        }[kind]
        return [
            load(proj_out, wide_out.at[index, low:low + RANK], 8 + i) for i, (index, low) in enumerate(places)
        ]

    def proj_in_loads():
        return [load(proj_in, wide_in.at[i * RANK:(i + 1) * RANK], 10 + i) for i in range(2)]

    def block_source(index):
        half = slice(index % 2 * TOKENS, (index % 2 + 1) * TOKENS)
        return (pool_in, val_in, pool_top, val_top)[index // 2].at[half]

    def block_load(source):
        return load(source, block, 7)

    @pl.when(layer >= 2)
    def _():
        def body(j, carry):
            share_local(j).start()
            return carry
        lax.fori_loop(0, CHUNKS, body, 0)

    def share_pair(p):
        for kind, partner in ((3, above), (2, below)):
            @on(kind)
            def _():
                share_out(2 * p, partner).start()
                share_out(2 * p + 1, partner).start()

    for pair in range(AHEAD):
        share_pair(pair)
    for kind in range(4):
        @on(kind)
        def _():
            for item in proj_loads(kind) + loads(kind):
                item.start()
    for item in proj_in_loads():
        item.start()
    block_load(block_source(0)).start()

    def gate_rows(index):
        base = pl.multiple_of(index * 32, 32)
        value = first[pl.ds(base, 32), :].astype(f32)
        top = second[pl.ds(base, 32), :].astype(f32)
        gated[pl.ds(base, 32), :] = (top * silu_slope(value)).astype(bf16)

    def gate_some(start, count):
        def body(i, carry):
            gate_rows(start + i)
            return carry
        lax.fori_loop(0, count, body, 0)

    def grad_copy(j, rows, device):
        return copy(grad.at[j, 0:rows], grad.at[j, 0:rows], grad_send.at[j], grad_recv.at[j], device)

    def upper_chunk(j, rows, device):
        total[0, 0:rows] = second[0:rows, columns(j)].astype(f32)

        def body(xi, carry):
            piece = held[j, xi].reshape(WIDTH // 4, COLS)
            left = gated[0:rows, pl.ds(pl.multiple_of(xi * (WIDTH // 4), WIDTH // 4), WIDTH // 4)]
            total[0, 0:rows] += jnp.dot(left, piece, preferred_element_type=f32)
            return carry
        lax.fori_loop(0, 4, body, 0)
        grad[j, 0:rows] = total[0, 0:rows].astype(bf16)
        grad_copy(j, rows, device).start()

    def add_product(n, q, rows):
        piece = held[n, q // 2, pl.ds(2 * (q % 2), 2)].reshape(4 * SHARE, COLS)
        left = gated[0:rows, pl.ds(pl.multiple_of(q * 2 * COLS, 2 * COLS), 2 * COLS)]
        total[n, 0:rows] += jnp.dot(left, piece, preferred_element_type=f32)

    def lower_weight(n, ready, rows):
        total[n, 0:rows] = jnp.zeros((rows, COLS), f32)
        total[n + 1, 0:rows] = jnp.zeros((rows, COLS), f32)

        def body(q, carry):
            add_product(n, q, rows)
            add_product(n + 1, q, rows)
            return carry
        lax.fori_loop(0, ready, body, 0)

    def lower_gate(q, rows):
        for k in (2 * q, 2 * q + 1):
            grad_copy(k, rows, above).wait_recv()

            def gating(i, carry):
                base = pl.multiple_of(i * 64, 64)
                value = first[pl.ds(base, 64), columns(k)].astype(f32)
                up = grad[k, pl.ds(base, 64)].astype(f32)
                gated[pl.ds(base, 64), columns(k)] = (up * silu_slope(value)).astype(bf16)
                return carry
            lax.fori_loop(0, rows // 64, gating, 0)
            low_two[0:rows] += transposed(grad[k, 0:rows], wide_out[1, :, columns(k)])

    def lower_grad(q, ready, rows):
        lower_gate(q, rows)

        def body(n, carry):
            add_product(2 * n, q, rows)
            add_product(2 * n + 1, q, rows)
            return carry
        lax.fori_loop(0, ready // 2, body, 0)

    def when_in(t, lag, what):
        @pl.when((t >= lag) & (t < PAIRS + lag))
        def _():
            what(t - lag)

    def early(t):
        @pl.when(t == 0)
        def _():
            for kind in range(4):
                @on(kind)
                def _():
                    for item in proj_loads(kind):
                        item.wait()
                    for item in proj_out_copies(kind):
                        item.start()
            folded[:, :, :, 0:RANK] = jnp.zeros((4, 4, 2, RANK, 2 * RANK), bf16)
            low_two[...] = jnp.zeros((MAIN, 2 * RANK), f32)

        @pl.when(t == 1)
        def _():
            for item in proj_in_loads():
                item.wait()
            for kind in range(4):
                @on(kind)
                def _():
                    for item in loads(kind):
                        item.wait()

        for index in range(4):
            turn_of = 1 + index + jnp.where((layer == 1) & (index > 1), 2, 0)

            @pl.when(t == turn_of)
            def _():
                block_load(block_source(index)).wait()
                low_in[index] = transposed(block[...], wide_in[...])
                if index == 1:
                    @on(1)
                    def _():
                        block_load(weight).start()

                    @pl.when(layer != 1)
                    def _():
                        block_load(block_source(2)).start()
                elif index < 3:
                    block_load(block_source(index + 1)).start()
                else:
                    @on(3)
                    def _():
                        block_load(block_source(4)).start()
        for index in range(4, 8):
            @pl.when((t == 1 + index) & (layer == 3))
            def _():
                block_load(block_source(index)).wait()
                low_mid[pl.ds((index - 4) * TOKENS, TOKENS)] = transposed(block[...], wide_out[1])
                if index < 7:
                    block_load(block_source(index + 1)).start()

        @pl.when((t >= 1) & (t < 5) & (layer == 3))
        def _():
            gate_some(3 * (t - 1), jnp.minimum(3, MAIN // 32 - 3 * (t - 1)))

        for kind, when in ((2, 9), (1, 3)):
            @pl.when((t == when) & (layer == kind))
            def _():
                for item in proj_in_copies(kind):
                    item.wait_recv()
                for item in proj_chip_copies(kind):
                    item.start()

            @pl.when((t == when + 1) & (layer == kind))
            def _():
                proj_chip_arrived(kind)
                if kind == 1:
                    wide_out[1, RANK:2 * RANK] = wide_out[1, 0:RANK]

        @pl.when((t == 4) & (layer == 1))
        def _():
            block_load(weight).wait()
            folded[x, z, c, RANK:2 * RANK] = transposed(wide_out[0, RANK:2 * RANK], block[...]).astype(bf16)
            mine = folded.at[x, z, c, RANK:2 * RANK]
            copy(mine, mine, fold_send.at[12], fold_recv.at[12], above).start()
            block_load(block_source(2)).start()

        for index, stage in enumerate(fold_stages[:6]):
            lag = jnp.where(layer == 1, FOLD_ONE, FOLD_TWO)

            @pl.when((t == lag + index) & ((layer == 1) | (layer == 2)))
            def _():
                if index == 0:
                    @on(2)
                    def _():
                        mine = folded.at[x, z, c, RANK:2 * RANK]
                        copy(mine, mine, fold_send.at[12], fold_recv.at[12], above).wait_recv()
                for part in stage:
                    part()

    def step(t, carry):
        @pl.when(t + AHEAD < PAIRS)
        def _():
            share_pair(t + AHEAD)
        for kind, partner in ((3, above), (2, below)):
            @pl.when((t >= 1) & (t <= REST // SLICE) & (layer == kind))
            def _():
                rest_slice(t - 1, partner).start()

        @pl.when((t >= 1) & (t < 9) & (layer == 1))
        def _():
            pool_part(2 * (t - 1)).start()
            pool_part(2 * (t - 1) + 1).start()

            @pl.when(t % 2 == 1)
            def _():
                val_part((t - 1) // 2).start()

        when_in(t, 0, have_share)
        for lag, index in ((0, 0), (LAG_FORWARD, 1), (LAG_ROW, 2), (LAG_ROW_FORWARD, 3), (LAG_LAST, 4)):
            when_in(t, lag, run_stage(index))
        early(t)
        when_in(t, LAG_USE, run_stage(5))

        @pl.when((t == LAG_USE + LATE) & (layer < 2))
        def _():
            for i in range(REST // SLICE):
                rest_slice(i, above).wait_recv()

            @on(0)
            def _():
                gate_some(0, REST // 32)

                def body(j, inner_carry):
                    upper_chunk(j, REST, above)
                    return inner_carry
                lax.fori_loop(0, 2 * LATE, body, 0)

        for kind, rows, target, begin in ((3, MAIN, below, LAG_USE), (0, REST, above, LAG_USE + LATE)):
            @pl.when((layer == kind) & (t >= begin) & (t < PAIRS + LAG_USE))
            def _():
                upper_chunk(2 * (t - LAG_USE), rows, target)
                upper_chunk(2 * (t - LAG_USE) + 1, rows, target)

        whole = jnp.minimum(2 * (t - LAG_USE) + 2, CHUNKS)
        begin_rest = LAG_GRAD + LATE
        ready_rest = jnp.where(t <= begin_rest, 0, jnp.where(t < begin_rest + LATE, 2 * (t - begin_rest), t - LAG_GRAD))
        for kind, rows, ready in ((2, MAIN, jnp.maximum(t - LAG_GRAD, 0)), (1, REST, ready_rest)):
            @pl.when((layer == kind) & (t >= LAG_USE) & (t < PAIRS + LAG_USE))
            def _():
                lower_weight(2 * (t - LAG_USE), ready, rows)

        @pl.when((layer == 2) & (t >= LAG_GRAD) & (t < PAIRS + LAG_GRAD - 1))
        def _():
            lower_grad(t - LAG_GRAD, whole, MAIN)

        @pl.when((layer == 1) & (t >= begin_rest) & (t < begin_rest + LATE))
        def _():
            lower_grad(2 * (t - begin_rest), whole, REST)
            lower_grad(2 * (t - begin_rest) + 1, whole, REST)

        @pl.when((layer == 1) & (t >= begin_rest + LATE) & (t < PAIRS + LAG_GRAD - 1))
        def _():
            lower_grad(t - LAG_GRAD, whole, REST)
        return carry

    lax.fori_loop(0, PAIRS + LAG_GRAD - 1, step, 0)

    def drain(p, carry):
        run_stage(6)(p)

        @pl.when(layer >= 2)
        def _():
            share_out(2 * p, above).wait_send()
            share_out(2 * p + 1, above).wait_send()
        for kind, rows in ((3, MAIN), (0, REST)):
            @on(kind)
            def _():
                grad_copy(2 * p, rows, above).wait_send()
                grad_copy(2 * p + 1, rows, above).wait_send()
        return carry
    lax.fori_loop(0, PAIRS, drain, 0)

    @pl.when(layer >= 2)
    def _():
        for i in range(REST // SLICE):
            rest_slice(i, above).wait_send()

    @on(1)
    def _():
        for item in main_parts():
            item.wait_send()
        mine = folded.at[x, z, c, RANK:2 * RANK]
        copy(mine, mine, fold_send.at[12], fold_recv.at[12], above).wait_send()

    @pl.when((layer == 1) | (layer == 2))
    def _():
        fold_stages[6][0]()
    for kind in (2, 1, 0):
        @on(kind)
        def _():
            for item in proj_out_copies(kind) + proj_chip_copies(kind):
                item.wait_send()

    def finish(kind, rows):
        if kind == 2:
            for item in main_parts():
                item.wait_recv()
        lower_gate(PAIRS - 1, rows)
        low_mid[0:rows] = jnp.zeros((rows, 2 * RANK), f32)

        def body(i, carry):
            for n in (2 * i, 2 * i + 1):
                add_product(n, PAIRS - 1, rows)
                for base in range(0, rows, 64):
                    part = slice(base, base + 64)
                    up = grad[n, part].astype(f32)
                    value = second[part, columns(n)].astype(f32)
                    low = (up + total[n, part]).astype(bf16)
                    first[part, columns(n)] = low
                    grad[n, part] = (low.astype(f32) * silu_slope(value)).astype(bf16)
                fold = folded[n // 4, n % 4]
                left = jnp.concatenate([first[0:rows, columns(n)], grad[n, 0:rows]], 1)
                right = jnp.concatenate([wide_out[0, :, columns(n)], fold[0], fold[1]], 1)
                low_mid[0:rows] += transposed(left, right)
            return carry
        lax.fori_loop(0, PAIRS, body, 0)

    wide = (RANK, 2 * RANK)
    lower = low_half(wide)
    lower_rows = low_half((TOKENS, 2 * RANK))

    tokens = lax.broadcasted_iota(jnp.int32, (TOKENS, 2 * RANK), 0)
    valid = [
        (tokens < jnp.where(lower_rows, lens[0], lens[1])).astype(f32) for lens in (pool_len, val_len)
    ]

    def swap(value):
        return pltpu.roll(value, RANK, 1)

    def put(index, slot, value, mask):
        outgoing[index, slot] = (value * valid[mask]).astype(bf16)

    @on(3)
    def _():
        rows = [low_mid[i * TOKENS:(i + 1) * TOKENS] for i in range(4)]
        landed[0] = (jnp.where(lower_rows, rows[0], rows[1]) * valid[0]).astype(bf16)
        landed[1] = (jnp.where(lower_rows, rows[2], rows[3]) * valid[1]).astype(bf16)
        landed[2] = jnp.zeros_like(landed[2])

    @on(2)
    def _():
        finish(2, MAIN)
        def short(ref):
            return jnp.concatenate([ref[2 * TOKENS:MAIN], jnp.zeros((TOKENS - FIRST, 2 * RANK), f32)], 0)

        mid = [low_mid[0:TOKENS], low_mid[TOKENS:2 * TOKENS], short(low_mid)]
        two = [low_two[0:TOKENS], low_two[TOKENS:2 * TOKENS], short(low_two)]
        put(1, 0, jnp.where(lower_rows, mid[0], swap(mid[1])), 0)
        put(1, 1, jnp.where(lower_rows, mid[2], 0.0), 1)
        put(0, 0, jnp.where(lower_rows, swap(mid[0]), mid[1]), 0)
        put(0, 1, jnp.where(lower_rows, swap(mid[2]), 0.0), 1)
        landed[0] = (jnp.where(lower_rows, two[0], two[1]) * valid[0]).astype(bf16)
        landed[1] = (jnp.where(lower_rows, two[2], 0.0) * valid[1]).astype(bf16)

    @on(1)
    def _():
        finish(1, REST)
        def split(ref):
            other_tokens = REST - TOKENS
            return (
                jnp.concatenate([jnp.zeros((TOKENS - other_tokens, 2 * RANK), f32), ref[0:other_tokens]], 0),
                ref[other_tokens:REST],
            )

        one, two = split(low_mid), split(low_two)
        put(0, 1, jnp.where(lower_rows, swap(one[0]), one[1]), 1)
        put(2, 1, jnp.where(lower_rows, two[0], two[1]), 1)
        landed[2] = (jnp.where(lower_rows, one[0], swap(one[1])) * valid[1]).astype(bf16)

    def low(source, slot, plane):
        return copy(source, landed.at[slot], low_send.at[slot + 3 * plane], low_recv.at[slot], {"layer": plane})

    def lows(kind):
        if kind == 2:
            return [low(outgoing.at[1, 0], 0, 1), low(outgoing.at[1, 1], 1, 1),
                    low(outgoing.at[0, 0], 0, 0), low(outgoing.at[0, 1], 1, 0)]
        if kind == 1:
            return [low(outgoing.at[0, 1], 2, 0), low(outgoing.at[2, 1], 2, 2)]
        return []

    def lows_in(kind):
        return [low(landed.at[slot], slot, (kind + 1) % 4) for slot in {3: (), 2: (2,), 1: (0, 1), 0: (0, 1, 2)}[kind]]

    for kind in (2, 1):
        @pl.when(layer == kind)
        def _():
            for item in lows(kind):
                item.start()

    for kind in (2, 1, 0):
        @pl.when(layer == kind)
        def _():
            for item in lows_in(kind):
                item.wait_recv()

    def across_tokens(left, right):
        return lax.dot_general(left, right, (((0,), (0,)), ((), ())), precision=highest, preferred_element_type=f32)

    def blocks(value):
        return jnp.where(lower, value[0:RANK], value[RANK:2 * RANK])

    def both(value):
        return value + swap(value)

    pool_low = jnp.where(lower_rows, low_in[0], low_in[1]) * valid[0]
    val_low = jnp.where(lower_rows, low_in[2], low_in[3]) * valid[1]
    pool_out = landed[0].astype(f32)
    val_out = landed[1].astype(f32) + landed[2].astype(f32)
    vals[x, z, c] = blocks(across_tokens(val_out, val_low)).astype(bf16)
    part_in = both(blocks(across_tokens(pool_low, pool_low)))
    part_out = both(blocks(across_tokens(pool_out, pool_out)))
    factors[x * 2 + c, 0:RANK] = jnp.where(lower, part_in, part_out)
    factors[x * 2 + c, RANK:RANK + 8] = jnp.full((8, 2 * RANK), (pool_len[0] + pool_len[1]).astype(f32))

    mine = x * 2 + c
    sent_one = [copy(factors.at[mine], factors.at[mine], fac_send.at[i], fac_recv.at[mine], n[3]) for i, n in enumerate(near)]
    sent_one += [copy(vals.at[x, z, c], vals.at[x, z, c], val_send.at[i], val_recv.at[mine], n[3]) for i, n in enumerate(near)]
    for item in sent_one:
        item.start()
    pool_grads = blocks(across_tokens(pool_low, pool_out))
    for slot, xi, ci, device in near:
        copy(factors.at[slot], factors.at[slot], fac_send.at[0], fac_recv.at[slot], device).wait_recv()
    factors_z[z] = sum(factors[i] for i in range(1, 8)) + factors[0]
    sent_two = [copy(factors_z.at[z], factors_z.at[z], facz_send.at[i], facz_recv.at[z], a[1]) for i, a in enumerate(across)]
    for item in sent_two:
        item.start()
    for slot, xi, ci, device in near:
        copy(vals.at[xi, z, ci], vals.at[xi, z, ci], val_send.at[0], val_recv.at[slot], device).wait_recv()
    sent_three = [copy(vals.at[:, z], vals.at[:, z], valz_send.at[i], valz_recv.at[z], a[1]) for i, a in enumerate(across)]
    for item in sent_three:
        item.start()
    for zi, device in across:
        copy(factors_z.at[zi], factors_z.at[zi], facz_send.at[0], facz_recv.at[zi], device).wait_recv()
    factor_sum = factors_z[0] + factors_z[1] + factors_z[2] + factors_z[3]
    inverse = damped_inverses(factor_sum[0:RANK] / factor_sum[RANK:RANK + 1])
    inv_in = inverse[:, 0:RANK]
    turned = swap(inverse)
    twice = jnp.where(lower, turned, inverse)
    inv_out = jnp.concatenate([jnp.where(lower, twice, 0.0), jnp.where(lower, 0.0, twice)], 0)
    scaled = jnp.dot(inv_in, pool_grads, precision=highest, preferred_element_type=f32)
    scaled = jnp.dot(scaled, inv_out, precision=highest, preferred_element_type=f32)
    coarse = scaled.astype(bf16)
    fine = (scaled - coarse.astype(f32)).astype(bf16)
    empty = jnp.zeros(wide, bf16)

    def spread(value):
        return jnp.concatenate(
            [jnp.concatenate([value, empty], 1), jnp.concatenate([empty, value], 1)], 0
        )

    coarse, fine = spread(coarse), spread(fine)
    for zi, device in across:
        copy(vals.at[:, zi], vals.at[:, zi], valz_send.at[0], valz_recv.at[zi], device).wait_recv()
    every = vals[...].reshape(32 * RANK, 2 * RANK)
    product = jnp.dot(every, coarse, preferred_element_type=f32) + jnp.dot(every, fine, preferred_element_type=f32)
    at_row = lax.broadcasted_iota(jnp.int32, product.shape, 0) % RANK
    at_lane = lax.broadcasted_iota(jnp.int32, product.shape, 1) % RANK
    summed = jnp.where(at_row == at_lane, product, 0.0).reshape(32, RANK, 4 * RANK).sum(1)
    group = lax.broadcasted_iota(jnp.int32, (8, 4 * RANK), 1) // RANK
    picks = (lax.broadcasted_iota(jnp.int32, (8, 4 * RANK), 0) == group).astype(f32)
    part = lax.dot_general(picks, summed, (((1,), (1,)), ((), ())), precision=highest, preferred_element_type=f32)
    layers[layer] = jnp.concatenate([part, jnp.zeros((8, 96), f32)], 1)
    sent_last = [copy(layers.at[layer], layers.at[layer], lay_send.at[i], lay_recv.at[layer], q[1]) for i, q in enumerate(planes)]
    for item in sent_last:
        item.start()
    for plane, device in planes:
        copy(layers.at[plane], layers.at[plane], lay_send.at[0], lay_recv.at[plane], device).wait_recv()
    table = (layers[0] + layers[1] + layers[2] + layers[3]) * (1.0 / (RANK * TOKENS))
    lane = lax.broadcasted_iota(jnp.int32, (128, 16), 0)
    spot_of = lax.broadcasted_iota(jnp.int32, (128, 16), 1) + 16 * layer

    def placed(index):
        return jnp.dot(
            table, (2 * lane + index == spot_of).astype(f32), precision=highest, preferred_element_type=f32
        )

    scores_out[...] = placed(0)[0:2] + placed(1)[2:4]

    for item in sent_one + sent_two + sent_three + sent_last:
        item.wait_send()
    for kind in (2, 1):
        @pl.when(layer == kind)
        def _():
            for item in lows(kind):
                item.wait_send()


def whole(*operands):
    anywhere = pl.BlockSpec(memory_space=pl.ANY)
    inside = pl.BlockSpec(memory_space=pltpu.VMEM)
    dma = pltpu.SemaphoreType.DMA
    bf16, f32 = jnp.bfloat16, jnp.float32
    return pl.pallas_call(
        whole_kernel,
        out_shape=jax.ShapeDtypeStruct((2, 16), f32),
        in_specs=[anywhere] * 7 + [pl.BlockSpec(memory_space=pltpu.SMEM)] * 2,
        out_specs=inside,
        scratch_shapes=[
            pltpu.VMEM((CHUNKS, 4, 4, 2, SHARE, COLS), bf16),
            pltpu.VMEM((MAIN, WIDTH), bf16),
            pltpu.VMEM((MAIN, WIDTH), bf16),
            pltpu.VMEM((MAIN, WIDTH), bf16),
            pltpu.VMEM((CHUNKS, MAIN, COLS), bf16),
            pltpu.VMEM((CHUNKS, MAIN, COLS), f32),
            pltpu.VMEM((TOKENS, WIDTH), bf16),
            pltpu.VMEM((2 * RANK, WIDTH), bf16),
            pltpu.VMEM((2, 2 * RANK, WIDTH), bf16),
            pltpu.VMEM((4, 4, 2, 2 * RANK, SHARE), bf16),
            pltpu.VMEM((4 * TOKENS, 2 * RANK), f32),
            pltpu.VMEM((MAIN, 2 * RANK), f32),
            pltpu.VMEM((4, TOKENS, 2 * RANK), f32),
            pltpu.VMEM((3, 2, TOKENS, 2 * RANK), bf16),
            pltpu.VMEM((3, TOKENS, 2 * RANK), bf16),
            pltpu.VMEM((8, RANK + 8, 2 * RANK), f32),
            pltpu.VMEM((4, RANK + 8, 2 * RANK), f32),
            pltpu.VMEM((4, 4, 2, RANK, 2 * RANK), bf16),
            pltpu.VMEM((4, 8, 128), f32),
            dma((CHUNKS, 13)), dma((CHUNKS, 13)), dma((CHUNKS,)), dma((CHUNKS,)), dma((24,)), dma((24,)),
            dma((CHUNKS + 12,)), dma((13,)), dma((13,)), dma((7,)), dma((7,)),
            dma((12,)), dma((3,)), dma((7,)), dma((8,)), dma((7,)), dma((8,)),
            dma((3,)), dma((4,)), dma((3,)), dma((4,)), dma((3,)), dma((4,)),
        ],
        compiler_params=pltpu.CompilerParams(
            collective_id=0, has_side_effects=True, vmem_limit_bytes=62 * 1024 * 1024
        ),
        name="whole",
    )(*operands)


def on_device(
    pool_inputs, val_inputs, pool_top, val_top, weight, proj_in, proj_out, pool_len, val_len
):
    return whole(
        *(rows.reshape(-1, WIDTH) for rows in (pool_inputs[0], val_inputs[0], pool_top, val_top)), weight[0], proj_in[0].T, proj_out[0].T, pool_len, val_len
    )


def solution(mesh):
    placed = (
        P("layer", "trace", None, None),
        P("layer", "trace", None, None),
        P("trace", None, None),
        P("trace", None, None),
        P("layer", "trace", None),
        P("layer", None, None),
        P("layer", None, None),
        P("trace"),
        P("trace"),
    )
    return jax.shard_map(
        on_device, mesh=mesh, in_specs=placed, out_specs=P("trace", "layer"), check_vma=False
    )
```

```python
import functools

import jax
import jax.numpy as jnp
from jax import lax
from jax.experimental import pallas as pl
from jax.experimental.pallas import tpu as pltpu
from jax.sharding import PartitionSpec as P

MESH = pl.DeviceIdType.MESH
WIDTH = 4096
TOKENS = 128
RANK = 64
CHUNKS = 16
COLS = WIDTH // CHUNKS
PAIRS = CHUNKS // 2
SHARE = 128
MAIN = 320
REST = 192
FIRST = MAIN - 2 * TOKENS
LATE = 2
LAG_FORWARD, LAG_ROW, LAG_ROW_FORWARD, LAG_LAST, LAG_USE = 1, 2, 3, 4, 5
LAG_GRAD = 6
AHEAD = 3
SLICE = 32
PART = 16
FOLD_ONE, FOLD_TWO = 5, 7


def silu_slope(values):
    logistic = jax.nn.sigmoid(values)
    return logistic * (1.0 + values * (1.0 - logistic))


def low_half(shape):
    return lax.broadcasted_iota(jnp.int32, shape, len(shape) - 1) < RANK


def damped_inverses(pair):
    rows = lax.broadcasted_iota(jnp.int32, pair.shape, 0)
    lanes = lax.broadcasted_iota(jnp.int32, pair.shape, 1)
    lower = lanes < RANK
    column = jnp.where(lower, lanes, lanes - RANK)
    diagonal = rows == column
    on_diagonal = jnp.where(diagonal, pair, 0.0)
    trace_first = jnp.sum(jnp.where(lower, on_diagonal, 0.0), keepdims=True)
    trace_second = jnp.sum(jnp.where(lower, 0.0, on_diagonal), keepdims=True)
    scale_back = RANK / jnp.where(lower, trace_first, trace_second)
    value = jnp.where(diagonal, pair * scale_back + 0.1, pair * scale_back)
    at = column[0:1]

    def spread(k):
        return jnp.where(
            lower,
            jnp.broadcast_to(value[:, k:k + 1], pair.shape),
            jnp.broadcast_to(value[:, RANK + k:RANK + k + 1], pair.shape),
        )

    for k in range(0, RANK, 2):
        one, two = spread(k), spread(k + 1)
        a, b = one[k:k + 1], two[k:k + 1]
        c, d = one[k + 1:k + 2], two[k + 1:k + 2]
        scale = 1.0 / (a * d - b * c)
        a, b, c, d = a * scale, b * scale, c * scale, d * scale
        upper, under = value[k:k + 1], value[k + 1:k + 2]
        row_one = jnp.where(at == k, d, jnp.where(at == k + 1, -b, d * upper - b * under))
        row_two = jnp.where(at == k, -c, jnp.where(at == k + 1, a, a * under - c * upper))
        one = jnp.where(rows == k, -1.0, jnp.where(rows == k + 1, 0.0, one))
        two = jnp.where(rows == k + 1, -1.0, jnp.where(rows == k, 0.0, two))
        gone = (rows == k) | (rows == k + 1) | (column == k) | (column == k + 1)
        value = jnp.where(gone, 0.0, value) - one * row_one - two * row_two
    return value * scale_back


def whole_kernel(
    pool_in, val_in, pool_top, val_top, weight, proj_in, proj_out, pool_len, val_len,
    scores_out,
    held, first, second, gated, grad, total, block, wide_in, wide_out, folded,
    low_mid, low_two, low_in, outgoing,
    landed, factors, factors_z, vals, layers,
    send, recv, grad_send, grad_recv, act_send, act_recv, local, fold_send, fold_recv, proj_send, proj_recv,
    low_send, low_recv, fac_send, fac_recv, val_send, val_recv, facz_send, facz_recv, valz_send, valz_recv,
    lay_send, lay_recv,
):
    layer = lax.axis_index("layer")
    trace = lax.axis_index("trace")
    x, z, c = trace // 8, (trace // 2) % 4, trace % 2
    xp, xm, xo = (x + 1) % 4, (x + 3) % 4, (x + 2) % 4
    zp, zm, zo = (z + 1) % 4, (z + 3) % 4, (z + 2) % 4
    other = 1 - c
    highest = lax.Precision.HIGHEST
    f32, bf16 = jnp.float32, jnp.bfloat16

    def at(xi, zi, ci):
        return {"trace": xi * 8 + zi * 2 + ci}

    above = {"layer": (layer + 1) % 4}
    below = {"layer": (layer + 3) % 4}
    sibling = at(x, z, other)

    near = []
    for dx in range(4):
        for dc in range(2):
            if dx or dc:
                xi, ci = (x + dx) % 4, (c + dc) % 2
                near.append((xi * 2 + ci, xi, ci, at(xi, z, ci)))
    across = [((z + dz) % 4, at(x, (z + dz) % 4, c)) for dz in (1, 3, 2)]
    planes = [((layer + dl) % 4, {"layer": (layer + dl) % 4}) for dl in (1, 3, 2)]
    barrier = pltpu.get_barrier_semaphore()
    for device in [n[3] for n in near] + [a[1] for a in across] + [q[1] for q in planes]:
        pl.semaphore_signal(barrier, inc=1, device_id=device, device_id_type=MESH)
    pl.semaphore_wait(barrier, len(near) + len(across) + len(planes))

    def copy(src, dst, send_sem, recv_sem, device):
        return pltpu.make_async_remote_copy(
            src_ref=src, dst_ref=dst, send_sem=send_sem, recv_sem=recv_sem, device_id=device, device_id_type=MESH
        )

    def columns(j):
        return pl.ds(pl.multiple_of(j * COLS, COLS), COLS)

    def transposed(left, right):
        return lax.dot_general(left, right, (((1,), (1,)), ((), ())), preferred_element_type=f32)

    def on(kind):
        return pl.when(layer == kind)

    def own(j):
        return held.at[j, x, z, c]

    def share_out(j, device):
        return copy(weight.at[:, columns(j)], own(j), send.at[j, 12], recv.at[j, 12], device)

    def share_local(j):
        return pltpu.make_async_copy(weight.at[:, columns(j)], own(j), local.at[j])

    def load(src, dst, index):
        return pltpu.make_async_copy(src, dst, local.at[CHUNKS + index])

    def row_loads(pool, val, target, base):
        return [
            load(pool, target.at[0:2 * TOKENS], base),
            load(val.at[0:FIRST], target.at[2 * TOKENS:MAIN], base + 1),
        ]

    def loads(kind):
        return {
            3: lambda: row_loads(pool_in, val_in, first, 0) + row_loads(pool_top, val_top, second, 3),
            2: lambda: row_loads(pool_in, val_in, first, 0),
            1: lambda: [load(val_in.at[FIRST:2 * TOKENS], second.at[0:REST], 0)],
            0: lambda: [load(val_top.at[FIRST:2 * TOKENS], second.at[0:REST], 0)],
        }[kind]()

    def rows_of(base, i):
        return pl.ds(pl.multiple_of(base + i * SLICE, SLICE), SLICE)

    def rest_slice(i, device):
        return copy(
            val_in.at[rows_of(FIRST, i)], first.at[rows_of(0, i)], act_send.at[i], act_recv.at[i], device
        )

    def main_part(source, low, i, base):
        rows = pl.ds(pl.multiple_of(i * PART, PART), PART)
        there = pl.ds(pl.multiple_of(low + i * PART, PART), PART)
        return copy(source.at[rows], second.at[there], act_send.at[base + i], act_recv.at[base + i], above)

    def pool_part(i):
        return main_part(pool_in, 0, i, 0)

    def val_part(i):
        return main_part(val_in, 2 * TOKENS, i, 2 * TOKENS // PART)

    def main_parts():
        return [pool_part(i) for i in range(2 * TOKENS // PART)] + [val_part(i) for i in range(FIRST // PART)]

    def gather_stages(j, view, flip, sems, part):
        send_j, recv_j = sems
        ahead, behind, far = (zp, zm, zo) if flip else (xp, xm, xo)
        up, down, beyond = (xp, xm, xo) if flip else (zp, zm, zo)
        lo, mid, hi = part

        def spot(along, over, ci, rows):
            return view(over, along, ci, *rows) if flip else view(along, over, ci, *rows)

        me_along, me_over = (z, x) if flip else (x, z)

        def to_along(i):
            return at(x, i, c) if flip else at(i, z, c)

        def to_over(i):
            return at(i, z, c) if flip else at(x, i, c)

        full = (lo, hi)
        every = slice(0, 4)

        def push(ref, slot, device):
            copy(ref, ref, send_j(j, slot), recv_j(j, slot), device).start()

        def arrived(ref, slot):
            copy(ref, ref, send_j(j, slot), recv_j(j, slot), sibling).wait_recv()

        def share():
            ref = spot(me_along, me_over, c, full)
            push(ref, 0, to_along(ahead))
            push(ref, 1, to_along(behind))

        def forward_up():
            arrived(spot(behind, me_over, c, full), 0)
            push(spot(behind, me_over, c, (lo, mid)), 2, to_along(ahead))

        def forward_down():
            arrived(spot(ahead, me_over, c, full), 1)
            push(spot(ahead, me_over, c, (mid, hi)), 3, to_along(behind))

        def row():
            arrived(spot(far, me_over, c, (lo, mid)), 2)
            arrived(spot(far, me_over, c, (mid, hi)), 3)
            ref = spot(every, me_over, c, full)
            push(ref, 4, to_over(up))
            push(ref, 5, to_over(down))

        def row_up():
            arrived(spot(every, down, c, full), 4)
            push(spot(slice(0, 2), down, c, full), 6, to_over(up))

        def row_down():
            arrived(spot(every, up, c, full), 5)
            push(spot(slice(2, 4), up, c, full), 7, to_over(down))

        def last():
            arrived(spot(slice(0, 2), beyond, c, full), 6)
            arrived(spot(slice(2, 4), beyond, c, full), 7)

        def over_chip(slot, over):
            return lambda: push(spot(every, over, c, full), slot, sibling)

        def whole():
            for slot, over in ((8, me_over), (9, down), (10, up), (11, beyond)):
                arrived(spot(every, over, other, full), slot)

        def drain():
            def left(ref, slot):
                copy(ref, ref, send_j(j, slot), recv_j(j, slot), sibling).wait_send()

            for slot in (0, 1):
                left(spot(me_along, me_over, c, full), slot)
            left(spot(me_along, me_over, c, (lo, mid)), 2)
            left(spot(me_along, me_over, c, (mid, hi)), 3)
            for slot in (4, 5, 8, 9, 10, 11):
                left(spot(every, me_over, c, full), slot)
            left(spot(slice(0, 2), me_over, c, full), 6)
            left(spot(slice(2, 4), me_over, c, full), 7)

        return (
            [share], [forward_up, forward_down], [row, over_chip(8, me_over)],
            [row_up, row_down, over_chip(9, down), over_chip(10, up)], [last, over_chip(11, beyond)], [whole], [drain],
        )

    def weight_view(j):
        return lambda xi, zi, ci, lo, hi: held.at[j, xi, zi, ci, lo:hi]

    weight_sems = (lambda j, slot: send.at[j, slot], lambda j, slot: recv.at[j, slot])
    fold_sems = (lambda j, slot: fold_send.at[slot], lambda j, slot: fold_recv.at[slot])

    def weight_stages(p):
        a, b = 2 * p, 2 * p + 1
        part = (0, SHARE // 2, SHARE)
        return zip(
            gather_stages(a, weight_view(a), False, weight_sems, part),
            gather_stages(b, weight_view(b), True, weight_sems, part),
        )

    def run_stage(index):
        def stage(p):
            for parts in zip(*list(weight_stages(p))[index]):
                for part in parts:
                    part()
        return stage

    def fold_view(xi, zi, ci, lo, hi):
        return folded.at[xi, zi, ci, lo:hi]

    fold_stages = gather_stages(0, fold_view, False, fold_sems, (RANK, RANK + RANK // 2, 2 * RANK))

    def have_share(p):
        for j in (2 * p, 2 * p + 1):
            @pl.when(layer >= 2)
            def _():
                share_local(j).wait()

            @pl.when(layer < 2)
            def _():
                copy(own(j), own(j), send.at[j, 12], recv.at[j, 12], sibling).wait_recv()

    def half_of(which, index, low, ci):
        return which.at[index, low:low + RANK, pl.ds(pl.multiple_of(ci * (WIDTH // 2), WIDTH // 2), WIDTH // 2)]

    def proj_copy(index, low, slot, device):
        ref = half_of(wide_out, index, low, c)
        return copy(ref, ref, proj_send.at[slot], proj_recv.at[slot], device)

    def proj_out_copies(kind):
        if kind == 2:
            return [proj_copy(1, 0, 3, {"layer": 1})]
        if kind == 1:
            return [proj_copy(0, 0, 0, {"layer": 2})]
        if kind == 0:
            return [proj_copy(0, RANK, 1, {"layer": 1}), proj_copy(0, RANK, 2, {"layer": 2})]
        return []

    def proj_in_copies(kind):
        if kind == 2:
            return [proj_copy(0, 0, 0, above), proj_copy(0, RANK, 2, above)]
        if kind == 1:
            return [proj_copy(0, RANK, 1, above), proj_copy(1, 0, 3, above)]
        return []

    def proj_chip_copies(kind):
        if kind == 2:
            return [proj_copy(0, 0, 4, sibling), proj_copy(0, RANK, 5, sibling)]
        if kind == 1:
            return [proj_copy(0, RANK, 5, sibling), proj_copy(1, 0, 6, sibling)]
        return []

    def proj_chip_arrived(kind):
        for index, low, slot in {2: ((0, 0, 4), (0, RANK, 5)), 1: ((0, RANK, 5), (1, 0, 6))}[kind]:
            ref = half_of(wide_out, index, low, other)
            copy(ref, ref, proj_send.at[slot], proj_recv.at[slot], sibling).wait_recv()

    def proj_loads(kind):
        places = {
            3: [(1, 0), (1, RANK)], 2: [(1, 0), (1, RANK)], 1: [(0, 0)], 0: [(0, RANK)],
        }[kind]
        return [
            load(proj_out, wide_out.at[index, low:low + RANK], 8 + i) for i, (index, low) in enumerate(places)
        ]

    def proj_in_loads():
        return [load(proj_in, wide_in.at[i * RANK:(i + 1) * RANK], 10 + i) for i in range(2)]

    def block_source(index):
        half = slice(index % 2 * TOKENS, (index % 2 + 1) * TOKENS)
        return (pool_in, val_in, pool_top, val_top)[index // 2].at[half]

    def block_load(source):
        return load(source, block, 7)

    @pl.when(layer >= 2)
    def _():
        def body(j, carry):
            share_local(j).start()
            return carry
        lax.fori_loop(0, CHUNKS, body, 0)

    def share_pair(p):
        for kind, partner in ((3, above), (2, below)):
            @on(kind)
            def _():
                share_out(2 * p, partner).start()
                share_out(2 * p + 1, partner).start()

    for pair in range(AHEAD):
        share_pair(pair)
    for kind in range(4):
        @on(kind)
        def _():
            for item in proj_loads(kind) + loads(kind):
                item.start()
    for item in proj_in_loads():
        item.start()
    block_load(block_source(0)).start()

    def gate_rows(index):
        base = pl.multiple_of(index * 32, 32)
        value = first[pl.ds(base, 32), :].astype(f32)
        top = second[pl.ds(base, 32), :].astype(f32)
        gated[pl.ds(base, 32), :] = (top * silu_slope(value)).astype(bf16)

    def gate_some(start, count):
        def body(i, carry):
            gate_rows(start + i)
            return carry
        lax.fori_loop(0, count, body, 0)

    def grad_copy(j, rows, device):
        return copy(grad.at[j, 0:rows], grad.at[j, 0:rows], grad_send.at[j], grad_recv.at[j], device)

    def upper_chunk(j, rows, device):
        total[0, 0:rows] = second[0:rows, columns(j)].astype(f32)

        def body(xi, carry):
            piece = held[j, xi].reshape(WIDTH // 4, COLS)
            left = gated[0:rows, pl.ds(pl.multiple_of(xi * (WIDTH // 4), WIDTH // 4), WIDTH // 4)]
            total[0, 0:rows] += jnp.dot(left, piece, preferred_element_type=f32)
            return carry
        lax.fori_loop(0, 4, body, 0)
        grad[j, 0:rows] = total[0, 0:rows].astype(bf16)
        grad_copy(j, rows, device).start()

    def add_product(n, q, rows):
        piece = held[n, q // 2, pl.ds(2 * (q % 2), 2)].reshape(4 * SHARE, COLS)
        left = gated[0:rows, pl.ds(pl.multiple_of(q * 2 * COLS, 2 * COLS), 2 * COLS)]
        total[n, 0:rows] += jnp.dot(left, piece, preferred_element_type=f32)

    def lower_weight(n, ready, rows):
        total[n, 0:rows] = jnp.zeros((rows, COLS), f32)
        total[n + 1, 0:rows] = jnp.zeros((rows, COLS), f32)

        def body(q, carry):
            add_product(n, q, rows)
            add_product(n + 1, q, rows)
            return carry
        lax.fori_loop(0, ready, body, 0)

    def lower_gate(q, rows):
        for k in (2 * q, 2 * q + 1):
            grad_copy(k, rows, above).wait_recv()

            def gating(i, carry):
                base = pl.multiple_of(i * 64, 64)
                value = first[pl.ds(base, 64), columns(k)].astype(f32)
                up = grad[k, pl.ds(base, 64)].astype(f32)
                gated[pl.ds(base, 64), columns(k)] = (up * silu_slope(value)).astype(bf16)
                return carry
            lax.fori_loop(0, rows // 64, gating, 0)
            low_two[0:rows] += transposed(grad[k, 0:rows], wide_out[1, :, columns(k)])

    def lower_grad(q, ready, rows):
        lower_gate(q, rows)

        def body(n, carry):
            add_product(2 * n, q, rows)
            add_product(2 * n + 1, q, rows)
            return carry
        lax.fori_loop(0, ready // 2, body, 0)

    def when_in(t, lag, what):
        @pl.when((t >= lag) & (t < PAIRS + lag))
        def _():
            what(t - lag)

    def early(t):
        @pl.when(t == 0)
        def _():
            for kind in range(4):
                @on(kind)
                def _():
                    for item in proj_loads(kind):
                        item.wait()
                    for item in proj_out_copies(kind):
                        item.start()
            folded[:, :, :, 0:RANK] = jnp.zeros((4, 4, 2, RANK, 2 * RANK), bf16)
            low_two[...] = jnp.zeros((MAIN, 2 * RANK), f32)

        @pl.when(t == 1)
        def _():
            for item in proj_in_loads():
                item.wait()
            for kind in range(4):
                @on(kind)
                def _():
                    for item in loads(kind):
                        item.wait()

        for index in range(4):
            turn_of = 1 + index + jnp.where((layer == 1) & (index > 1), 2, 0)

            @pl.when(t == turn_of)
            def _():
                block_load(block_source(index)).wait()
                low_in[index] = transposed(block[...], wide_in[...])
                if index == 1:
                    @on(1)
                    def _():
                        block_load(weight).start()

                    @pl.when(layer != 1)
                    def _():
                        block_load(block_source(2)).start()
                elif index < 3:
                    block_load(block_source(index + 1)).start()
                else:
                    @on(3)
                    def _():
                        block_load(block_source(4)).start()
        for index in range(4, 8):
            @pl.when((t == 1 + index) & (layer == 3))
            def _():
                block_load(block_source(index)).wait()
                low_mid[pl.ds((index - 4) * TOKENS, TOKENS)] = transposed(block[...], wide_out[1])
                if index < 7:
                    block_load(block_source(index + 1)).start()

        @pl.when((t >= 1) & (t < 5) & (layer == 3))
        def _():
            gate_some(3 * (t - 1), jnp.minimum(3, MAIN // 32 - 3 * (t - 1)))

        for kind, when in ((2, 9), (1, 3)):
            @pl.when((t == when) & (layer == kind))
            def _():
                for item in proj_in_copies(kind):
                    item.wait_recv()
                for item in proj_chip_copies(kind):
                    item.start()

            @pl.when((t == when + 1) & (layer == kind))
            def _():
                proj_chip_arrived(kind)
                if kind == 1:
                    wide_out[1, RANK:2 * RANK] = wide_out[1, 0:RANK]

        @pl.when((t == 4) & (layer == 1))
        def _():
            block_load(weight).wait()
            folded[x, z, c, RANK:2 * RANK] = transposed(wide_out[0, RANK:2 * RANK], block[...]).astype(bf16)
            mine = folded.at[x, z, c, RANK:2 * RANK]
            copy(mine, mine, fold_send.at[12], fold_recv.at[12], above).start()
            block_load(block_source(2)).start()

        for index, stage in enumerate(fold_stages[:6]):
            lag = jnp.where(layer == 1, FOLD_ONE, FOLD_TWO)

            @pl.when((t == lag + index) & ((layer == 1) | (layer == 2)))
            def _():
                if index == 0:
                    @on(2)
                    def _():
                        mine = folded.at[x, z, c, RANK:2 * RANK]
                        copy(mine, mine, fold_send.at[12], fold_recv.at[12], above).wait_recv()
                for part in stage:
                    part()

    def step(t, carry):
        @pl.when(t + AHEAD < PAIRS)
        def _():
            share_pair(t + AHEAD)
        for kind, partner in ((3, above), (2, below)):
            @pl.when((t >= 1) & (t <= REST // SLICE) & (layer == kind))
            def _():
                rest_slice(t - 1, partner).start()

        @pl.when((t >= 1) & (t < 9) & (layer == 1))
        def _():
            pool_part(2 * (t - 1)).start()
            pool_part(2 * (t - 1) + 1).start()

            @pl.when(t % 2 == 1)
            def _():
                val_part((t - 1) // 2).start()

        when_in(t, 0, have_share)
        for lag, index in ((0, 0), (LAG_FORWARD, 1), (LAG_ROW, 2), (LAG_ROW_FORWARD, 3), (LAG_LAST, 4)):
            when_in(t, lag, run_stage(index))
        early(t)
        when_in(t, LAG_USE, run_stage(5))

        @pl.when((t == LAG_USE + LATE) & (layer < 2))
        def _():
            for i in range(REST // SLICE):
                rest_slice(i, above).wait_recv()

            @on(0)
            def _():
                gate_some(0, REST // 32)

                def body(j, inner_carry):
                    upper_chunk(j, REST, above)
                    return inner_carry
                lax.fori_loop(0, 2 * LATE, body, 0)

        for kind, rows, target, begin in ((3, MAIN, below, LAG_USE), (0, REST, above, LAG_USE + LATE)):
            @pl.when((layer == kind) & (t >= begin) & (t < PAIRS + LAG_USE))
            def _():
                upper_chunk(2 * (t - LAG_USE), rows, target)
                upper_chunk(2 * (t - LAG_USE) + 1, rows, target)

        whole = jnp.minimum(2 * (t - LAG_USE) + 2, CHUNKS)
        begin_rest = LAG_GRAD + LATE
        ready_rest = jnp.where(t <= begin_rest, 0, jnp.where(t < begin_rest + LATE, 2 * (t - begin_rest), t - LAG_GRAD))
        for kind, rows, ready in ((2, MAIN, jnp.maximum(t - LAG_GRAD, 0)), (1, REST, ready_rest)):
            @pl.when((layer == kind) & (t >= LAG_USE) & (t < PAIRS + LAG_USE))
            def _():
                lower_weight(2 * (t - LAG_USE), ready, rows)

        @pl.when((layer == 2) & (t >= LAG_GRAD) & (t < PAIRS + LAG_GRAD - 1))
        def _():
            lower_grad(t - LAG_GRAD, whole, MAIN)

        @pl.when((layer == 1) & (t >= begin_rest) & (t < begin_rest + LATE))
        def _():
            lower_grad(2 * (t - begin_rest), whole, REST)
            lower_grad(2 * (t - begin_rest) + 1, whole, REST)

        @pl.when((layer == 1) & (t >= begin_rest + LATE) & (t < PAIRS + LAG_GRAD - 1))
        def _():
            lower_grad(t - LAG_GRAD, whole, REST)
        return carry

    lax.fori_loop(0, PAIRS + LAG_GRAD - 1, step, 0)

    def drain(p, carry):
        run_stage(6)(p)

        @pl.when(layer >= 2)
        def _():
            share_out(2 * p, above).wait_send()
            share_out(2 * p + 1, above).wait_send()
        for kind, rows in ((3, MAIN), (0, REST)):
            @on(kind)
            def _():
                grad_copy(2 * p, rows, above).wait_send()
                grad_copy(2 * p + 1, rows, above).wait_send()
        return carry
    lax.fori_loop(0, PAIRS, drain, 0)

    @pl.when(layer >= 2)
    def _():
        for i in range(REST // SLICE):
            rest_slice(i, above).wait_send()

    @on(1)
    def _():
        for item in main_parts():
            item.wait_send()
        mine = folded.at[x, z, c, RANK:2 * RANK]
        copy(mine, mine, fold_send.at[12], fold_recv.at[12], above).wait_send()

    @pl.when((layer == 1) | (layer == 2))
    def _():
        fold_stages[6][0]()
    for kind in (2, 1, 0):
        @on(kind)
        def _():
            for item in proj_out_copies(kind) + proj_chip_copies(kind):
                item.wait_send()

    def finish(kind, rows):
        if kind == 2:
            for item in main_parts():
                item.wait_recv()
        lower_gate(PAIRS - 1, rows)
        low_mid[0:rows] = jnp.zeros((rows, 2 * RANK), f32)

        def body(i, carry):
            for n in (2 * i, 2 * i + 1):
                add_product(n, PAIRS - 1, rows)
                for base in range(0, rows, 64):
                    part = slice(base, base + 64)
                    up = grad[n, part].astype(f32)
                    value = second[part, columns(n)].astype(f32)
                    low = (up + total[n, part]).astype(bf16)
                    first[part, columns(n)] = low
                    grad[n, part] = (low.astype(f32) * silu_slope(value)).astype(bf16)
                fold = folded[n // 4, n % 4]
                left = jnp.concatenate([first[0:rows, columns(n)], grad[n, 0:rows]], 1)
                right = jnp.concatenate([wide_out[0, :, columns(n)], fold[0], fold[1]], 1)
                low_mid[0:rows] += transposed(left, right)
            return carry
        lax.fori_loop(0, PAIRS, body, 0)

    wide = (RANK, 2 * RANK)
    lower = low_half(wide)
    lower_rows = low_half((TOKENS, 2 * RANK))

    tokens = lax.broadcasted_iota(jnp.int32, (TOKENS, 2 * RANK), 0)
    valid = [
        (tokens < jnp.where(lower_rows, lens[0], lens[1])).astype(f32) for lens in (pool_len, val_len)
    ]

    def swap(value):
        return pltpu.roll(value, RANK, 1)

    def put(index, slot, value, mask):
        outgoing[index, slot] = (value * valid[mask]).astype(bf16)

    @on(3)
    def _():
        rows = [low_mid[i * TOKENS:(i + 1) * TOKENS] for i in range(4)]
        landed[0] = (jnp.where(lower_rows, rows[0], rows[1]) * valid[0]).astype(bf16)
        landed[1] = (jnp.where(lower_rows, rows[2], rows[3]) * valid[1]).astype(bf16)
        landed[2] = jnp.zeros_like(landed[2])

    @on(2)
    def _():
        finish(2, MAIN)
        def short(ref):
            return jnp.concatenate([ref[2 * TOKENS:MAIN], jnp.zeros((TOKENS - FIRST, 2 * RANK), f32)], 0)

        mid = [low_mid[0:TOKENS], low_mid[TOKENS:2 * TOKENS], short(low_mid)]
        two = [low_two[0:TOKENS], low_two[TOKENS:2 * TOKENS], short(low_two)]
        put(1, 0, jnp.where(lower_rows, mid[0], swap(mid[1])), 0)
        put(1, 1, jnp.where(lower_rows, mid[2], 0.0), 1)
        put(0, 0, jnp.where(lower_rows, swap(mid[0]), mid[1]), 0)
        put(0, 1, jnp.where(lower_rows, swap(mid[2]), 0.0), 1)
        landed[0] = (jnp.where(lower_rows, two[0], two[1]) * valid[0]).astype(bf16)
        landed[1] = (jnp.where(lower_rows, two[2], 0.0) * valid[1]).astype(bf16)

    @on(1)
    def _():
        finish(1, REST)
        def split(ref):
            other_tokens = REST - TOKENS
            return (
                jnp.concatenate([jnp.zeros((TOKENS - other_tokens, 2 * RANK), f32), ref[0:other_tokens]], 0),
                ref[other_tokens:REST],
            )

        one, two = split(low_mid), split(low_two)
        put(0, 1, jnp.where(lower_rows, swap(one[0]), one[1]), 1)
        put(2, 1, jnp.where(lower_rows, two[0], two[1]), 1)
        landed[2] = (jnp.where(lower_rows, one[0], swap(one[1])) * valid[1]).astype(bf16)

    def low(source, slot, plane):
        return copy(source, landed.at[slot], low_send.at[slot + 3 * plane], low_recv.at[slot], {"layer": plane})

    def lows(kind):
        if kind == 2:
            return [low(outgoing.at[0, 0], 0, 0), low(outgoing.at[0, 1], 1, 0),
                    low(outgoing.at[1, 0], 0, 1), low(outgoing.at[1, 1], 1, 1)]
        if kind == 1:
            return [low(outgoing.at[0, 1], 2, 0), low(outgoing.at[2, 1], 2, 2)]
        return []

    def lows_in(kind):
        return [low(landed.at[slot], slot, (kind + 1) % 4) for slot in {3: (), 2: (2,), 1: (0, 1), 0: (0, 1, 2)}[kind]]

    for kind in (2, 1):
        @pl.when(layer == kind)
        def _():
            for item in lows(kind):
                item.start()

    for kind in (2, 1, 0):
        @pl.when(layer == kind)
        def _():
            for item in lows_in(kind):
                item.wait_recv()

    def across_tokens(left, right):
        return lax.dot_general(left, right, (((0,), (0,)), ((), ())), precision=highest, preferred_element_type=f32)

    def blocks(value):
        return jnp.where(lower, value[0:RANK], value[RANK:2 * RANK])

    def both(value):
        return value + swap(value)

    pool_low = jnp.where(lower_rows, low_in[0], low_in[1]) * valid[0]
    val_low = jnp.where(lower_rows, low_in[2], low_in[3]) * valid[1]
    pool_out = landed[0].astype(f32)
    val_out = landed[1].astype(f32) + landed[2].astype(f32)
    vals[x, z, c] = blocks(across_tokens(val_out, val_low)).astype(bf16)
    part_in = both(blocks(across_tokens(pool_low, pool_low)))
    part_out = both(blocks(across_tokens(pool_out, pool_out)))
    factors[x * 2 + c, 0:RANK] = jnp.where(lower, part_in, part_out)
    factors[x * 2 + c, RANK:RANK + 8] = jnp.full((8, 2 * RANK), (pool_len[0] + pool_len[1]).astype(f32))

    mine = x * 2 + c
    sent_one = [copy(factors.at[mine], factors.at[mine], fac_send.at[i], fac_recv.at[mine], n[3]) for i, n in enumerate(near)]
    sent_one += [copy(vals.at[x, z, c], vals.at[x, z, c], val_send.at[i], val_recv.at[mine], n[3]) for i, n in enumerate(near)]
    for item in sent_one:
        item.start()
    pool_grads = blocks(across_tokens(pool_low, pool_out))
    for slot, xi, ci, device in near:
        copy(factors.at[slot], factors.at[slot], fac_send.at[0], fac_recv.at[slot], device).wait_recv()
    factors_z[z] = sum(factors[i] for i in range(1, 8)) + factors[0]
    sent_two = [copy(factors_z.at[z], factors_z.at[z], facz_send.at[i], facz_recv.at[z], a[1]) for i, a in enumerate(across)]
    for item in sent_two:
        item.start()
    for slot, xi, ci, device in near:
        copy(vals.at[xi, z, ci], vals.at[xi, z, ci], val_send.at[0], val_recv.at[slot], device).wait_recv()
    sent_three = [copy(vals.at[:, z], vals.at[:, z], valz_send.at[i], valz_recv.at[z], a[1]) for i, a in enumerate(across)]
    for item in sent_three:
        item.start()
    for zi, device in across:
        copy(factors_z.at[zi], factors_z.at[zi], facz_send.at[0], facz_recv.at[zi], device).wait_recv()
    factor_sum = factors_z[0] + factors_z[1] + factors_z[2] + factors_z[3]
    inverse = damped_inverses(factor_sum[0:RANK] / factor_sum[RANK:RANK + 1])
    inv_in = inverse[:, 0:RANK]
    turned = swap(inverse)
    twice = jnp.where(lower, turned, inverse)
    inv_out = jnp.concatenate([jnp.where(lower, twice, 0.0), jnp.where(lower, 0.0, twice)], 0)
    scaled = jnp.dot(inv_in, pool_grads, precision=highest, preferred_element_type=f32)
    scaled = jnp.dot(scaled, inv_out, precision=highest, preferred_element_type=f32)
    coarse = scaled.astype(bf16)
    fine = (scaled - coarse.astype(f32)).astype(bf16)
    empty = jnp.zeros(wide, bf16)

    def spread(value):
        return jnp.concatenate(
            [jnp.concatenate([value, empty], 1), jnp.concatenate([empty, value], 1)], 0
        )

    coarse, fine = spread(coarse), spread(fine)
    for zi, device in across:
        copy(vals.at[:, zi], vals.at[:, zi], valz_send.at[0], valz_recv.at[zi], device).wait_recv()
    every = vals[...].reshape(32 * RANK, 2 * RANK)
    product = jnp.dot(every, coarse, preferred_element_type=f32) + jnp.dot(every, fine, preferred_element_type=f32)
    at_row = lax.broadcasted_iota(jnp.int32, product.shape, 0) % RANK
    at_lane = lax.broadcasted_iota(jnp.int32, product.shape, 1) % RANK
    summed = jnp.where(at_row == at_lane, product, 0.0).reshape(32, RANK, 4 * RANK).sum(1)
    group = lax.broadcasted_iota(jnp.int32, (8, 4 * RANK), 1) // RANK
    picks = (lax.broadcasted_iota(jnp.int32, (8, 4 * RANK), 0) == group).astype(f32)
    part = lax.dot_general(picks, summed, (((1,), (1,)), ((), ())), precision=highest, preferred_element_type=f32)
    layers[layer] = jnp.concatenate([part, jnp.zeros((8, 96), f32)], 1)
    sent_last = [copy(layers.at[layer], layers.at[layer], lay_send.at[i], lay_recv.at[layer], q[1]) for i, q in enumerate(planes)]
    for item in sent_last:
        item.start()
    for plane, device in planes:
        copy(layers.at[plane], layers.at[plane], lay_send.at[0], lay_recv.at[plane], device).wait_recv()
    table = (layers[0] + layers[1] + layers[2] + layers[3]) * (1.0 / (RANK * TOKENS))
    lane = lax.broadcasted_iota(jnp.int32, (128, 16), 0)
    spot_of = lax.broadcasted_iota(jnp.int32, (128, 16), 1) + 16 * layer

    def placed(index):
        return jnp.dot(
            table, (2 * lane + index == spot_of).astype(f32), precision=highest, preferred_element_type=f32
        )

    scores_out[...] = placed(0)[0:2] + placed(1)[2:4]

    for item in sent_one + sent_two + sent_three + sent_last:
        item.wait_send()
    for kind in (2, 1):
        @pl.when(layer == kind)
        def _():
            for item in lows(kind):
                item.wait_send()


def whole(*operands):
    anywhere = pl.BlockSpec(memory_space=pl.ANY)
    inside = pl.BlockSpec(memory_space=pltpu.VMEM)
    dma = pltpu.SemaphoreType.DMA
    bf16, f32 = jnp.bfloat16, jnp.float32
    return pl.pallas_call(
        whole_kernel,
        out_shape=jax.ShapeDtypeStruct((2, 16), f32),
        in_specs=[anywhere] * 7 + [pl.BlockSpec(memory_space=pltpu.SMEM)] * 2,
        out_specs=inside,
        scratch_shapes=[
            pltpu.VMEM((CHUNKS, 4, 4, 2, SHARE, COLS), bf16),
            pltpu.VMEM((MAIN, WIDTH), bf16),
            pltpu.VMEM((MAIN, WIDTH), bf16),
            pltpu.VMEM((MAIN, WIDTH), bf16),
            pltpu.VMEM((CHUNKS, MAIN, COLS), bf16),
            pltpu.VMEM((CHUNKS, MAIN, COLS), f32),
            pltpu.VMEM((TOKENS, WIDTH), bf16),
            pltpu.VMEM((2 * RANK, WIDTH), bf16),
            pltpu.VMEM((2, 2 * RANK, WIDTH), bf16),
            pltpu.VMEM((4, 4, 2, 2 * RANK, SHARE), bf16),
            pltpu.VMEM((4 * TOKENS, 2 * RANK), f32),
            pltpu.VMEM((MAIN, 2 * RANK), f32),
            pltpu.VMEM((4, TOKENS, 2 * RANK), f32),
            pltpu.VMEM((3, 2, TOKENS, 2 * RANK), bf16),
            pltpu.VMEM((3, TOKENS, 2 * RANK), bf16),
            pltpu.VMEM((8, RANK + 8, 2 * RANK), f32),
            pltpu.VMEM((4, RANK + 8, 2 * RANK), f32),
            pltpu.VMEM((4, 4, 2, RANK, 2 * RANK), bf16),
            pltpu.VMEM((4, 8, 128), f32),
            dma((CHUNKS, 13)), dma((CHUNKS, 13)), dma((CHUNKS,)), dma((CHUNKS,)), dma((24,)), dma((24,)),
            dma((CHUNKS + 12,)), dma((13,)), dma((13,)), dma((7,)), dma((7,)),
            dma((12,)), dma((3,)), dma((7,)), dma((8,)), dma((7,)), dma((8,)),
            dma((3,)), dma((4,)), dma((3,)), dma((4,)), dma((3,)), dma((4,)),
        ],
        compiler_params=pltpu.CompilerParams(
            collective_id=0, has_side_effects=True, vmem_limit_bytes=62 * 1024 * 1024
        ),
        name="whole",
    )(*operands)


def on_device(
    pool_inputs, val_inputs, pool_top, val_top, weight, proj_in, proj_out, pool_len, val_len
):
    return whole(
        *(rows.reshape(-1, WIDTH) for rows in (pool_inputs[0], val_inputs[0], pool_top, val_top)), weight[0], proj_in[0].T, proj_out[0].T, pool_len, val_len
    )


def solution(mesh):
    placed = (
        P("layer", "trace", None, None),
        P("layer", "trace", None, None),
        P("trace", None, None),
        P("trace", None, None),
        P("layer", "trace", None),
        P("layer", None, None),
        P("layer", None, None),
        P("trace"),
        P("trace"),
    )
    return jax.shard_map(
        on_device, mesh=mesh, in_specs=placed, out_specs=P("trace", "layer"), check_vma=False
    )
```

```python
import functools

import jax
import jax.numpy as jnp
from jax import lax
from jax.experimental import pallas as pl
from jax.experimental.pallas import tpu as pltpu
from jax.sharding import PartitionSpec as P

MESH = pl.DeviceIdType.MESH
WIDTH = 4096
TOKENS = 128
RANK = 64
CHUNKS = 16
COLS = WIDTH // CHUNKS
PAIRS = CHUNKS // 2
SHARE = 128
MAIN = 320
REST = 192
FIRST = MAIN - 2 * TOKENS
LATE = 2
LAG_FORWARD, LAG_ROW, LAG_ROW_FORWARD, LAG_LAST, LAG_USE = 1, 2, 3, 4, 5
LAG_GRAD = 6
AHEAD = 3
SLICE = 32
PART = 16
FOLD_ONE, FOLD_TWO = 5, 7


def silu_slope(values):
    logistic = jax.nn.sigmoid(values)
    return logistic * (1.0 + values * (1.0 - logistic))


def low_half(shape):
    return lax.broadcasted_iota(jnp.int32, shape, len(shape) - 1) < RANK


def damped_inverses(pair):
    rows = lax.broadcasted_iota(jnp.int32, pair.shape, 0)
    lanes = lax.broadcasted_iota(jnp.int32, pair.shape, 1)
    lower = lanes < RANK
    column = jnp.where(lower, lanes, lanes - RANK)
    diagonal = rows == column
    on_diagonal = jnp.where(diagonal, pair, 0.0)
    trace_first = jnp.sum(jnp.where(lower, on_diagonal, 0.0), keepdims=True)
    trace_second = jnp.sum(jnp.where(lower, 0.0, on_diagonal), keepdims=True)
    scale_back = RANK / jnp.where(lower, trace_first, trace_second)
    value = jnp.where(diagonal, pair * scale_back + 0.1, pair * scale_back)
    at = column[0:1]

    def spread(k):
        return jnp.where(
            lower,
            jnp.broadcast_to(value[:, k:k + 1], pair.shape),
            jnp.broadcast_to(value[:, RANK + k:RANK + k + 1], pair.shape),
        )

    for k in range(0, RANK, 2):
        one, two = spread(k), spread(k + 1)
        a, b = one[k:k + 1], two[k:k + 1]
        c, d = one[k + 1:k + 2], two[k + 1:k + 2]
        scale = 1.0 / (a * d - b * c)
        a, b, c, d = a * scale, b * scale, c * scale, d * scale
        upper, under = value[k:k + 1], value[k + 1:k + 2]
        row_one = jnp.where(at == k, d, jnp.where(at == k + 1, -b, d * upper - b * under))
        row_two = jnp.where(at == k, -c, jnp.where(at == k + 1, a, a * under - c * upper))
        one = jnp.where(rows == k, -1.0, jnp.where(rows == k + 1, 0.0, one))
        two = jnp.where(rows == k + 1, -1.0, jnp.where(rows == k, 0.0, two))
        gone = (rows == k) | (rows == k + 1) | (column == k) | (column == k + 1)
        value = jnp.where(gone, 0.0, value) - one * row_one - two * row_two
    return value * scale_back


def whole_kernel(
    pool_in, val_in, pool_top, val_top, weight, proj_in, proj_out, pool_len, val_len,
    scores_out,
    held, first, second, gated, grad, total, block, wide_in, wide_out, folded,
    low_mid, low_two, low_in, outgoing,
    landed, factors, factors_z, vals, layers,
    send, recv, grad_send, grad_recv, act_send, act_recv, local, fold_send, fold_recv, proj_send, proj_recv,
    low_send, low_recv, fac_send, fac_recv, val_send, val_recv, facz_send, facz_recv, valz_send, valz_recv,
    lay_send, lay_recv,
):
    layer = lax.axis_index("layer")
    trace = lax.axis_index("trace")
    x, z, c = trace // 8, (trace // 2) % 4, trace % 2
    xp, xm, xo = (x + 1) % 4, (x + 3) % 4, (x + 2) % 4
    zp, zm, zo = (z + 1) % 4, (z + 3) % 4, (z + 2) % 4
    other = 1 - c
    highest = lax.Precision.HIGHEST
    f32, bf16 = jnp.float32, jnp.bfloat16

    def at(xi, zi, ci):
        return {"trace": xi * 8 + zi * 2 + ci}

    above = {"layer": (layer + 1) % 4}
    below = {"layer": (layer + 3) % 4}
    sibling = at(x, z, other)

    near = []
    for dx in range(4):
        for dc in range(2):
            if dx or dc:
                xi, ci = (x + dx) % 4, (c + dc) % 2
                near.append((xi * 2 + ci, xi, ci, at(xi, z, ci)))
    across = [((z + dz) % 4, at(x, (z + dz) % 4, c)) for dz in (1, 3, 2)]
    planes = [((layer + dl) % 4, {"layer": (layer + dl) % 4}) for dl in (1, 3, 2)]
    barrier = pltpu.get_barrier_semaphore()
    for device in [n[3] for n in near] + [a[1] for a in across] + [q[1] for q in planes]:
        pl.semaphore_signal(barrier, inc=1, device_id=device, device_id_type=MESH)
    pl.semaphore_wait(barrier, len(near) + len(across) + len(planes))

    def copy(src, dst, send_sem, recv_sem, device):
        return pltpu.make_async_remote_copy(
            src_ref=src, dst_ref=dst, send_sem=send_sem, recv_sem=recv_sem, device_id=device, device_id_type=MESH
        )

    def columns(j):
        return pl.ds(pl.multiple_of(j * COLS, COLS), COLS)

    def transposed(left, right):
        return lax.dot_general(left, right, (((1,), (1,)), ((), ())), preferred_element_type=f32)

    def on(kind):
        return pl.when(layer == kind)

    def own(j):
        return held.at[j, x, z, c]

    def share_out(j, device):
        return copy(weight.at[:, columns(j)], own(j), send.at[j, 12], recv.at[j, 12], device)

    def share_local(j):
        return pltpu.make_async_copy(weight.at[:, columns(j)], own(j), local.at[j])

    def load(src, dst, index):
        return pltpu.make_async_copy(src, dst, local.at[CHUNKS + index])

    def row_loads(pool, val, target, base):
        return [
            load(pool, target.at[0:2 * TOKENS], base),
            load(val.at[0:FIRST], target.at[2 * TOKENS:MAIN], base + 1),
        ]

    def loads(kind):
        return {
            3: lambda: row_loads(pool_in, val_in, first, 0) + row_loads(pool_top, val_top, second, 3),
            2: lambda: row_loads(pool_in, val_in, first, 0),
            1: lambda: [load(val_in.at[FIRST:2 * TOKENS], second.at[0:REST], 0)],
            0: lambda: [load(val_top.at[FIRST:2 * TOKENS], second.at[0:REST], 0)],
        }[kind]()

    def rows_of(base, i):
        return pl.ds(pl.multiple_of(base + i * SLICE, SLICE), SLICE)

    def rest_slice(i, device):
        return copy(
            val_in.at[rows_of(FIRST, i)], first.at[rows_of(0, i)], act_send.at[i], act_recv.at[i], device
        )

    def main_part(source, low, i, base):
        rows = pl.ds(pl.multiple_of(i * PART, PART), PART)
        there = pl.ds(pl.multiple_of(low + i * PART, PART), PART)
        return copy(source.at[rows], second.at[there], act_send.at[base + i], act_recv.at[base + i], above)

    def pool_part(i):
        return main_part(pool_in, 0, i, 0)

    def val_part(i):
        return main_part(val_in, 2 * TOKENS, i, 2 * TOKENS // PART)

    def main_parts():
        return [pool_part(i) for i in range(2 * TOKENS // PART)] + [val_part(i) for i in range(FIRST // PART)]

    def gather_stages(j, view, flip, sems, part, apart):
        send_j, recv_j = sems
        ahead, behind, far = (zp, zm, zo) if flip else (xp, xm, xo)
        up, down, beyond = (xp, xm, xo) if flip else (zp, zm, zo)
        lo, mid, hi = part

        def spot(along, over, ci, rows):
            return view(over, along, ci, *rows) if flip else view(along, over, ci, *rows)

        me_along, me_over = (z, x) if flip else (x, z)

        def to_along(i):
            return at(x, i, c) if flip else at(i, z, c)

        def to_over(i):
            return at(i, z, c) if flip else at(x, i, c)

        full = (lo, hi)
        every = slice(0, 4)

        def push(ref, slot, device):
            copy(ref, ref, send_j(j, slot), recv_j(j, slot), device).start()

        def arrived(ref, slot):
            copy(ref, ref, send_j(j, slot), recv_j(j, slot), sibling).wait_recv()

        def share():
            ref = spot(me_along, me_over, c, full)
            push(ref, 0, to_along(ahead))
            push(ref, 1, to_along(behind))

        def forward_up():
            arrived(spot(behind, me_over, c, full), 0)
            push(spot(behind, me_over, c, (lo, mid)), 2, to_along(ahead))

        def forward_down():
            arrived(spot(ahead, me_over, c, full), 1)
            push(spot(ahead, me_over, c, (mid, hi)), 3, to_along(behind))

        def row():
            arrived(spot(far, me_over, c, (lo, mid)), 2)
            arrived(spot(far, me_over, c, (mid, hi)), 3)
            ref = spot(every, me_over, c, full)
            push(ref, 4, to_over(up))
            push(ref, 5, to_over(down))

        def row_up():
            arrived(spot(every, down, c, full), 4)
            push(spot(slice(0, 2), down, c, full), 6, to_over(up))

        def row_down():
            arrived(spot(every, up, c, full), 5)
            push(spot(slice(2, 4), up, c, full), 7, to_over(down))

        def last():
            arrived(spot(slice(0, 2), beyond, c, full), 6)
            arrived(spot(slice(2, 4), beyond, c, full), 7)

        def over_chip(slot, over):
            def row_push():
                pl.when(apart)(lambda: push(spot(every, over, c, full), slot, sibling))
            return row_push

        def over_chip_all():
            pl.when(jnp.logical_not(apart))(lambda: push(spot(every, every, c, full), 8, sibling))

        def whole():
            @pl.when(apart)
            def _():
                for slot, over in ((8, me_over), (9, down), (10, up), (11, beyond)):
                    arrived(spot(every, over, other, full), slot)

            pl.when(jnp.logical_not(apart))(lambda: arrived(spot(every, every, other, full), 8))

        def drain():
            def left(ref, slot):
                copy(ref, ref, send_j(j, slot), recv_j(j, slot), sibling).wait_send()

            for slot in (0, 1):
                left(spot(me_along, me_over, c, full), slot)
            left(spot(me_along, me_over, c, (lo, mid)), 2)
            left(spot(me_along, me_over, c, (mid, hi)), 3)
            for slot in (4, 5):
                left(spot(every, me_over, c, full), slot)

            @pl.when(apart)
            def _():
                for slot in (8, 9, 10, 11):
                    left(spot(every, me_over, c, full), slot)

            pl.when(jnp.logical_not(apart))(lambda: left(spot(every, every, c, full), 8))
            left(spot(slice(0, 2), me_over, c, full), 6)
            left(spot(slice(2, 4), me_over, c, full), 7)

        return (
            [share], [forward_up, forward_down], [row, over_chip(8, me_over)],
            [row_up, row_down, over_chip(9, down), over_chip(10, up)], [last, over_chip(11, beyond), over_chip_all], [whole], [drain],
        )

    def weight_view(j):
        return lambda xi, zi, ci, lo, hi: held.at[j, xi, zi, ci, lo:hi]

    weight_sems = (lambda j, slot: send.at[j, slot], lambda j, slot: recv.at[j, slot])
    fold_sems = (lambda j, slot: fold_send.at[slot], lambda j, slot: fold_recv.at[slot])

    def weight_stages(p):
        a, b = 2 * p, 2 * p + 1
        part = (0, SHARE // 2, SHARE)
        return zip(
            gather_stages(a, weight_view(a), False, weight_sems, part, p == PAIRS - 1),
            gather_stages(b, weight_view(b), True, weight_sems, part, p == PAIRS - 1),
        )

    def run_stage(index):
        def stage(p):
            for parts in zip(*list(weight_stages(p))[index]):
                for part in parts:
                    part()
        return stage

    def fold_view(xi, zi, ci, lo, hi):
        return folded.at[xi, zi, ci, lo:hi]

    fold_stages = gather_stages(0, fold_view, False, fold_sems, (RANK, RANK + RANK // 2, 2 * RANK), layer >= 0)

    def have_share(p):
        for j in (2 * p, 2 * p + 1):
            @pl.when(layer >= 2)
            def _():
                share_local(j).wait()

            @pl.when(layer < 2)
            def _():
                copy(own(j), own(j), send.at[j, 12], recv.at[j, 12], sibling).wait_recv()

    def half_of(which, index, low, ci):
        return which.at[index, low:low + RANK, pl.ds(pl.multiple_of(ci * (WIDTH // 2), WIDTH // 2), WIDTH // 2)]

    def proj_copy(index, low, slot, device):
        ref = half_of(wide_out, index, low, c)
        return copy(ref, ref, proj_send.at[slot], proj_recv.at[slot], device)

    def proj_out_copies(kind):
        if kind == 2:
            return [proj_copy(1, 0, 3, {"layer": 1})]
        if kind == 1:
            return [proj_copy(0, 0, 0, {"layer": 2})]
        if kind == 0:
            return [proj_copy(0, RANK, 1, {"layer": 1}), proj_copy(0, RANK, 2, {"layer": 2})]
        return []

    def proj_in_copies(kind):
        if kind == 2:
            return [proj_copy(0, 0, 0, above), proj_copy(0, RANK, 2, above)]
        if kind == 1:
            return [proj_copy(0, RANK, 1, above), proj_copy(1, 0, 3, above)]
        return []

    def proj_chip_copies(kind):
        if kind == 2:
            return [proj_copy(0, 0, 4, sibling), proj_copy(0, RANK, 5, sibling)]
        if kind == 1:
            return [proj_copy(0, RANK, 5, sibling), proj_copy(1, 0, 6, sibling)]
        return []

    def proj_chip_arrived(kind):
        for index, low, slot in {2: ((0, 0, 4), (0, RANK, 5)), 1: ((0, RANK, 5), (1, 0, 6))}[kind]:
            ref = half_of(wide_out, index, low, other)
            copy(ref, ref, proj_send.at[slot], proj_recv.at[slot], sibling).wait_recv()

    def proj_loads(kind):
        places = {
            3: [(1, 0), (1, RANK)], 2: [(1, 0), (1, RANK)], 1: [(0, 0)], 0: [(0, RANK)],
        }[kind]
        return [
            load(proj_out, wide_out.at[index, low:low + RANK], 8 + i) for i, (index, low) in enumerate(places)
        ]

    def proj_in_loads():
        return [load(proj_in, wide_in.at[i * RANK:(i + 1) * RANK], 10 + i) for i in range(2)]

    def block_source(index):
        half = slice(index % 2 * TOKENS, (index % 2 + 1) * TOKENS)
        return (pool_in, val_in, pool_top, val_top)[index // 2].at[half]

    def block_load(source):
        return load(source, block, 7)

    @pl.when(layer >= 2)
    def _():
        def body(j, carry):
            share_local(j).start()
            return carry
        lax.fori_loop(0, CHUNKS, body, 0)

    def share_pair(p):
        for kind, partner in ((3, above), (2, below)):
            @on(kind)
            def _():
                share_out(2 * p, partner).start()
                share_out(2 * p + 1, partner).start()

    for pair in range(AHEAD):
        share_pair(pair)
    for kind in range(4):
        @on(kind)
        def _():
            for item in proj_loads(kind) + loads(kind):
                item.start()
    for item in proj_in_loads():
        item.start()
    block_load(block_source(0)).start()

    def gate_rows(index):
        base = pl.multiple_of(index * 32, 32)
        value = first[pl.ds(base, 32), :].astype(f32)
        top = second[pl.ds(base, 32), :].astype(f32)
        gated[pl.ds(base, 32), :] = (top * silu_slope(value)).astype(bf16)

    def gate_some(start, count):
        def body(i, carry):
            gate_rows(start + i)
            return carry
        lax.fori_loop(0, count, body, 0)

    def grad_copy(j, rows, device):
        return copy(grad.at[j, 0:rows], grad.at[j, 0:rows], grad_send.at[j], grad_recv.at[j], device)

    def upper_chunk(j, rows, device):
        total[0, 0:rows] = second[0:rows, columns(j)].astype(f32)

        def body(xi, carry):
            piece = held[j, xi].reshape(WIDTH // 4, COLS)
            left = gated[0:rows, pl.ds(pl.multiple_of(xi * (WIDTH // 4), WIDTH // 4), WIDTH // 4)]
            total[0, 0:rows] += jnp.dot(left, piece, preferred_element_type=f32)
            return carry
        lax.fori_loop(0, 4, body, 0)
        grad[j, 0:rows] = total[0, 0:rows].astype(bf16)
        grad_copy(j, rows, device).start()

    def add_product(n, q, rows):
        piece = held[n, q // 2, pl.ds(2 * (q % 2), 2)].reshape(4 * SHARE, COLS)
        left = gated[0:rows, pl.ds(pl.multiple_of(q * 2 * COLS, 2 * COLS), 2 * COLS)]
        total[n, 0:rows] += jnp.dot(left, piece, preferred_element_type=f32)

    def lower_weight(n, ready, rows):
        total[n, 0:rows] = jnp.zeros((rows, COLS), f32)
        total[n + 1, 0:rows] = jnp.zeros((rows, COLS), f32)

        def body(q, carry):
            add_product(n, q, rows)
            add_product(n + 1, q, rows)
            return carry
        lax.fori_loop(0, ready, body, 0)

    def lower_gate(q, rows):
        for k in (2 * q, 2 * q + 1):
            grad_copy(k, rows, above).wait_recv()

            def gating(i, carry):
                base = pl.multiple_of(i * 64, 64)
                value = first[pl.ds(base, 64), columns(k)].astype(f32)
                up = grad[k, pl.ds(base, 64)].astype(f32)
                gated[pl.ds(base, 64), columns(k)] = (up * silu_slope(value)).astype(bf16)
                return carry
            lax.fori_loop(0, rows // 64, gating, 0)
            low_two[0:rows] += transposed(grad[k, 0:rows], wide_out[1, :, columns(k)])

    def lower_grad(q, ready, rows):
        lower_gate(q, rows)

        def body(n, carry):
            add_product(2 * n, q, rows)
            add_product(2 * n + 1, q, rows)
            return carry
        lax.fori_loop(0, ready // 2, body, 0)

    def when_in(t, lag, what):
        @pl.when((t >= lag) & (t < PAIRS + lag))
        def _():
            what(t - lag)

    def early(t):
        @pl.when(t == 0)
        def _():
            for kind in range(4):
                @on(kind)
                def _():
                    for item in proj_loads(kind):
                        item.wait()
                    for item in proj_out_copies(kind):
                        item.start()
            folded[:, :, :, 0:RANK] = jnp.zeros((4, 4, 2, RANK, 2 * RANK), bf16)
            low_two[...] = jnp.zeros((MAIN, 2 * RANK), f32)

        @pl.when(t == 1)
        def _():
            for item in proj_in_loads():
                item.wait()
            for kind in range(4):
                @on(kind)
                def _():
                    for item in loads(kind):
                        item.wait()

        for index in range(4):
            turn_of = 1 + index + jnp.where((layer == 1) & (index > 1), 2, 0)

            @pl.when(t == turn_of)
            def _():
                block_load(block_source(index)).wait()
                low_in[index] = transposed(block[...], wide_in[...])
                if index == 1:
                    @on(1)
                    def _():
                        block_load(weight).start()

                    @pl.when(layer != 1)
                    def _():
                        block_load(block_source(2)).start()
                elif index < 3:
                    block_load(block_source(index + 1)).start()
                else:
                    @on(3)
                    def _():
                        block_load(block_source(4)).start()
        for index in range(4, 8):
            @pl.when((t == 1 + index) & (layer == 3))
            def _():
                block_load(block_source(index)).wait()
                low_mid[pl.ds((index - 4) * TOKENS, TOKENS)] = transposed(block[...], wide_out[1])
                if index < 7:
                    block_load(block_source(index + 1)).start()

        @pl.when((t >= 1) & (t < 5) & (layer == 3))
        def _():
            gate_some(3 * (t - 1), jnp.minimum(3, MAIN // 32 - 3 * (t - 1)))

        for kind, when in ((2, 9), (1, 3)):
            @pl.when((t == when) & (layer == kind))
            def _():
                for item in proj_in_copies(kind):
                    item.wait_recv()
                for item in proj_chip_copies(kind):
                    item.start()

            @pl.when((t == when + 1) & (layer == kind))
            def _():
                proj_chip_arrived(kind)
                if kind == 1:
                    wide_out[1, RANK:2 * RANK] = wide_out[1, 0:RANK]

        @pl.when((t == 4) & (layer == 1))
        def _():
            block_load(weight).wait()
            folded[x, z, c, RANK:2 * RANK] = transposed(wide_out[0, RANK:2 * RANK], block[...]).astype(bf16)
            mine = folded.at[x, z, c, RANK:2 * RANK]
            copy(mine, mine, fold_send.at[12], fold_recv.at[12], above).start()
            block_load(block_source(2)).start()

        for index, stage in enumerate(fold_stages[:6]):
            lag = jnp.where(layer == 1, FOLD_ONE, FOLD_TWO)

            @pl.when((t == lag + index) & ((layer == 1) | (layer == 2)))
            def _():
                if index == 0:
                    @on(2)
                    def _():
                        mine = folded.at[x, z, c, RANK:2 * RANK]
                        copy(mine, mine, fold_send.at[12], fold_recv.at[12], above).wait_recv()
                for part in stage:
                    part()

    def step(t, carry):
        @pl.when(t + AHEAD < PAIRS)
        def _():
            share_pair(t + AHEAD)
        for kind, partner in ((3, above), (2, below)):
            @pl.when((t >= 1) & (t <= REST // SLICE) & (layer == kind))
            def _():
                rest_slice(t - 1, partner).start()

        @pl.when((t >= 1) & (t < 9) & (layer == 1))
        def _():
            pool_part(2 * (t - 1)).start()
            pool_part(2 * (t - 1) + 1).start()

            @pl.when(t % 2 == 1)
            def _():
                val_part((t - 1) // 2).start()

        when_in(t, 0, have_share)
        for lag, index in ((0, 0), (LAG_FORWARD, 1), (LAG_ROW, 2), (LAG_ROW_FORWARD, 3), (LAG_LAST, 4)):
            when_in(t, lag, run_stage(index))
        early(t)
        when_in(t, LAG_USE, run_stage(5))

        @pl.when((t == LAG_USE + LATE) & (layer < 2))
        def _():
            for i in range(REST // SLICE):
                rest_slice(i, above).wait_recv()

            @on(0)
            def _():
                gate_some(0, REST // 32)

                def body(j, inner_carry):
                    upper_chunk(j, REST, above)
                    return inner_carry
                lax.fori_loop(0, 2 * LATE, body, 0)

        for kind, rows, target, begin in ((3, MAIN, below, LAG_USE), (0, REST, above, LAG_USE + LATE)):
            @pl.when((layer == kind) & (t >= begin) & (t < PAIRS + LAG_USE))
            def _():
                upper_chunk(2 * (t - LAG_USE), rows, target)
                upper_chunk(2 * (t - LAG_USE) + 1, rows, target)

        whole = jnp.minimum(2 * (t - LAG_USE) + 2, CHUNKS)
        begin_rest = LAG_GRAD + LATE
        ready_rest = jnp.where(t <= begin_rest, 0, jnp.where(t < begin_rest + LATE, 2 * (t - begin_rest), t - LAG_GRAD))
        for kind, rows, ready in ((2, MAIN, jnp.maximum(t - LAG_GRAD, 0)), (1, REST, ready_rest)):
            @pl.when((layer == kind) & (t >= LAG_USE) & (t < PAIRS + LAG_USE))
            def _():
                lower_weight(2 * (t - LAG_USE), ready, rows)

        @pl.when((layer == 2) & (t >= LAG_GRAD) & (t < PAIRS + LAG_GRAD - 1))
        def _():
            lower_grad(t - LAG_GRAD, whole, MAIN)

        @pl.when((layer == 1) & (t >= begin_rest) & (t < begin_rest + LATE))
        def _():
            lower_grad(2 * (t - begin_rest), whole, REST)
            lower_grad(2 * (t - begin_rest) + 1, whole, REST)

        @pl.when((layer == 1) & (t >= begin_rest + LATE) & (t < PAIRS + LAG_GRAD - 1))
        def _():
            lower_grad(t - LAG_GRAD, whole, REST)
        return carry

    lax.fori_loop(0, PAIRS + LAG_GRAD - 1, step, 0)

    def drain(p, carry):
        run_stage(6)(p)

        @pl.when(layer >= 2)
        def _():
            share_out(2 * p, above).wait_send()
            share_out(2 * p + 1, above).wait_send()
        for kind, rows in ((3, MAIN), (0, REST)):
            @on(kind)
            def _():
                grad_copy(2 * p, rows, above).wait_send()
                grad_copy(2 * p + 1, rows, above).wait_send()
        return carry
    lax.fori_loop(0, PAIRS, drain, 0)

    @pl.when(layer >= 2)
    def _():
        for i in range(REST // SLICE):
            rest_slice(i, above).wait_send()

    @on(1)
    def _():
        for item in main_parts():
            item.wait_send()
        mine = folded.at[x, z, c, RANK:2 * RANK]
        copy(mine, mine, fold_send.at[12], fold_recv.at[12], above).wait_send()

    @pl.when((layer == 1) | (layer == 2))
    def _():
        fold_stages[6][0]()
    for kind in (2, 1, 0):
        @on(kind)
        def _():
            for item in proj_out_copies(kind) + proj_chip_copies(kind):
                item.wait_send()

    def finish(kind, rows):
        if kind == 2:
            for item in main_parts():
                item.wait_recv()
        lower_gate(PAIRS - 1, rows)
        low_mid[0:rows] = jnp.zeros((rows, 2 * RANK), f32)

        def body(i, carry):
            for n in (2 * i, 2 * i + 1):
                add_product(n, PAIRS - 1, rows)
                for base in range(0, rows, 64):
                    part = slice(base, base + 64)
                    up = grad[n, part].astype(f32)
                    value = second[part, columns(n)].astype(f32)
                    low = (up + total[n, part]).astype(bf16)
                    first[part, columns(n)] = low
                    grad[n, part] = (low.astype(f32) * silu_slope(value)).astype(bf16)
                fold = folded[n // 4, n % 4]
                left = jnp.concatenate([first[0:rows, columns(n)], grad[n, 0:rows]], 1)
                right = jnp.concatenate([wide_out[0, :, columns(n)], fold[0], fold[1]], 1)
                low_mid[0:rows] += transposed(left, right)
            return carry
        lax.fori_loop(0, PAIRS, body, 0)

    wide = (RANK, 2 * RANK)
    lower = low_half(wide)
    lower_rows = low_half((TOKENS, 2 * RANK))

    tokens = lax.broadcasted_iota(jnp.int32, (TOKENS, 2 * RANK), 0)
    valid = [
        (tokens < jnp.where(lower_rows, lens[0], lens[1])).astype(f32) for lens in (pool_len, val_len)
    ]

    def swap(value):
        return pltpu.roll(value, RANK, 1)

    def put(index, slot, value, mask):
        outgoing[index, slot] = (value * valid[mask]).astype(bf16)

    @on(3)
    def _():
        rows = [low_mid[i * TOKENS:(i + 1) * TOKENS] for i in range(4)]
        landed[0] = (jnp.where(lower_rows, rows[0], rows[1]) * valid[0]).astype(bf16)
        landed[1] = (jnp.where(lower_rows, rows[2], rows[3]) * valid[1]).astype(bf16)
        landed[2] = jnp.zeros_like(landed[2])

    @on(2)
    def _():
        finish(2, MAIN)
        def short(ref):
            return jnp.concatenate([ref[2 * TOKENS:MAIN], jnp.zeros((TOKENS - FIRST, 2 * RANK), f32)], 0)

        mid = [low_mid[0:TOKENS], low_mid[TOKENS:2 * TOKENS], short(low_mid)]
        two = [low_two[0:TOKENS], low_two[TOKENS:2 * TOKENS], short(low_two)]
        put(1, 0, jnp.where(lower_rows, mid[0], swap(mid[1])), 0)
        put(1, 1, jnp.where(lower_rows, mid[2], 0.0), 1)
        put(0, 0, jnp.where(lower_rows, swap(mid[0]), mid[1]), 0)
        put(0, 1, jnp.where(lower_rows, swap(mid[2]), 0.0), 1)
        landed[0] = (jnp.where(lower_rows, two[0], two[1]) * valid[0]).astype(bf16)
        landed[1] = (jnp.where(lower_rows, two[2], 0.0) * valid[1]).astype(bf16)

    @on(1)
    def _():
        finish(1, REST)
        def split(ref):
            other_tokens = REST - TOKENS
            return (
                jnp.concatenate([jnp.zeros((TOKENS - other_tokens, 2 * RANK), f32), ref[0:other_tokens]], 0),
                ref[other_tokens:REST],
            )

        one, two = split(low_mid), split(low_two)
        put(0, 1, jnp.where(lower_rows, swap(one[0]), one[1]), 1)
        put(2, 1, jnp.where(lower_rows, two[0], two[1]), 1)
        landed[2] = (jnp.where(lower_rows, one[0], swap(one[1])) * valid[1]).astype(bf16)

    def low(source, slot, plane):
        return copy(source, landed.at[slot], low_send.at[slot + 3 * plane], low_recv.at[slot], {"layer": plane})

    def lows(kind):
        if kind == 2:
            return [low(outgoing.at[0, 0], 0, 0), low(outgoing.at[0, 1], 1, 0),
                    low(outgoing.at[1, 0], 0, 1), low(outgoing.at[1, 1], 1, 1)]
        if kind == 1:
            return [low(outgoing.at[0, 1], 2, 0), low(outgoing.at[2, 1], 2, 2)]
        return []

    def lows_in(kind):
        return [low(landed.at[slot], slot, (kind + 1) % 4) for slot in {3: (), 2: (2,), 1: (0, 1), 0: (0, 1, 2)}[kind]]

    for kind in (2, 1):
        @pl.when(layer == kind)
        def _():
            for item in lows(kind):
                item.start()

    for kind in (2, 1, 0):
        @pl.when(layer == kind)
        def _():
            for item in lows_in(kind):
                item.wait_recv()

    def across_tokens(left, right):
        return lax.dot_general(left, right, (((0,), (0,)), ((), ())), precision=highest, preferred_element_type=f32)

    def blocks(value):
        return jnp.where(lower, value[0:RANK], value[RANK:2 * RANK])

    def both(value):
        return value + swap(value)

    pool_low = jnp.where(lower_rows, low_in[0], low_in[1]) * valid[0]
    val_low = jnp.where(lower_rows, low_in[2], low_in[3]) * valid[1]
    pool_out = landed[0].astype(f32)
    val_out = landed[1].astype(f32) + landed[2].astype(f32)
    vals[x, z, c] = blocks(across_tokens(val_out, val_low)).astype(bf16)
    part_in = both(blocks(across_tokens(pool_low, pool_low)))
    part_out = both(blocks(across_tokens(pool_out, pool_out)))
    factors[x * 2 + c, 0:RANK] = jnp.where(lower, part_in, part_out)
    factors[x * 2 + c, RANK:RANK + 8] = jnp.full((8, 2 * RANK), (pool_len[0] + pool_len[1]).astype(f32))

    mine = x * 2 + c
    sent_one = [copy(factors.at[mine], factors.at[mine], fac_send.at[i], fac_recv.at[mine], n[3]) for i, n in enumerate(near)]
    sent_one += [copy(vals.at[x, z, c], vals.at[x, z, c], val_send.at[i], val_recv.at[mine], n[3]) for i, n in enumerate(near)]
    for item in sent_one:
        item.start()
    pool_grads = blocks(across_tokens(pool_low, pool_out))
    for slot, xi, ci, device in near:
        copy(factors.at[slot], factors.at[slot], fac_send.at[0], fac_recv.at[slot], device).wait_recv()
    factors_z[z] = sum(factors[i] for i in range(1, 8)) + factors[0]
    sent_two = [copy(factors_z.at[z], factors_z.at[z], facz_send.at[i], facz_recv.at[z], a[1]) for i, a in enumerate(across)]
    for item in sent_two:
        item.start()
    for slot, xi, ci, device in near:
        copy(vals.at[xi, z, ci], vals.at[xi, z, ci], val_send.at[0], val_recv.at[slot], device).wait_recv()
    sent_three = [copy(vals.at[:, z], vals.at[:, z], valz_send.at[i], valz_recv.at[z], a[1]) for i, a in enumerate(across)]
    for item in sent_three:
        item.start()
    for zi, device in across:
        copy(factors_z.at[zi], factors_z.at[zi], facz_send.at[0], facz_recv.at[zi], device).wait_recv()
    factor_sum = factors_z[0] + factors_z[1] + factors_z[2] + factors_z[3]
    inverse = damped_inverses(factor_sum[0:RANK] / factor_sum[RANK:RANK + 1])
    inv_in = inverse[:, 0:RANK]
    turned = swap(inverse)
    twice = jnp.where(lower, turned, inverse)
    inv_out = jnp.concatenate([jnp.where(lower, twice, 0.0), jnp.where(lower, 0.0, twice)], 0)
    scaled = jnp.dot(inv_in, pool_grads, precision=highest, preferred_element_type=f32)
    scaled = jnp.dot(scaled, inv_out, precision=highest, preferred_element_type=f32)
    coarse = scaled.astype(bf16)
    fine = (scaled - coarse.astype(f32)).astype(bf16)
    empty = jnp.zeros(wide, bf16)

    def spread(value):
        return jnp.concatenate(
            [jnp.concatenate([value, empty], 1), jnp.concatenate([empty, value], 1)], 0
        )

    coarse, fine = spread(coarse), spread(fine)
    for zi, device in across:
        copy(vals.at[:, zi], vals.at[:, zi], valz_send.at[0], valz_recv.at[zi], device).wait_recv()
    every = vals[...].reshape(32 * RANK, 2 * RANK)
    product = jnp.dot(every, coarse, preferred_element_type=f32) + jnp.dot(every, fine, preferred_element_type=f32)
    at_row = lax.broadcasted_iota(jnp.int32, product.shape, 0) % RANK
    at_lane = lax.broadcasted_iota(jnp.int32, product.shape, 1) % RANK
    summed = jnp.where(at_row == at_lane, product, 0.0).reshape(32, RANK, 4 * RANK).sum(1)
    group = lax.broadcasted_iota(jnp.int32, (8, 4 * RANK), 1) // RANK
    picks = (lax.broadcasted_iota(jnp.int32, (8, 4 * RANK), 0) == group).astype(f32)
    part = lax.dot_general(picks, summed, (((1,), (1,)), ((), ())), precision=highest, preferred_element_type=f32)
    layers[layer] = jnp.concatenate([part, jnp.zeros((8, 96), f32)], 1)
    sent_last = [copy(layers.at[layer], layers.at[layer], lay_send.at[i], lay_recv.at[layer], q[1]) for i, q in enumerate(planes)]
    for item in sent_last:
        item.start()
    for plane, device in planes:
        copy(layers.at[plane], layers.at[plane], lay_send.at[0], lay_recv.at[plane], device).wait_recv()
    table = (layers[0] + layers[1] + layers[2] + layers[3]) * (1.0 / (RANK * TOKENS))
    lane = lax.broadcasted_iota(jnp.int32, (128, 16), 0)
    spot_of = lax.broadcasted_iota(jnp.int32, (128, 16), 1) + 16 * layer

    def placed(index):
        return jnp.dot(
            table, (2 * lane + index == spot_of).astype(f32), precision=highest, preferred_element_type=f32
        )

    scores_out[...] = placed(0)[0:2] + placed(1)[2:4]

    for item in sent_one + sent_two + sent_three + sent_last:
        item.wait_send()
    for kind in (2, 1):
        @pl.when(layer == kind)
        def _():
            for item in lows(kind):
                item.wait_send()


def whole(*operands):
    anywhere = pl.BlockSpec(memory_space=pl.ANY)
    inside = pl.BlockSpec(memory_space=pltpu.VMEM)
    dma = pltpu.SemaphoreType.DMA
    bf16, f32 = jnp.bfloat16, jnp.float32
    return pl.pallas_call(
        whole_kernel,
        out_shape=jax.ShapeDtypeStruct((2, 16), f32),
        in_specs=[anywhere] * 7 + [pl.BlockSpec(memory_space=pltpu.SMEM)] * 2,
        out_specs=inside,
        scratch_shapes=[
            pltpu.VMEM((CHUNKS, 4, 4, 2, SHARE, COLS), bf16),
            pltpu.VMEM((MAIN, WIDTH), bf16),
            pltpu.VMEM((MAIN, WIDTH), bf16),
            pltpu.VMEM((MAIN, WIDTH), bf16),
            pltpu.VMEM((CHUNKS, MAIN, COLS), bf16),
            pltpu.VMEM((CHUNKS, MAIN, COLS), f32),
            pltpu.VMEM((TOKENS, WIDTH), bf16),
            pltpu.VMEM((2 * RANK, WIDTH), bf16),
            pltpu.VMEM((2, 2 * RANK, WIDTH), bf16),
            pltpu.VMEM((4, 4, 2, 2 * RANK, SHARE), bf16),
            pltpu.VMEM((4 * TOKENS, 2 * RANK), f32),
            pltpu.VMEM((MAIN, 2 * RANK), f32),
            pltpu.VMEM((4, TOKENS, 2 * RANK), f32),
            pltpu.VMEM((3, 2, TOKENS, 2 * RANK), bf16),
            pltpu.VMEM((3, TOKENS, 2 * RANK), bf16),
            pltpu.VMEM((8, RANK + 8, 2 * RANK), f32),
            pltpu.VMEM((4, RANK + 8, 2 * RANK), f32),
            pltpu.VMEM((4, 4, 2, RANK, 2 * RANK), bf16),
            pltpu.VMEM((4, 8, 128), f32),
            dma((CHUNKS, 13)), dma((CHUNKS, 13)), dma((CHUNKS,)), dma((CHUNKS,)), dma((24,)), dma((24,)),
            dma((CHUNKS + 12,)), dma((13,)), dma((13,)), dma((7,)), dma((7,)),
            dma((12,)), dma((3,)), dma((7,)), dma((8,)), dma((7,)), dma((8,)),
            dma((3,)), dma((4,)), dma((3,)), dma((4,)), dma((3,)), dma((4,)),
        ],
        compiler_params=pltpu.CompilerParams(
            collective_id=0, has_side_effects=True, vmem_limit_bytes=62 * 1024 * 1024
        ),
        name="whole",
    )(*operands)


def on_device(
    pool_inputs, val_inputs, pool_top, val_top, weight, proj_in, proj_out, pool_len, val_len
):
    return whole(
        *(rows.reshape(-1, WIDTH) for rows in (pool_inputs[0], val_inputs[0], pool_top, val_top)), weight[0], proj_in[0].T, proj_out[0].T, pool_len, val_len
    )


def solution(mesh):
    placed = (
        P("layer", "trace", None, None),
        P("layer", "trace", None, None),
        P("trace", None, None),
        P("trace", None, None),
        P("layer", "trace", None),
        P("layer", None, None),
        P("layer", None, None),
        P("trace"),
        P("trace"),
    )
    return jax.shard_map(
        on_device, mesh=mesh, in_specs=placed, out_specs=P("trace", "layer"), check_vma=False
    )
```
